256 devices in a mesh: space: 128 (over y, x, z), chan: 2 (over core).
Axes of the slice: x: 4, y: 4, z: 8, core: 2. Of those that a mesh axis runs over, the one named last changes fastest.
Arguments:
- feats: bfloat16 [1024, 64, 512], P('space', 'chan'), may hold values from -6 to 6
- live_count: int32 [128], P('space'), may hold values from 1 to 8, 640 in all
- neighbours: int32 [1024, 26], P('space'), may hold values from 0 to 1024, as said below
- parent: int32 [1024], P('space'), may hold values from 0 to 1023, as said below
- fine_weight: bfloat16 [27, 64, 64], P(None, 'chan'), may hold values from -0.15625 to 0.15625
- coarse_weight: bfloat16 [27, 128, 64], P(None, 'chan'), may hold values from -0.15625 to 0.15625
- project_weight: bfloat16 [64, 128], P(None, 'chan'), may hold values from -0.5 to 0.5
- cotangent: bfloat16 [1024, 64, 512], P('space', 'chan'), may hold values from -6 to 6
Outputs:
- out_feats: bfloat16 [1024, 64, 512], P('space', 'chan')
- grad_feats: bfloat16 [1024, 64, 512], P('space', 'chan')
- fine_weight_grad: float32 [27, 64, 64], P(None, 'chan')
- coarse_weight_grad: float32 [27, 128, 64], P(None, 'chan')
- project_weight_grad: float32 [64, 128], P(None, 'chan')
The draws below stay inside these ranges and needn't reach their ends.
Inputs may be any that keep to these rules, and one draw needn't show every extreme that they name: `live_count`: some index of space has all 8 slots occupied. Entry [b, t] is the brick beside brick b in direction t, or 1024 where there is none. A brick's neighbours belong to its own index of space or to the indices just before and after it. The lists are symmetric: if entry [b, t] is b2 < 1024, entry [b2, 25 - t] is b. Every value occurs once; coarse brick j belongs to index j // 1 of space. A brick's parent lies on its own index of space or on the index just before or after it. Between two neighbouring indices, as many bricks of the lower have parents on the upper as the reverse, from 1 to 1; some pair of neighbouring indices has exactly 1.
All inputs are finite; a program needn't handle non-finite values. No bound on the sum of `live_count` on one device may be relied on, other than what follows from the above.
Results may differ from the reference program's by a relative error of at most 0.012.
Values may be sent and summed in bfloat16 or wider, within the bound.
A program may use at most 320 MiB of HBM per device.

```python
import math
import jax
import jax.numpy as jnp
import numpy as np
from jax import lax

C = 64
CC = 128
NB_DEV = 8
NBRICKS = 1024
NCOARSE = 128
MOVE = 1
N_SPACE = 128


def draw_neighbours(key, part):
    key = jax.random.fold_in(key, 11)
    half_cells = NB_DEV // 2
    exponent = half_cells.bit_length() - 1
    span_y = 2 ** (exponent // 2)
    span_z = half_cells // span_y
    device_keys = jax.random.split(key, N_SPACE)
    slot_of_cell = jax.vmap(lambda single: jax.random.permutation(single, NB_DEV))(device_keys).astype(jnp.int32)
    cell_index = jnp.arange(NB_DEV, dtype=jnp.int32)
    layer_x = cell_index // half_cells
    row_y = cell_index % half_cells // span_z
    row_z = cell_index % span_z
    owner_index = jnp.arange(N_SPACE, dtype=jnp.int32)[:, None]
    place_x = 2 * owner_index + layer_x[None, :]
    direction_lists = []
    for step_x in (-1, 0, 1):
        for step_y in (-1, 0, 1):
            for step_z in (-1, 0, 1):
                if step_x == 0 and step_y == 0 and (step_z == 0):
                    continue
                next_x = place_x + step_x
                next_y = jnp.broadcast_to(row_y[None, :] + step_y, next_x.shape)
                next_z = jnp.broadcast_to(row_z[None, :] + step_z, next_x.shape)
                inside = (next_x >= 0) & (next_x < 2 * N_SPACE) & (next_y >= 0) & (next_y < span_y) & (next_z >= 0) & (next_z < span_z)
                clip_x = jnp.clip(next_x, 0, 2 * N_SPACE - 1)
                next_owner = clip_x // 2
                next_cell = clip_x % 2 * half_cells + jnp.clip(next_y, 0, span_y - 1) * span_z + jnp.clip(next_z, 0, span_z - 1)
                target = next_owner * NB_DEV + slot_of_cell[next_owner, next_cell]
                direction_lists.append(jnp.where(inside, target, NBRICKS))
    by_cell = jnp.stack(direction_lists, axis=-1).astype(jnp.int32)
    by_slot = jnp.zeros_like(by_cell).at[jnp.broadcast_to(owner_index, slot_of_cell.shape), slot_of_cell].set(by_cell)
    return by_slot.reshape(NBRICKS, 26).astype(jnp.int32)


def draw_parent(key, part):
    key = jax.random.fold_in(key, 23)
    count_key, top_key, slot_key, order_key = jax.random.split(key, 4)
    owner = jnp.arange(N_SPACE, dtype=jnp.int32)
    counts = jax.random.randint(count_key, (N_SPACE,), 1, MOVE + 1).astype(jnp.int32)
    top_boundary = jax.random.randint(top_key, (), 0, N_SPACE - 1).astype(jnp.int32)
    counts = jnp.where(owner == top_boundary, MOVE, counts)
    counts = jnp.where(owner == N_SPACE - 1, 0, counts).astype(jnp.int32)
    left_counts = jnp.concatenate([jnp.zeros((1,), jnp.int32), counts[:-1]])
    local_slots = jax.vmap(lambda single: jax.random.permutation(single, NB_DEV))(jax.random.split(slot_key, N_SPACE)).astype(jnp.int32)
    base = owner[:, None] * NB_DEV + local_slots
    order = jax.vmap(lambda single: jax.random.permutation(single, NB_DEV))(jax.random.split(order_key, N_SPACE)).astype(jnp.int32)
    rank = jnp.argsort(order, axis=1).astype(jnp.int32)
    mirror = NB_DEV - 1 - rank
    next_base = jnp.roll(base, -1, axis=0)
    prev_base = jnp.roll(base, 1, axis=0)
    next_order = jnp.roll(order, -1, axis=0)
    prev_order = jnp.roll(order, 1, axis=0)
    take_right = jnp.take_along_axis(next_base, jnp.take_along_axis(next_order, mirror, axis=1), axis=1)
    take_left = jnp.take_along_axis(prev_base, jnp.take_along_axis(prev_order, mirror, axis=1), axis=1)
    result = jnp.where(rank < counts[:, None], take_right, jnp.where(rank >= NB_DEV - left_counts[:, None], take_left, base))
    return result.reshape(NBRICKS).astype(jnp.int32)


def levels(key, shape, cuts, smallest, top_value):
    def one(axis_at, blocks):
        heights = jax.random.uniform(jax.random.fold_in(jax.random.fold_in(key, 6), axis_at), (blocks,), jnp.float32, smallest / len(cuts), top_value / len(cuts))
        return jnp.repeat(jnp.exp(heights), shape[axis_at] // blocks).reshape((-1,) + (1,) * (len(shape) - axis_at - 1))

    loudness = one(*cuts[0])
    for cut in cuts[1:]:
        loudness = loudness * one(*cut)
    return loudness


def profile(count, total, limit, skew):
    weights = [(1 << 20) // math.isqrt(rank ** skew) + 1 for rank in range(2, count + 1)]
    surplus, given = total - limit - (count - 1), [1] * (count - 1)
    while surplus > 0:
        free = [i for i in range(count - 1) if given[i] < limit]
        whole, left = sum([weights[i] for i in free]), surplus
        for i in free:
            extra = min(limit - given[i], max(1, left * weights[i] // whole), surplus)
            given[i] = given[i] + extra
            surplus = surplus - extra
    return np.array([limit] + given)


def uneven_parts(own_key, number_of, total, bound, lean):
    if number_of == 2:
        one = jax.random.randint(own_key, (), max(1, total - bound), min(bound, total - 1) + 1)
        return jnp.stack([one, total - one])
    lengths = jnp.asarray(profile(number_of, total, bound, lean), jnp.int32)
    twos = (number_of - 1) // 2
    source_of, taker = lengths[1:1 + 2 * twos:2], lengths[2:2 + 2 * twos:2]
    margin = jnp.minimum(source_of - 1, bound - taker)
    passed = jax.random.randint(jax.random.fold_in(own_key, 1), (twos,), 0, 1 << 20) % (margin + 1)
    lengths = lengths.at[1:1 + 2 * twos:2].set(source_of - passed).at[2:2 + 2 * twos:2].set(taker + passed)
    return lengths[jax.random.permutation(jax.random.fold_in(own_key, 2), number_of)]


def gaussian(stream_key, extent, spread, reach, cuts=(), held_as=jnp.bfloat16):
    drawn = jax.random.normal(stream_key, extent, jnp.float32) * spread
    if len(cuts) > 0:
        drawn = levels(stream_key, extent, cuts, -0.22, 0.18) * drawn
    return jnp.clip(drawn, min=-reach, max=reach).astype(held_as)


def setup_inputs(seed: int = 0) -> dict:
    key_list = jax.random.split(jax.random.key(seed), 9)
    return {
        "feats": gaussian(key_list[0], (NBRICKS, C, 512), 1.0, 6.0, ((0, 128), (1, 2))),
        "live_count": uneven_parts(key_list[1], N_SPACE, NBRICKS * 5 // 8, NB_DEV, 2).astype(jnp.int32),
        "neighbours": draw_neighbours(jax.random.fold_in(key_list[8], 71), 0),
        "parent": draw_parent(jax.random.fold_in(key_list[8], 71), 0),
        "fine_weight": gaussian(key_list[4], (27, C, C), (27 * C) ** -0.5, 0.15625, ((1, 2),)),
        "coarse_weight": gaussian(key_list[5], (27, CC, C), (27 * C) ** -0.5, 0.15625, ((1, 2),)),
        "project_weight": gaussian(key_list[6], (C, CC), CC ** -0.5, 0.5, ((1, 2),)),
        "cotangent": gaussian(key_list[7], (NBRICKS, C, 512), 1.0, 6.0, ((0, 128), (1, 2))),
    }


def edge_range(position):
    if position == 0:
        return slice(7, 8)
    if position == 1:
        return slice(0, 8)
    return slice(0, 1)

def direction_slabs(full_table):
    slab_list = []
    for offset_x in range(3):
        for offset_y in range(3):
            for offset_z in range(3):
                if offset_x == 1 and offset_y == 1 and (offset_z == 1):
                    slab_list.append(None)
                else:
                    slab_list.append(full_table[:, :, edge_range(offset_x), edge_range(offset_y), edge_range(offset_z)])
    return slab_list

def assemble(pieces):
    planes = []
    for offset_x in range(3):
        row_list = []
        for offset_y in range(3):
            first = 9 * offset_x + 3 * offset_y
            row_list.append(jnp.concatenate(pieces[first:first + 3], axis=4))
        planes.append(jnp.concatenate(row_list, axis=3))
    return jnp.concatenate(planes, axis=2)

def tap_columns(padded):
    amount, channels = (padded.shape[0], padded.shape[1])
    shifted = []
    for offset_x in range(3):
        for offset_y in range(3):
            for offset_z in range(3):
                window = padded[:, :, offset_x:offset_x + 8, offset_y:offset_y + 8, offset_z:offset_z + 8]
                shifted.append(window.reshape(amount, channels, 512))
    return jnp.concatenate(shifted, axis=1)

def flat_weight(weight):
    return jnp.transpose(weight, (1, 0, 2)).reshape(weight.shape[1], -1)

def unflat_weight(matrix, channels):
    return jnp.transpose(matrix.reshape(matrix.shape[0], 27, channels), (1, 0, 2))

def flip_weight(weight):
    return jnp.transpose(weight[::-1], (0, 2, 1))

def pool_sum(field_in):
    amount, channels = (field_in.shape[0], field_in.shape[1])
    grouped = field_in.astype(jnp.float32).reshape(amount, channels, 4, 2, 4, 2, 4, 2)
    return grouped.sum(axis=(3, 5, 7)).reshape(amount, channels, 64)

def enlarge(octants):
    amount, channels = (octants.shape[0], octants.shape[1])
    expanded = jnp.broadcast_to(octants.reshape(amount, channels, 4, 1, 4, 1, 4, 1), (amount, channels, 4, 2, 4, 2, 4, 2))
    return expanded.reshape(amount, channels, 512)

def place_octants(octants):
    amount, channels = (octants.shape[0] // 8, octants.shape[1])
    grouped = octants.reshape(amount, 2, 2, 2, channels, 4, 4, 4)
    return jnp.transpose(grouped, (0, 4, 1, 5, 2, 6, 3, 7)).reshape(amount, channels, 512)

def split_octants(coarse):
    amount, channels = (coarse.shape[0], coarse.shape[1])
    grouped = coarse.reshape(amount, channels, 2, 4, 2, 4, 2, 4)
    return jnp.transpose(grouped, (0, 2, 4, 6, 1, 3, 5, 7)).reshape(amount * 8, channels, 64)

def fine_pass(field_in, neighbours, weight, cotangent_in):
    amount = neighbours.shape[0]
    channels = field_in.shape[1]
    full_table = jnp.concatenate([field_in, jnp.zeros((1, channels, 512), field_in.dtype)], axis=0)
    full_table = full_table.reshape(amount + 1, channels, 8, 8, 8)
    slab_list = direction_slabs(full_table)
    matrix = flat_weight(weight).astype(jnp.float32)
    block_rows = 64

    def advance(running, first_row):
        near_index = lax.dynamic_slice_in_dim(neighbours, first_row, block_rows, 0)
        pieces = []
        position = 0
        for slab_piece in slab_list:
            if slab_piece is None:
                pieces.append(lax.dynamic_slice_in_dim(full_table, first_row, block_rows, 0))
            else:
                pieces.append(jnp.take(slab_piece, near_index[:, position], axis=0))
                position += 1
        columns = tap_columns(assemble(pieces)).astype(jnp.float32)
        result = jnp.einsum('ok,bkv->bov', matrix, columns)
        if cotangent_in is not None:
            grad_rows = lax.dynamic_slice_in_dim(cotangent_in, first_row, block_rows, 0).astype(jnp.float32)
            running = running + jnp.einsum('bov,bkv->ok', grad_rows, columns)
        return (running, result)
    starts = jnp.arange(amount // block_rows, dtype=jnp.int32) * block_rows
    running, results = lax.scan(advance, jnp.zeros(matrix.shape, jnp.float32), starts)
    return (results.reshape(amount, matrix.shape[0], 512), unflat_weight(running, channels))

def coarse_pass(field_in, weight, cotangent_in):
    amount, channels = (field_in.shape[0], field_in.shape[1])
    matrix = flat_weight(weight).astype(jnp.float32)
    block_rows = 16

    def advance(running, first_row):
        block_piece = lax.dynamic_slice_in_dim(field_in, first_row, block_rows, 0).reshape(block_rows, channels, 8, 8, 8)
        padded = jnp.pad(block_piece, ((0, 0), (0, 0), (1, 1), (1, 1), (1, 1)))
        columns = tap_columns(padded).astype(jnp.float32)
        result = jnp.einsum('ok,bkv->bov', matrix, columns)
        if cotangent_in is not None:
            grad_rows = lax.dynamic_slice_in_dim(cotangent_in, first_row, block_rows, 0).astype(jnp.float32)
            running = running + jnp.einsum('bov,bkv->ok', grad_rows, columns)
        return (running, result)
    starts = jnp.arange(amount // block_rows, dtype=jnp.int32) * block_rows
    running, results = lax.scan(advance, jnp.zeros(matrix.shape, jnp.float32), starts)
    return (results.reshape(amount, matrix.shape[0], 512), unflat_weight(running, channels))

def reference(feats, live_count, neighbours, parent, fine_weight, coarse_weight, project_weight, cotangent):
    live_mask = (jnp.arange(NB_DEV, dtype=jnp.int32)[None, :] < live_count[:, None]).astype(jnp.float32).reshape(NBRICKS, 1, 1)
    pooled = (pool_sum(feats) * 0.125 * live_mask).astype(jnp.bfloat16)
    coarse_in = place_octants(jnp.zeros((NBRICKS, C, 64), jnp.bfloat16).at[parent].set(pooled))
    preactivation, unused = coarse_pass(coarse_in, coarse_weight, None)
    hidden = jax.nn.silu(preactivation).astype(jnp.bfloat16)
    coarse_out = jnp.einsum('cj,bjv->bcv', project_weight.astype(jnp.float32), hidden.astype(jnp.float32)).astype(jnp.bfloat16)
    up_octants = jnp.take(split_octants(coarse_out), parent, axis=0)
    mixed_feats = ((feats.astype(jnp.float32) + enlarge(up_octants).astype(jnp.float32)) * live_mask).astype(jnp.bfloat16)
    grad_rows = (cotangent.astype(jnp.float32) * live_mask).astype(jnp.bfloat16)
    out_raw, fine_raw = fine_pass(mixed_feats, neighbours, fine_weight, grad_rows)
    out_feats = (out_raw * live_mask).astype(jnp.bfloat16)
    back_raw, unused = fine_pass(grad_rows, neighbours, flip_weight(fine_weight), None)
    back_feats = (back_raw * live_mask).astype(jnp.bfloat16)
    up_grad = pool_sum(back_feats).astype(jnp.bfloat16)
    coarse_grad = place_octants(jnp.zeros((NBRICKS, C, 64), jnp.bfloat16).at[parent].set(up_grad))
    project_raw = jnp.einsum('bcv,bjv->cj', coarse_grad.astype(jnp.float32), hidden.astype(jnp.float32))
    hidden_grad = jnp.einsum('cj,bcv->bjv', project_weight.astype(jnp.float32), coarse_grad.astype(jnp.float32))
    sigmoid_pre = jax.nn.sigmoid(preactivation)
    pre_grad = (hidden_grad * sigmoid_pre * (1.0 + preactivation * (1.0 - sigmoid_pre))).astype(jnp.bfloat16)
    unused, coarse_raw = coarse_pass(coarse_in, coarse_weight, pre_grad)
    coarse_back_raw, unused = coarse_pass(pre_grad, flip_weight(coarse_weight), None)
    coarse_back = coarse_back_raw.astype(jnp.bfloat16)
    down_grad = jnp.take(split_octants(coarse_back), parent, axis=0)
    grad_feats = (back_feats.astype(jnp.float32) + live_mask * enlarge(down_grad).astype(jnp.float32) * 0.125).astype(jnp.bfloat16)
    fine_scale = 1.0 / math.sqrt(512.0 * NBRICKS)
    coarse_scale = 1.0 / math.sqrt(512.0 * NCOARSE)
    return (out_feats, grad_feats, fine_raw * fine_scale, coarse_raw * coarse_scale, project_raw * coarse_scale)
```

```python
import math

import jax
import jax.numpy as jnp
import numpy as np
from jax import lax
from jax.experimental import pallas as pl
from jax.experimental.pallas import tpu as pltpu
from jax.sharding import PartitionSpec as P


def extended(block, sides, width):
    for axis, dim in sides:
        count = lax.axis_size(axis)
        forward = [(i, i + 1) for i in range(count - 1)]
        backward = [(target, source) for source, target in forward]
        low = lax.ppermute(
            lax.slice_in_dim(block, block.shape[dim] - width, None, axis=dim), axis, forward
        )
        high = lax.ppermute(lax.slice_in_dim(block, 0, width, axis=dim), axis, backward)
        block = jnp.concatenate([low, block, high], axis=dim)
    return block


def lean_list():
    leans = []
    for lean_x in (-1, 0, 1):
        for lean_y in (-1, 0, 1):
            for lean_z in (-1, 0, 1):
                leans.append((lean_x, lean_y, lean_z))
    return leans


def pool_table():
    voxel = np.arange(512)
    octant_voxel = 16 * (voxel // 128) + 4 * (voxel // 16 % 4) + voxel % 8 // 2
    return (octant_voxel[:, None] == np.arange(64)[None, :]).astype(np.float32)


def octant_table():
    voxel = np.arange(512)
    coord_x = voxel // 64
    coord_y = voxel // 8 % 8
    coord_z = voxel % 8
    octant = 4 * (coord_x // 4) + 2 * (coord_y // 4) + coord_z // 4
    inner = 16 * (coord_x % 4) + 4 * (coord_y % 4) + coord_z % 4
    table = np.zeros((8, 64, 512), np.float32)
    table[octant, inner, voxel] = 1.0
    return table


def flip_weight(weight):
    return jnp.transpose(weight[::-1], (0, 2, 1))


def pool_sum(field_in):
    table = jnp.asarray(pool_table()).astype(jnp.bfloat16)
    return jnp.einsum("bcv,vu->bcu", field_in, table, preferred_element_type=jnp.float32)


def enlarge(octants):
    table = jnp.asarray(pool_table()).astype(jnp.bfloat16)
    return jnp.einsum("bcu,vu->bcv", octants, table, preferred_element_type=jnp.float32)


def place_octants(octants):
    amount, channels = (octants.shape[0] // 8, octants.shape[1])
    grouped = octants.reshape(amount, 8, channels, 64)
    table = jnp.asarray(octant_table()).astype(jnp.bfloat16)
    return jnp.einsum("jocu,ouv->jcv", grouped, table, preferred_element_type=jnp.float32).astype(
        jnp.bfloat16
    )


def split_octants(coarse):
    amount, channels = (coarse.shape[0], coarse.shape[1])
    table = jnp.asarray(octant_table()).astype(jnp.bfloat16)
    parts = jnp.einsum("jcv,ouv->jocu", coarse, table, preferred_element_type=jnp.float32).astype(
        jnp.bfloat16
    )
    return parts.reshape(amount * 8, channels, 64)


def select_rows(picker, values):
    return jnp.dot(picker, values, preferred_element_type=jnp.float32).astype(jnp.bfloat16)


def route_places(slot_list, dev_index, moving, bricks):
    direction = slot_list // bricks - dev_index
    to_left = (direction == -1).astype(jnp.int32)
    to_right = (direction == 1).astype(jnp.int32)
    left_rank = jnp.cumsum(to_left) - to_left
    right_rank = jnp.cumsum(to_right) - to_right
    return jnp.where(
        to_left == 1, left_rank, jnp.where(to_right == 1, moving + right_rank, 2 * moving)
    ).astype(jnp.int32)


def both_sides(widened, moving):
    return jnp.concatenate([widened[:moving], widened[3 * moving :]], axis=0)


def gather_back(local_part, send_pick, returned):
    total = local_part.astype(jnp.float32) + jnp.dot(
        send_pick.T, returned, preferred_element_type=jnp.float32
    )
    return total.astype(jnp.bfloat16)


SPANS = {-1: (slice(0, 1), slice(7, 8)), 0: (slice(1, 9), slice(0, 8)), 1: (slice(9, 10), slice(0, 1))}
KZ_ORDER = np.array([1, 0, 2])


def brick_kernel(with_conv, with_grad, masked, *refs):
    refs = list(refs)
    near_ref, live_ref, table_ref = refs[:3]
    del refs[:3]
    weight_ref = refs.pop(0) if with_conv else None
    grad_ref = refs.pop(0) if with_grad else None
    out_ref = refs.pop(0) if with_conv else None
    total_ref = refs.pop(0) if with_grad else None
    padded, columns = refs
    brick = pl.program_id(0)
    for index, (lean_x, lean_y, lean_z) in enumerate(lean_list()):
        slot = near_ref[brick, index]
        to_x, from_x = SPANS[lean_x]
        to_y, from_y = SPANS[lean_y]
        padded[lean_z + 1, to_x, to_y] = table_ref[slot, from_x, from_y]
    shape = (10, 8, 8, 128)
    place_z = lax.broadcasted_iota(jnp.int32, shape, 2)
    low_half = lax.broadcasted_iota(jnp.int32, shape, 3) < 64
    for tap_y in range(3):
        below = padded[0, :, tap_y : tap_y + 8]
        level = padded[1, :, tap_y : tap_y + 8]
        above = padded[2, :, tap_y : tap_y + 8]
        minus = pltpu.roll(jnp.where(place_z == 7, below, level), 1, 2)
        plus = pltpu.roll(jnp.where(place_z == 0, above, level), 7, 2)
        first = jnp.where(low_half, level, minus).reshape(640, 128)
        second = jnp.where(low_half, plus, 0.0).reshape(640, 128)
        start = 256 * tap_y
        columns[:, start : start + 128] = first.astype(jnp.bfloat16)
        columns[:, start + 128 : start + 256] = second.astype(jnp.bfloat16)
    if with_conv:
        total = None
        for tap_x in range(3):
            part = lax.dot_general(
                weight_ref[tap_x],
                columns[64 * tap_x : 64 * tap_x + 512, :],
                (((1,), (1,)), ((), ())),
                preferred_element_type=jnp.float32,
            )
            total = part if total is None else total + part
        if masked:
            total = jnp.where(brick < live_ref[0], total, 0.0)
        out_ref[0] = total.astype(out_ref.dtype)
    if with_grad:

        @pl.when(brick == 0)
        def clear():
            total_ref[...] = jnp.zeros_like(total_ref)

        for tap_x in range(3):
            total_ref[tap_x] += jnp.dot(
                grad_ref[0],
                columns[64 * tap_x : 64 * tap_x + 512, :],
                preferred_element_type=jnp.float32,
            )


def brick_pass(field_in, near, live_count, weight, grad_rows, out_dtype, masked):
    amount = near.shape[0]
    slots, channels = field_in.shape[:2]
    rows = weight.shape[1] if weight is not None else grad_rows.shape[1]
    table = jnp.transpose(field_in, (0, 2, 1)).astype(jnp.float32)
    table = jnp.concatenate([table, table], axis=2)
    table = jnp.concatenate([table, jnp.zeros((1, 512, 128), jnp.float32)], axis=0)
    table = table.reshape(slots + 1, 8, 8, 8, 128)
    operands = [near, live_count, table]
    in_specs = [
        pl.BlockSpec(memory_space=pltpu.SMEM),
        pl.BlockSpec(memory_space=pltpu.SMEM),
        pl.BlockSpec((slots + 1, 8, 8, 8, 128), lambda b: (0, 0, 0, 0, 0)),
    ]
    outs, out_specs = [], []
    if weight is not None:
        operands.append(weight_blocks(weight))
        in_specs.append(pl.BlockSpec((3, rows, 768), lambda b: (0, 0, 0)))
        outs.append(jax.ShapeDtypeStruct((amount, rows, 512), out_dtype))
        out_specs.append(pl.BlockSpec((1, rows, 512), lambda b: (b, 0, 0)))
    if grad_rows is not None:
        operands.append(grad_rows)
        in_specs.append(pl.BlockSpec((1, rows, 512), lambda b: (b, 0, 0)))
        outs.append(jax.ShapeDtypeStruct((3, rows, 768), jnp.float32))
        out_specs.append(pl.BlockSpec((3, rows, 768), lambda b: (0, 0, 0)))
    products = (weight is not None) + (grad_rows is not None)
    return pl.pallas_call(
        lambda *refs: brick_kernel(weight is not None, grad_rows is not None, masked, *refs),
        grid=(amount,),
        in_specs=in_specs,
        out_specs=out_specs,
        out_shape=outs,
        scratch_shapes=[
            pltpu.VMEM((3, 10, 10, 8, 128), jnp.float32),
            pltpu.VMEM((640, 768), jnp.bfloat16),
        ],
        compiler_params=pltpu.CompilerParams(vmem_limit_bytes=48 * 1024 * 1024),
        cost_estimate=pl.CostEstimate(
            flops=amount * products * 2 * rows * 2304 * 512,
            bytes_accessed=(slots + 1) * 512 * 128 * 4,
            transcendentals=0,
        ),
    )(*operands)


def weight_blocks(weight):
    rows, channels = weight.shape[1:]
    taps = weight.reshape(9, 3, rows, channels)[:, KZ_ORDER]
    taps = jnp.concatenate([taps, jnp.zeros_like(taps[:, :1])], axis=1)
    taps = taps.reshape(3, 3, 4, rows, channels)
    return jnp.transpose(taps, (0, 3, 1, 2, 4)).reshape(3, rows, 768)


def grad_taps(total):
    rows = total.shape[1]
    taps = total.reshape(3, rows, 3, 4, 64)
    taps = jnp.transpose(taps, (0, 2, 3, 1, 4)).reshape(9, 4, rows, 64)[:, KZ_ORDER]
    return taps.reshape(27, rows, 64)


def around(block):
    count = lax.axis_size("space")
    forward = [(i, i + 1) for i in range(count - 1)]
    backward = [(i + 1, i) for i in range(count - 1)]
    low = lax.ppermute(block, "space", forward)
    high = lax.ppermute(block, "space", backward)
    return jnp.concatenate([low, block, high], axis=0)


def sum_over_space(parts):
    sizes = [math.prod(part.shape) for part in parts]
    count = lax.axis_size("space")
    me = lax.axis_index("space")
    flat = jnp.concatenate([part.reshape(-1) for part in parts])
    unit = 1024 * count
    length = -(-sum(sizes) // unit) * unit
    flat = jnp.pad(flat, (0, length - sum(sizes))).reshape(-1, 128)
    strides = [1 << bit for bit in range(count.bit_length() - 1)][::-1]
    for stride in strides:
        upper = me // stride % 2 == 1
        half = flat.shape[0] // 2
        low, high = flat[:half], flat[half:]
        pairs = [(i, i ^ stride) for i in range(count)]
        arrived = lax.ppermute(jnp.where(upper, low, high), "space", pairs)
        flat = jnp.where(upper, high, low) + arrived
    for stride in strides[::-1]:
        upper = me // stride % 2 == 1
        pairs = [(i, i ^ stride) for i in range(count)]
        arrived = lax.ppermute(flat, "space", pairs)
        flat = jnp.where(
            upper, jnp.concatenate([arrived, flat]), jnp.concatenate([flat, arrived])
        )
    flat = flat.reshape(-1)
    totals, start = [], 0
    for part, size in zip(parts, sizes):
        totals.append(flat[start : start + size].reshape(part.shape))
        start += size
    return totals


def per_device(
    feats, live_count, neighbours, parent, fine_weight, coarse_weight, project_weight, cotangent
):
    bricks = feats.shape[0]
    half_channels = feats.shape[1]
    devices = lax.axis_size("space")
    own_index = lax.axis_index("space")
    moving = max(1, bricks // 8)
    coarse_bricks = bricks // 8
    live_mask = (jnp.arange(bricks, dtype=jnp.int32) < live_count[0]).astype(jnp.float32)[
        :, None, None
    ]
    near_parent = extended(parent, (("space", 0),), bricks)
    left_list = near_parent[:bricks]
    right_list = near_parent[2 * bricks :]
    send_place = route_places(parent, own_index, moving, bricks)
    left_place = route_places(left_list, own_index - 1, moving, bricks)
    right_place = route_places(right_list, own_index + 1, moving, bricks)
    local_ok = parent // bricks == own_index
    left_ok = (own_index > 0) & (left_place >= moving) & (left_place < 2 * moving)
    right_ok = (own_index < devices - 1) & (right_place < moving)
    dest_rows = jnp.concatenate([parent % bricks, left_list % bricks, right_list % bricks])
    source_cols = jnp.concatenate(
        [
            jnp.arange(bricks, dtype=jnp.int32),
            bricks + left_place - moving,
            bricks + moving + right_place,
        ]
    )
    valid = jnp.concatenate([local_ok, left_ok, right_ok])
    dest_rows = jnp.where(valid, dest_rows, 0)
    source_cols = jnp.where(valid, source_cols, 0)
    receive_pick = (
        jnp.zeros((bricks, bricks + 2 * moving), jnp.float32)
        .at[dest_rows, source_cols]
        .add(valid.astype(jnp.float32))
        .astype(jnp.bfloat16)
    )
    send_pick = (jnp.arange(2 * moving, dtype=jnp.int32)[:, None] == send_place[None, :]).astype(
        jnp.bfloat16
    )
    pooled = (pool_sum(feats) * 0.125 * live_mask).astype(jnp.bfloat16).reshape(bricks, -1)
    outgoing = select_rows(send_pick, pooled)
    widened = extended(outgoing, (("space", 0),), moving)
    arrived = select_rows(
        receive_pick, jnp.concatenate([pooled, both_sides(widened, moving)], axis=0)
    )
    coarse_half = place_octants(arrived.reshape(bricks, half_channels, 64))
    coarse_in = lax.all_gather(coarse_half, "chan", axis=1, tiled=True)
    lone = jnp.asarray(
        np.array([[0 if lean == (0, 0, 0) else coarse_bricks for lean in lean_list()]] * 1)
    ).astype(jnp.int32)
    lone = jnp.where(
        lone == coarse_bricks, lone, jnp.arange(coarse_bricks, dtype=jnp.int32)[:, None]
    )
    preactivation = brick_pass(
        coarse_in, lone, live_count, coarse_weight, None, jnp.float32, False
    )[0]
    hidden = jax.nn.silu(preactivation).astype(jnp.bfloat16)
    out_terms = jnp.einsum(
        "cj,bjv->bcv", project_weight, hidden, preferred_element_type=jnp.float32
    )
    coarse_out = lax.psum_scatter(out_terms, "chan", scatter_dimension=1, tiled=True).astype(
        jnp.bfloat16
    )
    back_source = select_rows(receive_pick.T, split_octants(coarse_out).reshape(bricks, -1))
    widened_back = extended(back_source[bricks:], (("space", 0),), moving)
    up_octants = gather_back(
        back_source[:bricks], send_pick, both_sides(widened_back, moving)
    ).reshape(bricks, half_channels, 64)
    mixed_feats = ((feats.astype(jnp.float32) + enlarge(up_octants)) * live_mask).astype(
        jnp.bfloat16
    )
    last_brick = devices * bricks
    near_local = jnp.where(
        neighbours >= last_brick, 3 * bricks, neighbours - (own_index - 1) * bricks
    ).astype(jnp.int32)
    slots = jnp.arange(bricks, dtype=jnp.int32)[:, None] + bricks
    near = jnp.concatenate([near_local[:, :13], slots, near_local[:, 13:]], axis=1)
    grad_rows = (cotangent.astype(jnp.float32) * live_mask).astype(jnp.bfloat16)
    grad_table = lax.all_gather(around(grad_rows), "chan", axis=1, tiled=True)
    whole_weight = lax.all_gather(fine_weight, "chan", axis=1, tiled=True)
    own_weight = lax.dynamic_slice_in_dim(
        whole_weight, lax.axis_index("chan") * half_channels, half_channels, 2
    )
    back_feats = brick_pass(
        grad_table, near, live_count, flip_weight(own_weight), None, jnp.bfloat16, True
    )[0]
    feat_table = lax.all_gather(around(mixed_feats), "chan", axis=1, tiled=True)
    out_feats, fine_total = brick_pass(
        feat_table, near, live_count, fine_weight, grad_rows, jnp.bfloat16, True
    )
    up_grad = pool_sum(back_feats).astype(jnp.bfloat16).reshape(bricks, -1)
    outgoing_grad = select_rows(send_pick, up_grad)
    widened_grad = extended(outgoing_grad, (("space", 0),), moving)
    arrived_grad = select_rows(
        receive_pick, jnp.concatenate([up_grad, both_sides(widened_grad, moving)], axis=0)
    )
    coarse_grad_half = place_octants(arrived_grad.reshape(bricks, half_channels, 64))
    coarse_grad = lax.all_gather(coarse_grad_half, "chan", axis=1, tiled=True)
    project_matrix = jnp.einsum(
        "bcv,bjv->cj", coarse_grad, hidden, preferred_element_type=jnp.float32
    )
    hidden_grad = jnp.einsum(
        "cj,bcv->bjv", project_weight, coarse_grad, preferred_element_type=jnp.float32
    )
    sigmoid_pre = jax.nn.sigmoid(preactivation)
    pre_grad = (hidden_grad * sigmoid_pre * (1.0 + preactivation * (1.0 - sigmoid_pre))).astype(
        jnp.bfloat16
    )
    coarse_total = brick_pass(
        coarse_in, lone, live_count, None, pre_grad, None, False
    )[0]
    coarse_terms = brick_pass(
        pre_grad, lone, live_count, flip_weight(coarse_weight), None, jnp.float32, False
    )[0]
    coarse_back = lax.psum_scatter(
        coarse_terms.astype(jnp.bfloat16), "chan", scatter_dimension=1, tiled=True
    )
    down_source = select_rows(receive_pick.T, split_octants(coarse_back).reshape(bricks, -1))
    widened_down = extended(down_source[bricks:], (("space", 0),), moving)
    down_grad = gather_back(
        down_source[:bricks], send_pick, both_sides(widened_down, moving)
    ).reshape(bricks, half_channels, 64)
    grad_feats = (back_feats.astype(jnp.float32) + live_mask * enlarge(down_grad) * 0.125).astype(
        jnp.bfloat16
    )
    fine_sum, coarse_sum, project_total = sum_over_space(
        (grad_taps(fine_total), grad_taps(coarse_total), project_matrix)
    )
    fine_scale = 1.0 / math.sqrt(512.0 * bricks * devices)
    coarse_scale = 1.0 / math.sqrt(512.0 * coarse_bricks * devices)
    fine_weight_grad = fine_sum * fine_scale
    coarse_weight_grad = coarse_sum * coarse_scale
    project_weight_grad = project_total * coarse_scale
    return (out_feats, grad_feats, fine_weight_grad, coarse_weight_grad, project_weight_grad)


def solution(mesh):
    placed = (
        P("space", "chan", None),
        P("space"),
        P("space", None),
        P("space"),
        P(None, "chan", None),
        P(None, "chan", None),
        P(None, "chan"),
        P("space", "chan", None),
    )
    return jax.shard_map(
        per_device,
        mesh=mesh,
        in_specs=placed,
        out_specs=(
            P("space", "chan", None),
            P("space", "chan", None),
            P(None, "chan", None),
            P(None, "chan", None),
            P(None, "chan"),
        ),
        check_vma=False,
    )
```

```python
import math

import jax
import jax.numpy as jnp
import numpy as np
from jax import lax
from jax.experimental import pallas as pl
from jax.experimental.pallas import tpu as pltpu
from jax.sharding import PartitionSpec as P


def lean_list():
    leans = []
    for lean_x in (-1, 0, 1):
        for lean_y in (-1, 0, 1):
            for lean_z in (-1, 0, 1):
                leans.append((lean_x, lean_y, lean_z))
    return leans


def pool_table():
    voxel = np.arange(512)
    octant_voxel = 16 * (voxel // 128) + 4 * (voxel // 16 % 4) + voxel % 8 // 2
    return (octant_voxel[:, None] == np.arange(64)[None, :]).astype(np.float32)


def octant_table():
    voxel = np.arange(512)
    coord_x = voxel // 64
    coord_y = voxel // 8 % 8
    coord_z = voxel % 8
    octant = 4 * (coord_x // 4) + 2 * (coord_y // 4) + coord_z // 4
    inner = 16 * (coord_x % 4) + 4 * (coord_y % 4) + coord_z % 4
    table = np.zeros((8, 64, 512), np.float32)
    table[octant, inner, voxel] = 1.0
    return table


def flip_weight(weight):
    return jnp.transpose(weight[::-1], (0, 2, 1))


def pool_sum(field_in):
    table = jnp.asarray(pool_table()).astype(jnp.bfloat16)
    return jnp.einsum("bcv,vu->bcu", field_in, table, preferred_element_type=jnp.float32)


def enlarge(octants):
    table = jnp.asarray(pool_table()).astype(jnp.bfloat16)
    return jnp.einsum("bcu,vu->bcv", octants, table, preferred_element_type=jnp.float32)


def place_octants(octants):
    amount, channels = (octants.shape[0] // 8, octants.shape[1])
    grouped = octants.reshape(amount, 8, channels, 64)
    table = jnp.asarray(octant_table()).astype(jnp.bfloat16)
    return jnp.einsum("jocu,ouv->jcv", grouped, table, preferred_element_type=jnp.float32).astype(
        jnp.bfloat16
    )


def split_octants(coarse):
    amount, channels = (coarse.shape[0], coarse.shape[1])
    table = jnp.asarray(octant_table()).astype(jnp.bfloat16)
    parts = jnp.einsum("jcv,ouv->jocu", coarse, table, preferred_element_type=jnp.float32).astype(
        jnp.bfloat16
    )
    return parts.reshape(amount * 8, channels, 64)


def select_rows(picker, values):
    return jnp.dot(picker, values, preferred_element_type=jnp.float32).astype(jnp.bfloat16)


def route_places(slot_list, dev_index, moving, bricks):
    direction = slot_list // bricks - dev_index
    to_left = (direction == -1).astype(jnp.int32)
    to_right = (direction == 1).astype(jnp.int32)
    left_rank = jnp.cumsum(to_left) - to_left
    right_rank = jnp.cumsum(to_right) - to_right
    return jnp.where(
        to_left == 1, left_rank, jnp.where(to_right == 1, moving + right_rank, 2 * moving)
    ).astype(jnp.int32)


def from_sides(rows, moving):
    count = lax.axis_size("space")
    low = lax.ppermute(rows[moving:], "space", [(i, i + 1) for i in range(count - 1)])
    high = lax.ppermute(rows[:moving], "space", [(i + 1, i) for i in range(count - 1)])
    return jnp.concatenate([low, high], axis=0)


def lone_bricks(amount):
    centre = jnp.arange(27, dtype=jnp.int32)[None, :] == 13
    return jnp.where(centre, jnp.arange(amount, dtype=jnp.int32)[:, None], amount)


def gather_back(local_part, send_pick, returned):
    total = local_part.astype(jnp.float32) + jnp.dot(
        send_pick.T, returned, preferred_element_type=jnp.float32
    )
    return total.astype(jnp.bfloat16)


SPANS = {-1: (slice(0, 1), slice(7, 8)), 0: (slice(1, 9), slice(0, 8)), 1: (slice(9, 10), slice(0, 1))}
KZ_ORDER = np.array([1, 0, 2])


def brick_kernel(with_conv, with_grad, masked, *refs):
    refs = list(refs)
    near_ref, live_ref, field_ref = refs[:3]
    del refs[:3]
    weight_ref = refs.pop(0) if with_conv else None
    grad_ref = refs.pop(0) if with_grad else None
    out_ref = refs.pop(0) if with_conv else None
    total_ref = refs.pop(0) if with_grad else None
    table, padded, columns = refs
    brick = pl.program_id(0)

    @pl.when(brick == 0)
    def fill():
        slots = field_ref.shape[0]

        def turn(slot, carry):
            field = field_ref[slot].astype(jnp.float32)
            turned = jnp.concatenate([field, field], axis=0).T
            table[slot] = turned.reshape(8, 8, 8, 128)
            return carry

        lax.fori_loop(0, slots, turn, 0)
        table[slots] = jnp.zeros((8, 8, 8, 128), jnp.float32)

    for index, (lean_x, lean_y, lean_z) in enumerate(lean_list()):
        slot = near_ref[brick, index]
        to_x, from_x = SPANS[lean_x]
        to_y, from_y = SPANS[lean_y]
        padded[lean_z + 1, to_x, to_y] = table[slot, from_x, from_y]
    shape = (10, 8, 8, 128)
    place_z = lax.broadcasted_iota(jnp.int32, shape, 2)
    low_half = lax.broadcasted_iota(jnp.int32, shape, 3) < 64
    for tap_y in range(3):
        below = padded[0, :, tap_y : tap_y + 8]
        level = padded[1, :, tap_y : tap_y + 8]
        above = padded[2, :, tap_y : tap_y + 8]
        minus = pltpu.roll(jnp.where(place_z == 7, below, level), 1, 2)
        plus = pltpu.roll(jnp.where(place_z == 0, above, level), 7, 2)
        first = jnp.where(low_half, level, minus).reshape(640, 128)
        second = jnp.where(low_half, plus, 0.0).reshape(640, 128)
        start = 256 * tap_y
        columns[:, start : start + 128] = first.astype(jnp.bfloat16)
        columns[:, start + 128 : start + 256] = second.astype(jnp.bfloat16)
    if with_conv:
        total = None
        for tap_x in range(3):
            part = lax.dot_general(
                weight_ref[0, tap_x],
                columns[64 * tap_x : 64 * tap_x + 512, :],
                (((1,), (1,)), ((), ())),
                preferred_element_type=jnp.float32,
            )
            total = part if total is None else total + part
        if masked:
            total = jnp.where(brick < live_ref[0], total, 0.0)
        out_ref[0] = total.astype(out_ref.dtype)
    if with_grad:

        @pl.when(brick == 0)
        def clear():
            total_ref[...] = jnp.zeros_like(total_ref)

        for tap_x in range(3):
            total_ref[tap_x] += jnp.dot(
                grad_ref[0],
                columns[64 * tap_x : 64 * tap_x + 512, :],
                preferred_element_type=jnp.float32,
            )


def brick_pass(field_in, near, live_count, weight, grad_rows, out_dtype, masked):
    amount = near.shape[0]
    slots = field_in.shape[0]
    rows = weight.shape[2] if weight is not None else grad_rows.shape[1]
    operands = [near, live_count, field_in]
    in_specs = [
        pl.BlockSpec(memory_space=pltpu.SMEM),
        pl.BlockSpec(memory_space=pltpu.SMEM),
        pl.BlockSpec((slots, 64, 512), lambda b: (0, 0, 0)),
    ]
    outs, out_specs = [], []
    if weight is not None:
        parts = weight.shape[0]
        operands.append(jnp.stack([weight_blocks(part) for part in weight]))
        in_specs.append(pl.BlockSpec((1, 3, rows, 768), lambda b: (b % parts, 0, 0, 0)))
        outs.append(jax.ShapeDtypeStruct((amount, rows, 512), out_dtype))
        out_specs.append(pl.BlockSpec((1, rows, 512), lambda b: (b, 0, 0)))
    if grad_rows is not None:
        operands.append(grad_rows)
        in_specs.append(pl.BlockSpec((1, rows, 512), lambda b: (b, 0, 0)))
        outs.append(jax.ShapeDtypeStruct((3, rows, 768), jnp.float32))
        out_specs.append(pl.BlockSpec((3, rows, 768), lambda b: (0, 0, 0)))
    products = (weight is not None) + (grad_rows is not None)
    return pl.pallas_call(
        lambda *refs: brick_kernel(weight is not None, grad_rows is not None, masked, *refs),
        grid=(amount,),
        in_specs=in_specs,
        out_specs=out_specs,
        out_shape=outs,
        scratch_shapes=[
            pltpu.VMEM((slots + 1, 8, 8, 8, 128), jnp.float32),
            pltpu.VMEM((3, 10, 10, 8, 128), jnp.float32),
            pltpu.VMEM((640, 768), jnp.bfloat16),
        ],
        compiler_params=pltpu.CompilerParams(vmem_limit_bytes=48 * 1024 * 1024),
        cost_estimate=pl.CostEstimate(
            flops=amount * products * 2 * rows * 2304 * 512,
            bytes_accessed=slots * 64 * 512 * 2,
            transcendentals=0,
        ),
    )(*operands)


def weight_blocks(weight):
    rows, channels = weight.shape[1:]
    taps = weight.reshape(9, 3, rows, channels)[:, KZ_ORDER]
    taps = jnp.concatenate([taps, jnp.zeros_like(taps[:, :1])], axis=1)
    taps = taps.reshape(3, 3, 4, rows, channels)
    return jnp.transpose(taps, (0, 3, 1, 2, 4)).reshape(3, rows, 768)


def grad_taps(total):
    rows = total.shape[1]
    taps = total.reshape(3, rows, 3, 4, 64)
    taps = jnp.transpose(taps, (0, 2, 3, 1, 4)).reshape(9, 4, rows, 64)[:, KZ_ORDER]
    return taps.reshape(27, rows, 64)


def around(block):
    count = lax.axis_size("space")
    forward = [(i, i + 1) for i in range(count - 1)]
    backward = [(i + 1, i) for i in range(count - 1)]
    low = lax.ppermute(block, "space", forward)
    high = lax.ppermute(block, "space", backward)
    return jnp.concatenate([low, block, high], axis=0)


def torus_sizes(count):
    return (4, 4, 8) if count == 128 else (1, 1, count)


def sum_kernel(sizes, data, total, part_first, part_second, part_last, own_first, own_second,
               whole_last, *sems):
    size_y, size_x, size_z = sizes
    me, core = lax.axis_index("space"), lax.axis_index("chan")
    at_z = me % size_z
    at_x = me // size_z % size_x
    at_y = me // (size_z * size_x)

    def along(axis, step):
        if axis == "x":
            return (at_y * size_x + (at_x + step) % size_x) * size_z + at_z
        if axis == "y":
            return ((at_y + step) % size_y * size_x + at_x) * size_z + at_z
        return (at_y * size_x + at_x) * size_z + (at_z + step) % size_z

    steps = {"x": size_x, "y": size_y, "z": size_z}
    place = {"x": at_x, "y": at_y, "z": at_z}
    orders = (("x", "y"), ("y", "x"))
    barrier = pltpu.get_barrier_semaphore()
    for axis in steps:
        for step in range(1, steps[axis]):
            pl.semaphore_signal(
                barrier,
                inc=1,
                device_id=(along(axis, step), core),
                device_id_type=pl.DeviceIdType.MESH,
            )
    pl.semaphore_wait(barrier, sum(steps.values()) - 3)
    started = []

    def send(source, target, phase, slot, axis, step):
        copy = pltpu.make_async_remote_copy(
            src_ref=source,
            dst_ref=target,
            send_sem=sems[2 * phase].at[slot],
            recv_sem=sems[2 * phase + 1].at[slot],
            device_id=(along(axis, step), core),
            device_id_type=pl.DeviceIdType.MESH,
        )
        copy.start()
        started.append(copy)
        return copy

    first = [(half, orders[half][0], orders[half][1]) for half in range(2)]
    copies = [[], []]
    for half, axis, _ in first:
        for step in range(1, steps[axis]):
            other = (place[axis] + step) % steps[axis]
            slot = half * (steps[axis] - 1) + step - 1
            copies[half].append(
                send(data.at[half, other], part_first.at[slot], 0, slot, axis, step)
            )
    seconds = [[], []]
    for half, axis, axis_two in first:
        value = data[half, place[axis]]
        for step in range(1, steps[axis]):
            copies[half][step - 1].wait_recv()
            value = value + part_first[half * (steps[axis] - 1) + step - 1]
        own_first[half] = value
        for step in range(1, steps[axis_two]):
            other = (place[axis_two] + step) % steps[axis_two]
            slot = half * (steps[axis_two] - 1) + step - 1
            seconds[half].append(
                send(own_first.at[half, other], part_second.at[slot], 1, slot, axis_two, step)
            )
    for half, _, axis in first:
        value = own_first[half, place[axis]]
        for step in range(1, steps[axis]):
            seconds[half][step - 1].wait_recv()
            value = value + part_second[half * (steps[axis] - 1) + step - 1]
        for level in range(size_z):
            own_second[level, half] = value[level]
    lasts = []
    for step in range(1, size_z):
        other = (at_z + step) % size_z
        lasts.append(
            send(own_second.at[other], part_last.at[step - 1], 2, step - 1, "z", step)
        )
    value = own_second[at_z]
    for step in range(1, size_z):
        lasts[step - 1].wait_recv()
        value = value + part_last[step - 1]
    whole_last[at_z] = value
    lasts = []
    for step in range(1, size_z):
        lasts.append(
            send(whole_last.at[at_z], whole_last.at[at_z], 3, step - 1, "z", step)
        )
    for copy in lasts:
        copy.wait_recv()
    seconds = [[], []]
    for half, axis, axis_two in first:
        for level in range(size_z):
            total[half, place[axis], place[axis_two], level] = whole_last[level, half]
        for step in range(1, steps[axis_two]):
            slot = half * (steps[axis_two] - 1) + step - 1
            spot = total.at[half, place[axis], place[axis_two]]
            seconds[half].append(send(spot, spot, 4, slot, axis_two, step))
    copies = []
    for half, axis, axis_two in first:
        for copy in seconds[half]:
            copy.wait_recv()
        spot = total.at[half, place[axis]]
        for step in range(1, steps[axis]):
            slot = half * (steps[axis] - 1) + step - 1
            copies.append(send(spot, spot, 5, slot, axis, step))
    for copy in copies:
        copy.wait_recv()
    for copy in started:
        copy.wait_send()


def sum_tiles(tiles):
    count = lax.axis_size("space")
    sizes = torus_sizes(count)
    side, size_z = sizes[1], sizes[2]
    piece = tiles.shape[0] // (2 * count)
    shape = (2, side, side, size_z, piece, 8, 128)
    peers = max(1, 2 * (side - 1))
    sems = []
    for number in (peers, peers, size_z - 1, size_z - 1, peers, peers):
        sems += [pltpu.SemaphoreType.DMA((number,)), pltpu.SemaphoreType.DMA((number,))]
    summed = pl.pallas_call(
        lambda *refs: sum_kernel(sizes, *refs),
        in_specs=[pl.BlockSpec(memory_space=pltpu.VMEM)],
        out_specs=pl.BlockSpec(memory_space=pltpu.VMEM),
        out_shape=jax.ShapeDtypeStruct(shape, jnp.float32),
        scratch_shapes=[
            pltpu.VMEM((peers,) + shape[2:], jnp.float32),
            pltpu.VMEM((peers,) + shape[3:], jnp.float32),
            pltpu.VMEM((size_z - 1, 2) + shape[4:], jnp.float32),
            pltpu.VMEM((2,) + shape[2:], jnp.float32),
            pltpu.VMEM((size_z, 2) + shape[4:], jnp.float32),
            pltpu.VMEM((size_z, 2) + shape[4:], jnp.float32),
        ]
        + sems,
        compiler_params=pltpu.CompilerParams(
            collective_id=1, has_side_effects=True, vmem_limit_bytes=32 * 1024 * 1024
        ),
        cost_estimate=pl.CostEstimate(
            flops=tiles.size * 4, bytes_accessed=tiles.size * 32, transcendentals=0
        ),
    )(tiles.reshape(shape))
    return summed.reshape(tiles.shape)


def sum_over_space(fine, coarse, project):
    wide = jnp.concatenate([fine.reshape(-1, 768), coarse.reshape(-1, 768)], axis=0)
    tiles = jnp.transpose(wide.reshape(-1, 8, 6, 128), (0, 2, 1, 3)).reshape(-1, 8, 128)
    small = project.reshape(-1, 8, 128)
    count = lax.axis_size("space")
    used = tiles.shape[0] + small.shape[0]
    spare = -used % (2 * count)
    tiles = jnp.concatenate([tiles, small, jnp.zeros((spare, 8, 128), jnp.float32)], axis=0)
    tiles = sum_tiles(tiles)
    wide_tiles = wide.shape[0] // 8 * 6
    wide = jnp.transpose(tiles[:wide_tiles].reshape(-1, 6, 8, 128), (0, 2, 1, 3)).reshape(-1, 768)
    fine_rows = 3 * fine.shape[1]
    return (
        wide[:fine_rows].reshape(fine.shape),
        wide[fine_rows:].reshape(coarse.shape),
        tiles[wide_tiles:used].reshape(project.shape),
    )


def per_device(
    feats, live_count, neighbours, parent, fine_weight, coarse_weight, project_weight, cotangent
):
    bricks = feats.shape[0]
    half_channels = feats.shape[1]
    devices = lax.axis_size("space")
    own_index = lax.axis_index("space")
    moving = max(1, bricks // 8)
    coarse_bricks = bricks // 8
    live_mask = (jnp.arange(bricks, dtype=jnp.int32) < live_count[0]).astype(jnp.float32)[
        :, None, None
    ]
    core = lax.axis_index("chan")
    whole_coarse = lax.all_gather(coarse_weight, "chan", axis=1, tiled=True)
    whole_project = lax.all_gather(project_weight, "chan", axis=1, tiled=True)
    whole_fine = lax.all_gather(fine_weight, "chan", axis=1, tiled=True)
    send_place = route_places(parent, own_index, moving, bricks)
    send_pick = (jnp.arange(2 * moving, dtype=jnp.int32)[:, None] == send_place[None, :]).astype(
        jnp.bfloat16
    )
    pooled = (pool_sum(feats) * 0.125 * live_mask).astype(jnp.bfloat16).reshape(bricks, -1)
    slot_rows = jnp.broadcast_to(
        (parent % bricks + 1).astype(jnp.bfloat16)[:, None], (bricks, 128)
    )
    outgoing = select_rows(send_pick, jnp.concatenate([pooled, slot_rows], axis=1))
    incoming = from_sides(outgoing, moving)
    incoming_slots = incoming[:, -1].astype(jnp.int32) - 1
    local_slots = jnp.where(parent // bricks == own_index, parent % bricks, -1)
    all_slots = jnp.concatenate([local_slots, incoming_slots])
    receive_pick = (jnp.arange(bricks, dtype=jnp.int32)[:, None] == all_slots[None, :]).astype(
        jnp.bfloat16
    )
    arrived = select_rows(receive_pick, jnp.concatenate([pooled, incoming[:, :-128]], axis=0))
    coarse_half = place_octants(arrived.reshape(bricks, half_channels, 64))
    coarse_in = lax.all_gather(coarse_half, "chan", axis=1, tiled=True)
    lone = lone_bricks(coarse_bricks)
    preactivation = brick_pass(
        coarse_in, lone, live_count, whole_coarse[None], None, jnp.float32, False
    )[0]
    hidden = jax.nn.silu(preactivation).astype(jnp.bfloat16)
    own_project = lax.dynamic_slice_in_dim(
        whole_project, core * half_channels, half_channels, 0
    )
    coarse_out = jnp.einsum(
        "cj,bjv->bcv", own_project, hidden, preferred_element_type=jnp.float32
    ).astype(jnp.bfloat16)
    back_source = select_rows(receive_pick.T, split_octants(coarse_out).reshape(bricks, -1))
    up_octants = gather_back(
        back_source[:bricks], send_pick, from_sides(back_source[bricks:], moving)
    ).reshape(bricks, half_channels, 64)
    mixed_feats = ((feats.astype(jnp.float32) + enlarge(up_octants)) * live_mask).astype(
        jnp.bfloat16
    )
    last_brick = devices * bricks
    near_local = jnp.where(
        neighbours >= last_brick, 3 * bricks, neighbours - (own_index - 1) * bricks
    ).astype(jnp.int32)
    slots = jnp.arange(bricks, dtype=jnp.int32)[:, None] + bricks
    near = jnp.concatenate([near_local[:, :13], slots, near_local[:, 13:]], axis=1)
    grad_rows = (cotangent.astype(jnp.float32) * live_mask).astype(jnp.bfloat16)
    grad_table = lax.all_gather(around(grad_rows), "chan", axis=1, tiled=True)
    own_weight = lax.dynamic_slice_in_dim(whole_fine, core * half_channels, half_channels, 2)
    back_feats = brick_pass(
        grad_table, near, live_count, flip_weight(own_weight)[None], None, jnp.bfloat16, True
    )[0]
    feat_table = lax.all_gather(around(mixed_feats), "chan", axis=1, tiled=True)
    out_feats, fine_total = brick_pass(
        feat_table, near, live_count, fine_weight[None], grad_rows, jnp.bfloat16, True
    )
    up_grad = pool_sum(back_feats).astype(jnp.bfloat16).reshape(bricks, -1)
    outgoing_grad = select_rows(send_pick, up_grad)
    arrived_grad = select_rows(
        receive_pick, jnp.concatenate([up_grad, from_sides(outgoing_grad, moving)], axis=0)
    )
    coarse_grad_half = place_octants(arrived_grad.reshape(bricks, half_channels, 64))
    coarse_grad = lax.all_gather(coarse_grad_half, "chan", axis=1, tiled=True)
    hidden_half = hidden.shape[1] // 2
    own_hidden = lax.dynamic_slice_in_dim(hidden, core * hidden_half, hidden_half, 1)
    project_matrix = jnp.einsum(
        "bcv,bjv->cj", coarse_grad, own_hidden, preferred_element_type=jnp.float32
    )
    hidden_grad = jnp.einsum(
        "cj,bcv->bjv", whole_project, coarse_grad, preferred_element_type=jnp.float32
    )
    sigmoid_pre = jax.nn.sigmoid(preactivation)
    pre_grad = (hidden_grad * sigmoid_pre * (1.0 + preactivation * (1.0 - sigmoid_pre))).astype(
        jnp.bfloat16
    )
    own_pre_grad = lax.dynamic_slice_in_dim(pre_grad, core * hidden_half, hidden_half, 1)
    coarse_total = brick_pass(
        coarse_in, lone, live_count, None, own_pre_grad, None, False
    )[0]
    own_coarse = flip_weight(
        lax.dynamic_slice_in_dim(whole_coarse, core * half_channels, half_channels, 2)
    )
    coarse_terms = brick_pass(
        pre_grad.reshape(2 * coarse_bricks, hidden_half, 512),
        lone_bricks(2 * coarse_bricks),
        live_count,
        jnp.stack([own_coarse[:, :, :hidden_half], own_coarse[:, :, hidden_half:]]),
        None,
        jnp.float32,
        False,
    )[0]
    coarse_back = (
        coarse_terms.reshape(coarse_bricks, 2, half_channels, 512).sum(1).astype(jnp.bfloat16)
    )
    down_source = select_rows(receive_pick.T, split_octants(coarse_back).reshape(bricks, -1))
    down_grad = gather_back(
        down_source[:bricks], send_pick, from_sides(down_source[bricks:], moving)
    ).reshape(bricks, half_channels, 64)
    grad_feats = (back_feats.astype(jnp.float32) + live_mask * enlarge(down_grad) * 0.125).astype(
        jnp.bfloat16
    )
    fine_sum, coarse_sum, project_total = sum_over_space(
        fine_total, coarse_total, project_matrix
    )
    fine_sum, coarse_sum = grad_taps(fine_sum), grad_taps(coarse_sum)
    fine_scale = 1.0 / math.sqrt(512.0 * bricks * devices)
    coarse_scale = 1.0 / math.sqrt(512.0 * coarse_bricks * devices)
    fine_weight_grad = fine_sum * fine_scale
    coarse_weight_grad = coarse_sum * coarse_scale
    project_weight_grad = project_total * coarse_scale
    return (out_feats, grad_feats, fine_weight_grad, coarse_weight_grad, project_weight_grad)


def solution(mesh):
    placed = (
        P("space", "chan", None),
        P("space"),
        P("space", None),
        P("space"),
        P(None, "chan", None),
        P(None, "chan", None),
        P(None, "chan"),
        P("space", "chan", None),
    )
    return jax.shard_map(
        per_device,
        mesh=mesh,
        in_specs=placed,
        out_specs=(
            P("space", "chan", None),
            P("space", "chan", None),
            P(None, "chan", None),
            P(None, "chan", None),
            P(None, "chan"),
        ),
        check_vma=False,
    )
```

```python
import math

import jax
import jax.numpy as jnp
import numpy as np
from jax import lax
from jax.experimental import pallas as pl
from jax.experimental.pallas import tpu as pltpu
from jax.sharding import PartitionSpec as P


def lean_list():
    leans = []
    for lean_x in (-1, 0, 1):
        for lean_y in (-1, 0, 1):
            for lean_z in (-1, 0, 1):
                leans.append((lean_x, lean_y, lean_z))
    return leans


def pool_table():
    voxel = np.arange(512)
    octant_voxel = 16 * (voxel // 128) + 4 * (voxel // 16 % 4) + voxel % 8 // 2
    return (octant_voxel[:, None] == np.arange(64)[None, :]).astype(np.float32)


def octant_table():
    voxel = np.arange(512)
    coord_x = voxel // 64
    coord_y = voxel // 8 % 8
    coord_z = voxel % 8
    octant = 4 * (coord_x // 4) + 2 * (coord_y // 4) + coord_z // 4
    inner = 16 * (coord_x % 4) + 4 * (coord_y % 4) + coord_z % 4
    table = np.zeros((8, 64, 512), np.float32)
    table[octant, inner, voxel] = 1.0
    return table


def flip_weight(weight):
    return jnp.transpose(weight[::-1], (0, 2, 1))


def pool_sum(field_in):
    table = jnp.asarray(pool_table()).astype(jnp.bfloat16)
    return jnp.einsum("bcv,vu->bcu", field_in, table, preferred_element_type=jnp.float32)


def enlarge(octants):
    table = jnp.asarray(pool_table()).astype(jnp.bfloat16)
    return jnp.einsum("bcu,vu->bcv", octants, table, preferred_element_type=jnp.float32)


def place_octants(octants):
    amount, channels = (octants.shape[0] // 8, octants.shape[1])
    grouped = octants.reshape(amount, 8, channels, 64)
    table = jnp.asarray(octant_table()).astype(jnp.bfloat16)
    return jnp.einsum("jocu,ouv->jcv", grouped, table, preferred_element_type=jnp.float32).astype(
        jnp.bfloat16
    )


def split_octants(coarse):
    amount, channels = (coarse.shape[0], coarse.shape[1])
    table = jnp.asarray(octant_table()).astype(jnp.bfloat16)
    parts = jnp.einsum("jcv,ouv->jocu", coarse, table, preferred_element_type=jnp.float32).astype(
        jnp.bfloat16
    )
    return parts.reshape(amount * 8, channels, 64)


def select_rows(picker, values):
    return jnp.dot(picker, values, preferred_element_type=jnp.float32).astype(jnp.bfloat16)


def route_places(slot_list, dev_index, moving, bricks):
    direction = slot_list // bricks - dev_index
    to_left = (direction == -1).astype(jnp.int32)
    to_right = (direction == 1).astype(jnp.int32)
    left_rank = jnp.cumsum(to_left) - to_left
    right_rank = jnp.cumsum(to_right) - to_right
    return jnp.where(
        to_left == 1, left_rank, jnp.where(to_right == 1, moving + right_rank, 2 * moving)
    ).astype(jnp.int32)


def lone_bricks(amount):
    centre = jnp.arange(27, dtype=jnp.int32)[None, :] == 13
    return jnp.where(centre, jnp.arange(amount, dtype=jnp.int32)[:, None], amount)


def select_both(picker, body, moved):
    values = jnp.concatenate([body.reshape(2, -1, 2048), moved], axis=1)
    picked = jnp.einsum("rs,csv->rcv", picker, values, preferred_element_type=jnp.float32)
    return picked.astype(jnp.bfloat16).reshape(picker.shape[0], -1, 64)


def gather_back(local_part, send_pick, returned):
    total = local_part.astype(jnp.float32) + jnp.dot(
        send_pick.T, returned, preferred_element_type=jnp.float32
    )
    return total.astype(jnp.bfloat16)


SPANS = {-1: (slice(0, 1), slice(7, 8)), 0: (slice(1, 9), slice(0, 8)), 1: (slice(9, 10), slice(0, 1))}
KZ_ORDER = np.array([1, 0, 2])


def greet(devices):
    barrier = pltpu.get_barrier_semaphore()
    for device in devices:
        pl.semaphore_signal(
            barrier, inc=1, device_id=device, device_id_type=pl.DeviceIdType.MESH
        )
    pl.semaphore_wait(barrier, len(devices))


def nearby(count):
    me, core = lax.axis_index("space"), lax.axis_index("chan")
    return ((me + count - 1) % count, core), ((me + 1) % count, core), (me, 1 - core)


def sender(send_sems, recv_sems):
    def send(number, source, target, device):
        copy = pltpu.make_async_remote_copy(
            src_ref=source,
            dst_ref=target,
            send_sem=send_sems.at[number],
            recv_sem=recv_sems.at[number],
            device_id=device,
            device_id_type=pl.DeviceIdType.MESH,
        )
        copy.start()
        return copy

    return send


def trade_kernel(count, amount, *refs):
    rows, own = refs[:2]
    shares = refs[2 : 2 + amount]
    rows_all, fields = refs[2 + amount : 4 + amount]
    shares_all = refs[4 + amount : 4 + 2 * amount]
    send_sems, recv_sems = refs[4 + 2 * amount :]
    core = lax.axis_index("chan")
    left, right, mate = nearby(count)
    left_mate, right_mate = (left[0], 1 - core), (right[0], 1 - core)
    greet((left, right, mate, left_mate, right_mate))
    send = sender(send_sems, recv_sems)
    quick = [
        send(0, rows.at[0], rows_all.at[core, 1], left),
        send(1, rows.at[1], rows_all.at[core, 0], right),
        send(2, rows.at[0], rows_all.at[core, 1], left_mate),
        send(3, rows.at[1], rows_all.at[core, 0], right_mate),
    ]
    to_right = send(4, own, fields.at[core, 0], right)
    to_left = send(5, own, fields.at[core, 2], left)
    for number, (share, share_all) in enumerate(zip(shares, shares_all)):
        quick.append(send(8 + number, share, share_all.at[core], mate))
        share_all[core] = share[...]
    quick.append(send(8 + amount, own, fields.at[core, 1], mate))
    fields[core, 1] = own[...]
    to_right.wait_recv()
    quick.append(send(6, fields.at[core, 0], fields.at[core, 0], mate))
    to_left.wait_recv()
    quick.append(send(7, fields.at[core, 2], fields.at[core, 2], mate))
    for copy in quick:
        copy.wait_recv()
    for copy in quick + [to_right, to_left]:
        copy.wait_send()


def trade(rows, own, shares, number):
    count = lax.axis_size("space")
    amount = len(shares)
    shapes = [(2,) + rows.shape, (2, 3) + own.shape] + [(2,) + share.shape for share in shares]
    return pl.pallas_call(
        lambda *refs: trade_kernel(count, amount, *refs),
        in_specs=[pl.BlockSpec(memory_space=pltpu.VMEM)] * (2 + amount),
        out_specs=[pl.BlockSpec(memory_space=pltpu.VMEM)] * (2 + amount),
        out_shape=[jax.ShapeDtypeStruct(shape, rows.dtype) for shape in shapes],
        scratch_shapes=[
            pltpu.SemaphoreType.DMA((9 + amount,)),
            pltpu.SemaphoreType.DMA((9 + amount,)),
        ],
        compiler_params=pltpu.CompilerParams(
            collective_id=number, has_side_effects=True, vmem_limit_bytes=32 * 1024 * 1024
        ),
    )(rows, own, *shares)


def ride_along(count, ride, ride_out, ride_in, send_sems, recv_sems):
    brick = pl.program_id(0)
    left, right, _ = nearby(count)

    def copies():
        return [
            pltpu.make_async_remote_copy(
                src_ref=ride.at[side],
                dst_ref=ride_in.at[1 - side],
                send_sem=send_sems.at[side],
                recv_sem=recv_sems.at[side],
                device_id=device,
                device_id_type=pl.DeviceIdType.MESH,
            )
            for side, device in enumerate((left, right))
        ]

    @pl.when(brick == 0)
    def hail():
        barrier = pltpu.get_barrier_semaphore()
        for device in (left, right):
            pl.semaphore_signal(
                barrier, inc=1, device_id=device, device_id_type=pl.DeviceIdType.MESH
            )

    @pl.when(brick == 1)
    def depart():
        pl.semaphore_wait(pltpu.get_barrier_semaphore(), 2)
        for copy in copies():
            copy.start()

    @pl.when(brick == pl.num_programs(0) - 1)
    def arrive():
        for copy in copies():
            copy.wait()
        ride_out[...] = ride_in[...]


def brick_kernel(count, with_conv, with_grad, masked, *refs):
    refs = list(refs)
    near_ref, live_ref, field_ref = refs[:3]
    del refs[:3]
    weight_ref = refs.pop(0) if with_conv else None
    grad_ref = refs.pop(0) if with_grad else None
    ride_ref = refs.pop(0) if count else None
    out_ref = refs.pop(0) if with_conv else None
    total_ref = refs.pop(0) if with_grad else None
    ride_out = refs.pop(0) if count else None
    table, padded, columns = refs[:3]
    brick = pl.program_id(0)
    if count:
        ride_along(count, ride_ref, ride_out, *refs[3:])

    @pl.when(brick == 0)
    def fill():
        slots = table.shape[0] - 1
        table[slots] = jnp.zeros((8, 8, 8, 128), jnp.float32)
        halves = len(field_ref.shape) == 5
        amount = field_ref.shape[2]

        def turn(slot, carry):
            if halves:
                place, one = slot // amount, slot % amount
                field = jnp.concatenate(
                    [field_ref[0, place, one], field_ref[1, place, one]], axis=0
                ).astype(jnp.float32)
            else:
                field = field_ref[slot].astype(jnp.float32)
            turned = jnp.concatenate([field, field], axis=0).T
            table[slot] = turned.reshape(8, 8, 8, 128)
            return carry

        lax.fori_loop(0, slots, turn, 0)

    for index, (lean_x, lean_y, lean_z) in enumerate(lean_list()):
        slot = near_ref[brick, index]
        to_x, from_x = SPANS[lean_x]
        to_y, from_y = SPANS[lean_y]
        padded[lean_z + 1, to_x, to_y] = table[slot, from_x, from_y]
    shape = (10, 8, 8, 128)
    place_z = lax.broadcasted_iota(jnp.int32, shape, 2)
    low_half = lax.broadcasted_iota(jnp.int32, shape, 3) < 64
    for tap_y in range(3):
        below = padded[0, :, tap_y : tap_y + 8]
        level = padded[1, :, tap_y : tap_y + 8]
        above = padded[2, :, tap_y : tap_y + 8]
        minus = pltpu.roll(jnp.where(place_z == 7, below, level), 1, 2)
        plus = pltpu.roll(jnp.where(place_z == 0, above, level), 7, 2)
        first = jnp.where(low_half, level, minus).reshape(640, 128)
        second = jnp.where(low_half, plus, 0.0).reshape(640, 128)
        start = 256 * tap_y
        columns[:, start : start + 128] = first.astype(jnp.bfloat16)
        columns[:, start + 128 : start + 256] = second.astype(jnp.bfloat16)
    if with_conv:
        total = None
        for tap_x in range(3):
            part = lax.dot_general(
                weight_ref[0, tap_x],
                columns[64 * tap_x : 64 * tap_x + 512, :],
                (((1,), (1,)), ((), ())),
                preferred_element_type=jnp.float32,
            )
            total = part if total is None else total + part
        if masked:
            total = jnp.where(brick < live_ref[0], total, 0.0)
        out_ref[0] = total.astype(out_ref.dtype)
    if with_grad:

        @pl.when(brick == 0)
        def clear():
            total_ref[...] = jnp.zeros_like(total_ref)

        for tap_x in range(3):
            total_ref[tap_x] += jnp.dot(
                grad_ref[0],
                columns[64 * tap_x : 64 * tap_x + 512, :],
                preferred_element_type=jnp.float32,
            )


def brick_pass(
    field_in, near, live_count, weight, grad_rows, out_dtype, masked, ride=None, number=None
):
    amount = near.shape[0]
    count = 0 if ride is None else lax.axis_size("space")
    slots = 3 * field_in.shape[2] if field_in.ndim == 5 else field_in.shape[0]
    rows = weight.shape[2] if weight is not None else grad_rows.shape[1]
    operands = [near, live_count, field_in]
    in_specs = [
        pl.BlockSpec(memory_space=pltpu.SMEM),
        pl.BlockSpec(memory_space=pltpu.SMEM),
        pl.BlockSpec(field_in.shape, lambda b: (0,) * field_in.ndim),
    ]
    outs, out_specs = [], []
    if weight is not None:
        parts = weight.shape[0]
        operands.append(jnp.stack([weight_blocks(part) for part in weight]))
        in_specs.append(pl.BlockSpec((1, 3, rows, 768), lambda b: (b % parts, 0, 0, 0)))
        outs.append(jax.ShapeDtypeStruct((amount, rows, 512), out_dtype))
        out_specs.append(pl.BlockSpec((1, rows, 512), lambda b: (b, 0, 0)))
    if grad_rows is not None:
        operands.append(grad_rows)
        in_specs.append(pl.BlockSpec((1, rows, 512), lambda b: (b, 0, 0)))
        outs.append(jax.ShapeDtypeStruct((3, rows, 768), jnp.float32))
        out_specs.append(pl.BlockSpec((3, rows, 768), lambda b: (0, 0, 0)))
    scratch = [
        pltpu.VMEM((slots + 1, 8, 8, 8, 128), jnp.float32),
        pltpu.VMEM((3, 10, 10, 8, 128), jnp.float32),
        pltpu.VMEM((640, 768), jnp.bfloat16),
    ]
    if count:
        operands.append(ride)
        in_specs.append(pl.BlockSpec(ride.shape, lambda b: (0, 0, 0)))
        outs.append(jax.ShapeDtypeStruct(ride.shape, ride.dtype))
        out_specs.append(pl.BlockSpec(ride.shape, lambda b: (0, 0, 0)))
        scratch += [
            pltpu.VMEM(ride.shape, ride.dtype),
            pltpu.SemaphoreType.DMA((2,)),
            pltpu.SemaphoreType.DMA((2,)),
        ]
    remote = {"collective_id": number, "has_side_effects": True} if count else {}
    products = (weight is not None) + (grad_rows is not None)
    return pl.pallas_call(
        lambda *refs: brick_kernel(count, weight is not None, grad_rows is not None, masked, *refs),
        grid=(amount,),
        in_specs=in_specs,
        out_specs=out_specs,
        out_shape=outs,
        scratch_shapes=scratch,
        compiler_params=pltpu.CompilerParams(vmem_limit_bytes=48 * 1024 * 1024, **remote),
        cost_estimate=pl.CostEstimate(
            flops=amount * products * 2 * rows * 2304 * 512,
            bytes_accessed=slots * 64 * 512 * 2,
            transcendentals=0,
        ),
    )(*operands)


def weight_blocks(weight):
    rows, channels = weight.shape[1:]
    taps = weight.reshape(9, 3, rows, channels)[:, KZ_ORDER]
    taps = jnp.concatenate([taps, jnp.zeros_like(taps[:, :1])], axis=1)
    taps = taps.reshape(3, 3, 4, rows, channels)
    return jnp.transpose(taps, (0, 3, 1, 2, 4)).reshape(3, rows, 768)


def torus_sizes(count):
    return (4, 4, 8) if count == 128 else (1, 1, count)


def sum_kernel(sizes, data, total, part_first, part_second, part_last, own_first, own_second,
               whole_last, *sems):
    size_y, size_x, size_z = sizes
    me, core = lax.axis_index("space"), lax.axis_index("chan")
    at_z = me % size_z
    at_x = me // size_z % size_x
    at_y = me // (size_z * size_x)

    def along(axis, step):
        if axis == "x":
            return (at_y * size_x + (at_x + step) % size_x) * size_z + at_z
        if axis == "y":
            return ((at_y + step) % size_y * size_x + at_x) * size_z + at_z
        return (at_y * size_x + at_x) * size_z + (at_z + step) % size_z

    steps = {"x": size_x, "y": size_y, "z": size_z}
    place = {"x": at_x, "y": at_y, "z": at_z}
    orders = (("x", "y"), ("y", "x"))
    barrier = pltpu.get_barrier_semaphore()
    for axis in steps:
        for step in range(1, steps[axis]):
            pl.semaphore_signal(
                barrier,
                inc=1,
                device_id=(along(axis, step), core),
                device_id_type=pl.DeviceIdType.MESH,
            )
    pl.semaphore_wait(barrier, sum(steps.values()) - 3)
    started = []

    def send(source, target, phase, slot, axis, step):
        copy = pltpu.make_async_remote_copy(
            src_ref=source,
            dst_ref=target,
            send_sem=sems[2 * phase].at[slot],
            recv_sem=sems[2 * phase + 1].at[slot],
            device_id=(along(axis, step), core),
            device_id_type=pl.DeviceIdType.MESH,
        )
        copy.start()
        started.append(copy)
        return copy

    first = [(half, orders[half][0], orders[half][1]) for half in range(2)]
    copies = [[], []]
    for half, axis, _ in first:
        for step in range(1, steps[axis]):
            other = (place[axis] + step) % steps[axis]
            slot = half * (steps[axis] - 1) + step - 1
            copies[half].append(
                send(data.at[half, other], part_first.at[slot], 0, slot, axis, step)
            )
    seconds = [[], []]
    for half, axis, axis_two in first:
        value = data[half, place[axis]]
        for step in range(1, steps[axis]):
            copies[half][step - 1].wait_recv()
            value = value + part_first[half * (steps[axis] - 1) + step - 1]
        own_first[half] = value
        for step in range(1, steps[axis_two]):
            other = (place[axis_two] + step) % steps[axis_two]
            slot = half * (steps[axis_two] - 1) + step - 1
            seconds[half].append(
                send(own_first.at[half, other], part_second.at[slot], 1, slot, axis_two, step)
            )
    for half, _, axis in first:
        value = own_first[half, place[axis]]
        for step in range(1, steps[axis]):
            seconds[half][step - 1].wait_recv()
            value = value + part_second[half * (steps[axis] - 1) + step - 1]
        for level in range(size_z):
            own_second[level, half] = value[level]
    lasts = []
    for step in range(1, size_z):
        other = (at_z + step) % size_z
        lasts.append(
            send(own_second.at[other], part_last.at[step - 1], 2, step - 1, "z", step)
        )
    value = own_second[at_z]
    for step in range(1, size_z):
        lasts[step - 1].wait_recv()
        value = value + part_last[step - 1]
    whole_last[at_z] = value
    lasts = []
    for step in range(1, size_z):
        lasts.append(
            send(whole_last.at[at_z], whole_last.at[at_z], 3, step - 1, "z", step)
        )
    for copy in lasts:
        copy.wait_recv()
    seconds = [[], []]
    for half, axis, axis_two in first:
        for level in range(size_z):
            total[half, place[axis], place[axis_two], level] = whole_last[level, half]
        for step in range(1, steps[axis_two]):
            slot = half * (steps[axis_two] - 1) + step - 1
            spot = total.at[half, place[axis], place[axis_two]]
            seconds[half].append(send(spot, spot, 4, slot, axis_two, step))
    copies = []
    for half, axis, axis_two in first:
        for copy in seconds[half]:
            copy.wait_recv()
        spot = total.at[half, place[axis]]
        for step in range(1, steps[axis]):
            slot = half * (steps[axis] - 1) + step - 1
            copies.append(send(spot, spot, 5, slot, axis, step))
    for copy in copies:
        copy.wait_recv()
    for copy in started:
        copy.wait_send()


def sum_tiles(tiles):
    count = lax.axis_size("space")
    sizes = torus_sizes(count)
    side, size_z = sizes[1], sizes[2]
    piece = tiles.shape[0] // (2 * count)
    shape = (2, side, side, size_z, piece, 8, 128)
    peers = max(1, 2 * (side - 1))
    sems = []
    for number in (peers, peers, size_z - 1, size_z - 1, peers, peers):
        sems += [pltpu.SemaphoreType.DMA((number,)), pltpu.SemaphoreType.DMA((number,))]
    summed = pl.pallas_call(
        lambda *refs: sum_kernel(sizes, *refs),
        in_specs=[pl.BlockSpec(memory_space=pltpu.VMEM)],
        out_specs=pl.BlockSpec(memory_space=pltpu.VMEM),
        out_shape=jax.ShapeDtypeStruct(shape, jnp.float32),
        scratch_shapes=[
            pltpu.VMEM((peers,) + shape[2:], jnp.float32),
            pltpu.VMEM((peers,) + shape[3:], jnp.float32),
            pltpu.VMEM((size_z - 1, 2) + shape[4:], jnp.float32),
            pltpu.VMEM((2,) + shape[2:], jnp.float32),
            pltpu.VMEM((size_z, 2) + shape[4:], jnp.float32),
            pltpu.VMEM((size_z, 2) + shape[4:], jnp.float32),
        ]
        + sems,
        compiler_params=pltpu.CompilerParams(
            collective_id=1, has_side_effects=True, vmem_limit_bytes=32 * 1024 * 1024
        ),
        cost_estimate=pl.CostEstimate(
            flops=tiles.size * 4, bytes_accessed=tiles.size * 32, transcendentals=0
        ),
    )(tiles.reshape(shape))
    return summed.reshape(tiles.shape)


def finish_kernel(places, tiles, *outs):
    for (start, scale), out in zip(places, outs):
        blocks = out.shape[1] // 8
        for tap_x in range(3):
            for block in range(blocks):
                first = start + 6 * (tap_x * blocks + block)
                for tap_y in range(3):
                    pair = tiles[first + 2 * tap_y]
                    last = tiles[first + 2 * tap_y + 1]
                    rows = slice(8 * block, 8 * block + 8)
                    tap = 9 * tap_x + 3 * tap_y
                    out[tap, rows, :] = pair[:, 64:] * scale
                    out[tap + 1, rows, :] = pair[:, :64] * scale
                    out[tap + 2, rows, :] = last[:, :64] * scale


def sum_over_space(fine, coarse, project, fine_scale, coarse_scale):
    wide = jnp.concatenate([fine.reshape(-1, 768), coarse.reshape(-1, 768)], axis=0)
    tiles = jnp.transpose(wide.reshape(-1, 8, 6, 128), (0, 2, 1, 3)).reshape(-1, 8, 128)
    small = project.reshape(-1, 8, 128)
    count = lax.axis_size("space")
    fine_tiles = 3 * fine.shape[1] // 8 * 6
    used = tiles.shape[0] + small.shape[0]
    spare = -used % (2 * count)
    tiles = jnp.concatenate([tiles, small, jnp.zeros((spare, 8, 128), jnp.float32)], axis=0)
    tiles = sum_tiles(tiles)
    places = ((0, fine_scale), (fine_tiles, coarse_scale))
    fine_sum, coarse_sum = pl.pallas_call(
        lambda *refs: finish_kernel(places, *refs),
        in_specs=[pl.BlockSpec(memory_space=pltpu.VMEM)],
        out_specs=[pl.BlockSpec(memory_space=pltpu.VMEM)] * 2,
        out_shape=[
            jax.ShapeDtypeStruct((27, fine.shape[1], 64), jnp.float32),
            jax.ShapeDtypeStruct((27, coarse.shape[1], 64), jnp.float32),
        ],
    )(tiles)
    return fine_sum, coarse_sum, tiles[used - small.shape[0] : used].reshape(project.shape)


def per_device(
    feats, live_count, neighbours, parent, fine_weight, coarse_weight, project_weight, cotangent
):
    bricks = feats.shape[0]
    half_channels = feats.shape[1]
    devices = lax.axis_size("space")
    own_index = lax.axis_index("space")
    moving = max(1, bricks // 8)
    coarse_bricks = bricks // 8
    live_mask = (jnp.arange(bricks, dtype=jnp.int32) < live_count[0]).astype(jnp.float32)[
        :, None, None
    ]
    core = lax.axis_index("chan")
    send_place = route_places(parent, own_index, moving, bricks)
    send_pick = (jnp.arange(2 * moving, dtype=jnp.int32)[:, None] == send_place[None, :]).astype(
        jnp.bfloat16
    )
    pooled = (pool_sum(feats) * 0.125 * live_mask).astype(jnp.bfloat16).reshape(bricks, -1)
    slot_rows = jnp.broadcast_to(
        (parent % bricks + 1).astype(jnp.bfloat16)[:, None], (bricks, 2048)
    )
    outgoing = select_rows(send_pick, jnp.concatenate([pooled, slot_rows], axis=1))
    grad_rows = (cotangent.astype(jnp.float32) * live_mask).astype(jnp.bfloat16)
    incoming, grad_fields, both_pooled, both_coarse, both_fine, both_project = trade(
        outgoing.reshape(2, moving * 32, 128),
        grad_rows,
        [pooled.reshape(bricks * 16, 128), coarse_weight, fine_weight, project_weight],
        2,
    )
    whole_coarse = jnp.concatenate([both_coarse[0], both_coarse[1]], axis=1)
    whole_fine = jnp.concatenate([both_fine[0], both_fine[1]], axis=1)
    whole_project = jnp.concatenate([both_project[0], both_project[1]], axis=1)
    incoming = incoming.reshape(2, 2 * moving, 4096)
    incoming_slots = incoming[0, :, -1].astype(jnp.int32) - 1
    local_slots = jnp.where(parent // bricks == own_index, parent % bricks, -1)
    all_slots = jnp.concatenate([local_slots, incoming_slots])
    receive_pick = (jnp.arange(bricks, dtype=jnp.int32)[:, None] == all_slots[None, :]).astype(
        jnp.bfloat16
    )
    arrived = select_both(receive_pick, both_pooled, incoming[:, :, :2048])
    coarse_in = place_octants(arrived)
    lone = lone_bricks(coarse_bricks)
    preactivation = brick_pass(
        coarse_in, lone, live_count, whole_coarse[None], None, jnp.float32, False
    )[0]
    hidden = jax.nn.silu(preactivation).astype(jnp.bfloat16)
    own_project = lax.dynamic_slice_in_dim(
        whole_project, core * half_channels, half_channels, 0
    )
    coarse_out = jnp.einsum(
        "cj,bjv->bcv", own_project, hidden, preferred_element_type=jnp.float32
    ).astype(jnp.bfloat16)
    back_source = select_rows(receive_pick.T, split_octants(coarse_out).reshape(bricks, -1))
    last_brick = devices * bricks
    near_local = jnp.where(
        neighbours >= last_brick, 3 * bricks, neighbours - (own_index - 1) * bricks
    ).astype(jnp.int32)
    slots = jnp.arange(bricks, dtype=jnp.int32)[:, None] + bricks
    near = jnp.concatenate([near_local[:, :13], slots, near_local[:, 13:]], axis=1)
    own_weight = lax.dynamic_slice_in_dim(whole_fine, core * half_channels, half_channels, 2)
    back_feats, rode_back = brick_pass(
        grad_fields,
        near,
        live_count,
        flip_weight(own_weight)[None],
        None,
        jnp.bfloat16,
        True,
        back_source[bricks:].reshape(2, moving * 16, 128),
        3,
    )
    up_octants = gather_back(
        back_source[:bricks], send_pick, rode_back.reshape(2 * moving, -1)
    ).reshape(bricks, half_channels, 64)
    mixed_feats = ((feats.astype(jnp.float32) + enlarge(up_octants)) * live_mask).astype(
        jnp.bfloat16
    )
    up_grad = pool_sum(back_feats).astype(jnp.bfloat16).reshape(bricks, -1)
    outgoing_grad = select_rows(send_pick, up_grad)
    incoming_grad, feat_fields, both_grad = trade(
        outgoing_grad.reshape(2, moving * 16, 128),
        mixed_feats,
        [up_grad.reshape(bricks * 16, 128)],
        4,
    )
    coarse_grad = place_octants(
        select_both(receive_pick, both_grad, incoming_grad.reshape(2, 2 * moving, 2048))
    )
    hidden_half = hidden.shape[1] // 2
    own_hidden = lax.dynamic_slice_in_dim(hidden, core * hidden_half, hidden_half, 1)
    project_matrix = jnp.einsum(
        "bcv,bjv->cj", coarse_grad, own_hidden, preferred_element_type=jnp.float32
    )
    hidden_grad = jnp.einsum(
        "cj,bcv->bjv", whole_project, coarse_grad, preferred_element_type=jnp.float32
    )
    sigmoid_pre = jax.nn.sigmoid(preactivation)
    pre_grad = (hidden_grad * sigmoid_pre * (1.0 + preactivation * (1.0 - sigmoid_pre))).astype(
        jnp.bfloat16
    )
    own_pre_grad = lax.dynamic_slice_in_dim(pre_grad, core * hidden_half, hidden_half, 1)
    coarse_total = brick_pass(
        coarse_in, lone, live_count, None, own_pre_grad, None, False
    )[0]
    own_coarse = flip_weight(
        lax.dynamic_slice_in_dim(whole_coarse, core * half_channels, half_channels, 2)
    )
    coarse_terms = brick_pass(
        pre_grad.reshape(2 * coarse_bricks, hidden_half, 512),
        lone_bricks(2 * coarse_bricks),
        live_count,
        jnp.stack([own_coarse[:, :, :hidden_half], own_coarse[:, :, hidden_half:]]),
        None,
        jnp.float32,
        False,
    )[0]
    coarse_back = (
        coarse_terms.reshape(coarse_bricks, 2, half_channels, 512).sum(1).astype(jnp.bfloat16)
    )
    down_source = select_rows(receive_pick.T, split_octants(coarse_back).reshape(bricks, -1))
    out_feats, fine_total, rode_down = brick_pass(
        feat_fields,
        near,
        live_count,
        fine_weight[None],
        grad_rows,
        jnp.bfloat16,
        True,
        down_source[bricks:].reshape(2, moving * 16, 128),
        5,
    )
    down_grad = gather_back(
        down_source[:bricks], send_pick, rode_down.reshape(2 * moving, -1)
    ).reshape(bricks, half_channels, 64)
    grad_feats = (back_feats.astype(jnp.float32) + live_mask * enlarge(down_grad) * 0.125).astype(
        jnp.bfloat16
    )
    fine_scale = 1.0 / math.sqrt(512.0 * bricks * devices)
    coarse_scale = 1.0 / math.sqrt(512.0 * coarse_bricks * devices)
    fine_weight_grad, coarse_weight_grad, project_total = sum_over_space(
        fine_total, coarse_total, project_matrix, fine_scale, coarse_scale
    )
    project_weight_grad = project_total * coarse_scale
    return (out_feats, grad_feats, fine_weight_grad, coarse_weight_grad, project_weight_grad)


def solution(mesh):
    placed = (
        P("space", "chan", None),
        P("space"),
        P("space", None),
        P("space"),
        P(None, "chan", None),
        P(None, "chan", None),
        P(None, "chan"),
        P("space", "chan", None),
    )
    return jax.shard_map(
        per_device,
        mesh=mesh,
        in_specs=placed,
        out_specs=(
            P("space", "chan", None),
            P("space", "chan", None),
            P(None, "chan", None),
            P(None, "chan", None),
            P(None, "chan"),
        ),
        check_vma=False,
    )
```

```python
import math

import jax
import jax.numpy as jnp
import numpy as np
from jax import lax
from jax.experimental import pallas as pl
from jax.experimental.pallas import tpu as pltpu
from jax.sharding import PartitionSpec as P


def lean_list():
    leans = []
    for lean_x in (-1, 0, 1):
        for lean_y in (-1, 0, 1):
            for lean_z in (-1, 0, 1):
                leans.append((lean_x, lean_y, lean_z))
    return leans


def pool_table():
    voxel = np.arange(512)
    octant_voxel = 16 * (voxel // 128) + 4 * (voxel // 16 % 4) + voxel % 8 // 2
    return (octant_voxel[:, None] == np.arange(64)[None, :]).astype(np.float32)


def octant_table():
    voxel = np.arange(512)
    coord_x = voxel // 64
    coord_y = voxel // 8 % 8
    coord_z = voxel % 8
    octant = 4 * (coord_x // 4) + 2 * (coord_y // 4) + coord_z // 4
    inner = 16 * (coord_x % 4) + 4 * (coord_y % 4) + coord_z % 4
    table = np.zeros((8, 64, 512), np.float32)
    table[octant, inner, voxel] = 1.0
    return table


def flip_weight(weight):
    return jnp.transpose(weight[::-1], (0, 2, 1))


def pool_sum(field_in):
    table = jnp.asarray(pool_table()).astype(jnp.bfloat16)
    return jnp.einsum("bcv,vu->bcu", field_in, table, preferred_element_type=jnp.float32)


def enlarge(octants):
    table = jnp.asarray(pool_table()).astype(jnp.bfloat16)
    return jnp.einsum("bcu,vu->bcv", octants, table, preferred_element_type=jnp.float32)


def place_octants(octants):
    amount, channels = (octants.shape[0] // 8, octants.shape[1])
    grouped = octants.reshape(amount, 8, channels, 64)
    table = jnp.asarray(octant_table()).astype(jnp.bfloat16)
    return jnp.einsum("jocu,ouv->jcv", grouped, table, preferred_element_type=jnp.float32).astype(
        jnp.bfloat16
    )


def split_octants(coarse):
    amount, channels = (coarse.shape[0], coarse.shape[1])
    table = jnp.asarray(octant_table()).astype(jnp.bfloat16)
    parts = jnp.einsum("jcv,ouv->jocu", coarse, table, preferred_element_type=jnp.float32).astype(
        jnp.bfloat16
    )
    return parts.reshape(amount * 8, channels, 64)


def select_rows(picker, values):
    return jnp.dot(picker, values, preferred_element_type=jnp.float32).astype(jnp.bfloat16)


def route_places(slot_list, dev_index, moving, bricks):
    direction = slot_list // bricks - dev_index
    to_left = (direction == -1).astype(jnp.int32)
    to_right = (direction == 1).astype(jnp.int32)
    left_rank = jnp.cumsum(to_left) - to_left
    right_rank = jnp.cumsum(to_right) - to_right
    return jnp.where(
        to_left == 1, left_rank, jnp.where(to_right == 1, moving + right_rank, 2 * moving)
    ).astype(jnp.int32)


def lone_bricks(amount):
    centre = jnp.arange(27, dtype=jnp.int32)[None, :] == 13
    return jnp.where(centre, jnp.arange(amount, dtype=jnp.int32)[:, None], amount)


def select_both(picker, body, moved):
    values = jnp.concatenate([body.reshape(2, -1, 2048), moved], axis=1)
    picked = jnp.einsum("rs,csv->rcv", picker, values, preferred_element_type=jnp.float32)
    return picked.astype(jnp.bfloat16).reshape(picker.shape[0], -1, 64)


def gather_back(local_part, send_pick, returned):
    total = local_part.astype(jnp.float32) + jnp.dot(
        send_pick.T, returned, preferred_element_type=jnp.float32
    )
    return total.astype(jnp.bfloat16)


SPANS = {-1: (slice(0, 1), slice(7, 8)), 0: (slice(1, 9), slice(0, 8)), 1: (slice(9, 10), slice(0, 1))}
TAP_ORDER = np.array([1, 0, 2, 5, 4, 3, 7, 6, 8])
WIDTH = 640


def greet(devices):
    barrier = pltpu.get_barrier_semaphore()
    for device in devices:
        pl.semaphore_signal(
            barrier, inc=1, device_id=device, device_id_type=pl.DeviceIdType.MESH
        )
    pl.semaphore_wait(barrier, len(devices))


def nearby(count):
    me, core = lax.axis_index("space"), lax.axis_index("chan")
    return ((me + count - 1) % count, core), ((me + 1) % count, core), (me, 1 - core)


def sender(send_sems, recv_sems):
    def send(number, source, target, device):
        copy = pltpu.make_async_remote_copy(
            src_ref=source,
            dst_ref=target,
            send_sem=send_sems.at[number],
            recv_sem=recv_sems.at[number],
            device_id=device,
            device_id_type=pl.DeviceIdType.MESH,
        )
        copy.start()
        return copy

    return send


def trade_kernel(count, amount, *refs):
    rows, own = refs[:2]
    shares = refs[2 : 2 + amount]
    rows_all, fields = refs[2 + amount : 4 + amount]
    shares_all = refs[4 + amount : 4 + 2 * amount]
    send_sems, recv_sems = refs[4 + 2 * amount :]
    core = lax.axis_index("chan")
    left, right, mate = nearby(count)
    left_mate, right_mate = (left[0], 1 - core), (right[0], 1 - core)
    greet((left, right, mate, left_mate, right_mate))
    send = sender(send_sems, recv_sems)
    quick = [
        send(0, rows.at[0], rows_all.at[core, 1], left),
        send(1, rows.at[1], rows_all.at[core, 0], right),
        send(2, rows.at[0], rows_all.at[core, 1], left_mate),
        send(3, rows.at[1], rows_all.at[core, 0], right_mate),
    ]
    to_right = send(4, own, fields.at[core, 0], right)
    to_left = send(5, own, fields.at[core, 2], left)
    for number, (share, share_all) in enumerate(zip(shares, shares_all)):
        quick.append(send(8 + number, share, share_all.at[core], mate))
        share_all[core] = share[...]
    quick.append(send(8 + amount, own, fields.at[core, 1], mate))
    fields[core, 1] = own[...]
    to_right.wait_recv()
    quick.append(send(6, fields.at[core, 0], fields.at[core, 0], mate))
    to_left.wait_recv()
    quick.append(send(7, fields.at[core, 2], fields.at[core, 2], mate))
    for copy in quick:
        copy.wait_recv()
    for copy in quick + [to_right, to_left]:
        copy.wait_send()


def trade(rows, own, shares, number):
    count = lax.axis_size("space")
    amount = len(shares)
    shapes = [(2,) + rows.shape, (2, 3) + own.shape] + [(2,) + share.shape for share in shares]
    return pl.pallas_call(
        lambda *refs: trade_kernel(count, amount, *refs),
        in_specs=[pl.BlockSpec(memory_space=pltpu.VMEM)] * (2 + amount),
        out_specs=[pl.BlockSpec(memory_space=pltpu.VMEM)] * (2 + amount),
        out_shape=[jax.ShapeDtypeStruct(shape, rows.dtype) for shape in shapes],
        scratch_shapes=[
            pltpu.SemaphoreType.DMA((9 + amount,)),
            pltpu.SemaphoreType.DMA((9 + amount,)),
        ],
        compiler_params=pltpu.CompilerParams(
            collective_id=number, has_side_effects=True, vmem_limit_bytes=32 * 1024 * 1024
        ),
    )(rows, own, *shares)


def ride_copies(count, refs):
    return [
        pltpu.make_async_remote_copy(
            src_ref=refs["ride"].at[side],
            dst_ref=refs["ride_in"].at[1 - side],
            send_sem=refs["ride_send"].at[side],
            recv_sem=refs["ride_recv"].at[side],
            device_id=device,
            device_id_type=pl.DeviceIdType.MESH,
        )
        for side, device in enumerate(nearby(count)[:2])
    ]


def hail(devices):
    barrier = pltpu.get_barrier_semaphore()
    for device in devices:
        pl.semaphore_signal(
            barrier, inc=1, device_id=device, device_id_type=pl.DeviceIdType.MESH
        )


def torus_sizes(count):
    return (4, 4, 8) if count == 128 else (1, 1, count)


class TorusSum:
    def __init__(self, count, axes, refs, label):
        size_y, size_x, size_z = torus_sizes(count)
        me, self.core = lax.axis_index("space"), lax.axis_index("chan")
        self.sizes = {"y": size_y, "x": size_x, "z": size_z}
        self.place = {
            "y": me // (size_z * size_x),
            "x": me // size_z % size_x,
            "z": me % size_z,
        }
        self.axes = axes
        self.refs = {name: refs[label + name] for name in SUM_NAMES}

    def device(self, axis, step):
        at = dict(self.place)
        at[axis] = (at[axis] + step) % self.sizes[axis]
        return (at["y"] * self.sizes["x"] + at["x"]) * self.sizes["z"] + at["z"], self.core

    def peers(self):
        return [
            self.device(axis, step) for axis in self.axes for step in range(1, self.sizes[axis])
        ]

    def copies(self, phase):
        refs = self.refs
        axis = (self.axes + self.axes[::-1])[phase]
        made = []
        for step in range(1, self.sizes[axis]):
            other = (self.place[axis] + step) % self.sizes[axis]
            if phase < 3:
                source = refs[("data", "own_a", "own_b")[phase]].at[other]
                target = refs[("part_a", "part_b", "part_z")[phase]].at[step - 1]
            else:
                here = [self.place[name] for name in self.axes]
                if phase == 3:
                    source = refs["whole"].at[here[2]]
                elif phase == 4:
                    source = refs["total"].at[here[0], here[1]]
                else:
                    source = refs["total"].at[here[0]]
                target = source
            made.append(
                pltpu.make_async_remote_copy(
                    src_ref=source,
                    dst_ref=target,
                    send_sem=refs["send"].at[phase, step - 1],
                    recv_sem=refs["recv"].at[phase, step - 1],
                    device_id=self.device(axis, step),
                    device_id_type=pl.DeviceIdType.MESH,
                )
            )
        return made

    def summed(self, kept, parts, axis):
        value = self.refs[kept][self.place[axis]]
        for step in range(1, self.sizes[axis]):
            value = value + self.refs[parts][step - 1]
        return value

    def start(self, phase):
        refs = self.refs
        at_a, at_b, at_z = [self.place[axis] for axis in self.axes]
        if phase == 1:
            refs["own_a"][...] = self.summed("data", "part_a", self.axes[0])
        elif phase == 2:
            refs["own_b"][...] = self.summed("own_a", "part_b", self.axes[1])
        elif phase == 3:
            refs["whole"][at_z] = self.summed("own_b", "part_z", "z")
        elif phase == 4:
            refs["total"][at_a, at_b] = refs["whole"][...]
        for copy in self.copies(phase):
            copy.start()

    def wait(self, phase):
        for copy in self.copies(phase):
            copy.wait_recv()

    def leave(self):
        for phase in range(6):
            for copy in self.copies(phase):
                copy.wait_send()


SUM_NAMES = (
    "data", "part_a", "own_a", "part_b", "own_b", "part_z", "whole", "total", "send", "recv"
)


def sum_scratch(count, axes, rows, label, with_data):
    sizes = dict(zip("yxz", torus_sizes(count)))
    a, b, z = [sizes[axis] for axis in axes]
    piece = (128 // count, rows, 128)
    shapes = {
        "part_a": (max(1, a - 1), b, z),
        "own_a": (b, z),
        "part_b": (max(1, b - 1), z),
        "own_b": (z,),
        "part_z": (z - 1,),
        "whole": (z,),
        "total": (a, b, z),
    }
    if with_data:
        shapes["data"] = (a, b, z)
    scratch = {
        label + name: pltpu.VMEM(shape + piece, jnp.float32) for name, shape in shapes.items()
    }
    most = max(a, b, z) - 1
    scratch[label + "send"] = pltpu.SemaphoreType.DMA((6, most))
    scratch[label + "recv"] = pltpu.SemaphoreType.DMA((6, most))
    return scratch, (a, b, z) + piece


def fine_pieces(acc):
    pieces = []
    for tap_x in range(3):
        for block in range(acc.shape[1] // 4):
            for lane in range(WIDTH // 128):
                pieces.append((tap_x, slice(4 * block, 4 * block + 4), slice(128 * lane, 128 * lane + 128)))
    return pieces


def brick_kernel(count, masked, names, *refs):
    refs = dict(zip(names, refs))
    field_ref, table, padded, columns = [
        refs[name] for name in ("field", "table", "padded", "columns")
    ]
    brick = pl.program_id(0)
    last = pl.num_programs(0) - 1
    sums = "wide_data" in refs
    if sums:
        wide = TorusSum(count, ("x", "y", "z"), refs, "wide_")
        slim = TorusSum(count, ("y", "x", "z"), refs, "slim_")

    @pl.when(brick == 0)
    def fill():
        if count:
            greeted = list(nearby(count)[:2]) + (wide.peers() if sums else [])
            hail(greeted)
        slots = table.shape[0] - 1
        table[slots] = jnp.zeros((8, 8, 8, 128), jnp.float32)
        halves = len(field_ref.shape) == 5
        amount = field_ref.shape[2]

        def turn(slot, carry):
            if halves:
                place, one = slot // amount, slot % amount
                field = jnp.concatenate(
                    [field_ref[0, place, one], field_ref[1, place, one]], axis=0
                ).astype(jnp.float32)
            else:
                field = field_ref[slot].astype(jnp.float32)
            turned = jnp.concatenate([field, field], axis=0).T
            table[slot] = turned.reshape(8, 8, 8, 128)
            return carry

        lax.fori_loop(0, slots, turn, 0)
        if "acc" in refs:
            refs["acc"][...] = jnp.zeros_like(refs["acc"])
        if count:
            pl.semaphore_wait(pltpu.get_barrier_semaphore(), len(greeted))
            for copy in ride_copies(count, refs):
                copy.start()
        if sums:
            wide.start(0)

    if sums:

        @pl.when(brick == last - 2)
        def second():
            wide.wait(0)
            wide.start(1)

        @pl.when(brick == last)
        def third():
            wide.wait(1)
            wide.start(2)

    for index, (lean_x, lean_y, lean_z) in enumerate(lean_list()):
        slot = refs["near"][brick, index]
        to_x, from_x = SPANS[lean_x]
        to_y, from_y = SPANS[lean_y]
        padded[lean_z + 1, to_x, to_y] = table[slot, from_x, from_y]
    shape = (10, 8, 8, 128)
    place_z = lax.broadcasted_iota(jnp.int32, shape, 2)
    low_half = lax.broadcasted_iota(jnp.int32, shape, 3) < 64

    def put(position, low, high):
        both = jnp.where(low_half, low, high).reshape(640, 128)
        columns[:, 128 * position : 128 * position + 128] = both.astype(jnp.bfloat16)

    ahead = []
    for tap_y, position in enumerate((0, 2, 3)):
        below = padded[0, :, tap_y : tap_y + 8]
        level = padded[1, :, tap_y : tap_y + 8]
        above = padded[2, :, tap_y : tap_y + 8]
        minus = pltpu.roll(jnp.where(place_z == 7, below, level), 1, 2)
        put(position, level, minus)
        ahead.append(pltpu.roll(jnp.where(place_z == 0, above, level), 7, 2))
        if tap_y == 1:
            put(1, ahead[0], ahead[1])
    put(4, ahead[2], 0.0)
    if "weight" in refs:
        total = None
        for tap_x in range(3):
            part = lax.dot_general(
                refs["weight"][0, tap_x],
                columns[64 * tap_x : 64 * tap_x + 512, :],
                (((1,), (1,)), ((), ())),
                preferred_element_type=jnp.float32,
            )
            total = part if total is None else total + part
        if masked:
            total = jnp.where(brick < refs["live"][0], total, 0.0)
        refs["out"][0] = total.astype(refs["out"].dtype)
    if "grad" in refs:
        for tap_x in range(3):
            refs["acc"][tap_x] += jnp.dot(
                refs["grad"][0],
                columns[64 * tap_x : 64 * tap_x + 512, :],
                preferred_element_type=jnp.float32,
            )

    @pl.when(brick == last)
    def close():
        if sums:
            acc, data = refs["acc"], refs["slim_data"]
            cells = list(np.ndindex(data.shape[:4]))
            spans = fine_pieces(acc)
            for cell, span in zip(cells, spans):
                data[cell] = acc[span]
            for cell in cells[len(spans) :]:
                data[cell] = jnp.zeros(data.shape[4:], jnp.float32)
            slim.start(0)
            for phase in range(3):
                wide.wait(2 + phase)
                wide.start(3 + phase)
                slim.wait(phase)
                slim.start(phase + 1)
            wide.wait(5)
            refs["wide_out"][...] = refs["wide_total"][...]
            for phase in range(3, 5):
                slim.wait(phase)
                slim.start(phase + 1)
            slim.wait(5)
            refs["slim_out"][...] = refs["slim_total"][...]
            wide.leave()
            slim.leave()
        elif "acc" in refs:
            refs["total"][...] = refs["acc"][...]
        if count:
            for copy in ride_copies(count, refs):
                copy.wait()
            refs["ride_out"][...] = refs["ride_in"][...]


def brick_pass(
    field_in, near, live_count, weight, grad_rows, out_dtype, masked, ride=None, number=None,
    wide=None,
):
    amount = near.shape[0]
    count = 0 if ride is None else lax.axis_size("space")
    slots = 3 * field_in.shape[2] if field_in.ndim == 5 else field_in.shape[0]
    rows = weight.shape[2] if weight is not None else grad_rows.shape[1]
    ins, outs, scratch = {}, {}, {}

    def whole(shape):
        return pl.BlockSpec(shape, lambda b: (0,) * len(shape))

    def result(name, shape, dtype, spec=None):
        outs[name] = (jax.ShapeDtypeStruct(shape, dtype), spec or whole(shape))

    ins["near"] = (near, pl.BlockSpec(memory_space=pltpu.SMEM))
    ins["live"] = (live_count, pl.BlockSpec(memory_space=pltpu.SMEM))
    ins["field"] = (field_in, whole(field_in.shape))
    scratch["table"] = pltpu.VMEM((slots + 1, 8, 8, 8, 128), jnp.float32)
    scratch["padded"] = pltpu.VMEM((3, 10, 10, 8, 128), jnp.float32)
    scratch["columns"] = pltpu.VMEM((640, WIDTH), jnp.bfloat16)
    by_brick = pl.BlockSpec((1, rows, 512), lambda b: (b, 0, 0))
    if weight is not None:
        parts = weight.shape[0]
        blocks = jnp.stack([weight_blocks(part) for part in weight])
        ins["weight"] = (
            blocks, pl.BlockSpec((1, 3, rows, WIDTH), lambda b: (b % parts, 0, 0, 0))
        )
        result("out", (amount, rows, 512), out_dtype, by_brick)
    if grad_rows is not None:
        ins["grad"] = (grad_rows, by_brick)
        scratch["acc"] = pltpu.VMEM((3, rows, WIDTH), jnp.float32)
        if wide is None:
            result("total", (3, rows, WIDTH), jnp.float32)
    if wide is not None:
        wide_scratch, wide_shape = sum_scratch(count, "xyz", 8, "wide_", False)
        slim_scratch, slim_shape = sum_scratch(count, "yxz", 4, "slim_", True)
        scratch.update(wide_scratch)
        scratch.update(slim_scratch)
        ins["wide_data"] = (wide.reshape(wide_shape), whole(wide_shape))
        result("wide_out", wide_shape, jnp.float32)
        result("slim_out", slim_shape, jnp.float32)
    if count:
        ins["ride"] = (ride, whole(ride.shape))
        result("ride_out", ride.shape, ride.dtype)
        scratch["ride_in"] = pltpu.VMEM(ride.shape, ride.dtype)
        scratch["ride_send"] = pltpu.SemaphoreType.DMA((2,))
        scratch["ride_recv"] = pltpu.SemaphoreType.DMA((2,))
    names = list(ins) + list(outs) + list(scratch)
    remote = {"collective_id": number, "has_side_effects": True} if count else {}
    products = (weight is not None) + (grad_rows is not None)
    return pl.pallas_call(
        lambda *refs: brick_kernel(count, masked, names, *refs),
        grid=(amount,),
        in_specs=[spec for _, spec in ins.values()],
        out_specs=[spec for _, spec in outs.values()],
        out_shape=[shape for shape, _ in outs.values()],
        scratch_shapes=list(scratch.values()),
        compiler_params=pltpu.CompilerParams(vmem_limit_bytes=48 * 1024 * 1024, **remote),
        cost_estimate=pl.CostEstimate(
            flops=amount * products * 2 * rows * 3 * WIDTH * 512,
            bytes_accessed=slots * 64 * 512 * 2,
            transcendentals=0,
        ),
    )(*[value for value, _ in ins.values()])


def weight_blocks(weight):
    rows, channels = weight.shape[1:]
    taps = weight.reshape(3, 9, rows, channels)[:, TAP_ORDER]
    taps = jnp.concatenate([taps, jnp.zeros_like(taps[:, :1])], axis=1)
    return jnp.transpose(taps, (0, 2, 1, 3)).reshape(3, rows, WIDTH)


def finish_kernel(scales, slim, wide, fine_out, coarse_out):
    for pieces, out, scale in zip((slim, wide), (fine_out, coarse_out), scales):
        high = pieces.shape[1]
        blocks = out.shape[1] // high
        for tap_x in range(3):
            for block in range(blocks):
                first = WIDTH // 128 * (tap_x * blocks + block)
                rows = slice(high * block, high * block + high)
                for place, tap in enumerate(TAP_ORDER):
                    lanes = slice(64 * (place % 2), 64 * (place % 2) + 64)
                    out[9 * tap_x + int(tap), rows, :] = pieces[first + place // 2, :, lanes] * scale


def wide_pieces(coarse, project):
    tiles = jnp.transpose(coarse.reshape(-1, 8, WIDTH // 128, 128), (0, 2, 1, 3))
    tiles = tiles.reshape(-1, 8, 128)
    small = project.reshape(-1, 8, 128)
    spare = 128 - tiles.shape[0] - small.shape[0]
    return jnp.concatenate([tiles, small, jnp.zeros((spare, 8, 128), jnp.float32)], axis=0)


def finish(slim, wide, fine_rows, coarse_rows, scales):
    slim, wide = slim.reshape(128, 4, 128), wide.reshape(128, 8, 128)
    fine_sum, coarse_sum = pl.pallas_call(
        lambda *refs: finish_kernel(scales, *refs),
        in_specs=[pl.BlockSpec(memory_space=pltpu.VMEM)] * 2,
        out_specs=[pl.BlockSpec(memory_space=pltpu.VMEM)] * 2,
        out_shape=[
            jax.ShapeDtypeStruct((27, rows, 64), jnp.float32) for rows in (fine_rows, coarse_rows)
        ],
    )(slim, wide)
    used = 3 * coarse_rows // 8 * (WIDTH // 128)
    return fine_sum, coarse_sum, wide[used : used + 4].reshape(64, 64)


def per_device(
    feats, live_count, neighbours, parent, fine_weight, coarse_weight, project_weight, cotangent
):
    bricks = feats.shape[0]
    half_channels = feats.shape[1]
    devices = lax.axis_size("space")
    own_index = lax.axis_index("space")
    moving = max(1, bricks // 8)
    coarse_bricks = bricks // 8
    live_mask = (jnp.arange(bricks, dtype=jnp.int32) < live_count[0]).astype(jnp.float32)[
        :, None, None
    ]
    core = lax.axis_index("chan")
    send_place = route_places(parent, own_index, moving, bricks)
    send_pick = (jnp.arange(2 * moving, dtype=jnp.int32)[:, None] == send_place[None, :]).astype(
        jnp.bfloat16
    )
    pooled = (pool_sum(feats) * 0.125 * live_mask).astype(jnp.bfloat16).reshape(bricks, -1)
    slot_rows = jnp.broadcast_to(
        (parent % bricks + 1).astype(jnp.bfloat16)[:, None], (bricks, 2048)
    )
    outgoing = select_rows(send_pick, jnp.concatenate([pooled, slot_rows], axis=1))
    grad_rows = (cotangent.astype(jnp.float32) * live_mask).astype(jnp.bfloat16)
    incoming, grad_fields, both_pooled, both_coarse, both_fine, both_project = trade(
        outgoing.reshape(2, moving * 32, 128),
        grad_rows,
        [pooled.reshape(bricks * 16, 128), coarse_weight, fine_weight, project_weight],
        2,
    )
    whole_coarse = jnp.concatenate([both_coarse[0], both_coarse[1]], axis=1)
    whole_fine = jnp.concatenate([both_fine[0], both_fine[1]], axis=1)
    whole_project = jnp.concatenate([both_project[0], both_project[1]], axis=1)
    incoming = incoming.reshape(2, 2 * moving, 4096)
    incoming_slots = incoming[0, :, -1].astype(jnp.int32) - 1
    local_slots = jnp.where(parent // bricks == own_index, parent % bricks, -1)
    all_slots = jnp.concatenate([local_slots, incoming_slots])
    receive_pick = (jnp.arange(bricks, dtype=jnp.int32)[:, None] == all_slots[None, :]).astype(
        jnp.bfloat16
    )
    arrived = select_both(receive_pick, both_pooled, incoming[:, :, :2048])
    coarse_in = place_octants(arrived)
    lone = lone_bricks(coarse_bricks)
    preactivation = brick_pass(
        coarse_in, lone, live_count, whole_coarse[None], None, jnp.float32, False
    )[0]
    hidden = jax.nn.silu(preactivation).astype(jnp.bfloat16)
    own_project = lax.dynamic_slice_in_dim(
        whole_project, core * half_channels, half_channels, 0
    )
    coarse_out = jnp.einsum(
        "cj,bjv->bcv", own_project, hidden, preferred_element_type=jnp.float32
    ).astype(jnp.bfloat16)
    back_source = select_rows(receive_pick.T, split_octants(coarse_out).reshape(bricks, -1))
    last_brick = devices * bricks
    near_local = jnp.where(
        neighbours >= last_brick, 3 * bricks, neighbours - (own_index - 1) * bricks
    ).astype(jnp.int32)
    slots = jnp.arange(bricks, dtype=jnp.int32)[:, None] + bricks
    near = jnp.concatenate([near_local[:, :13], slots, near_local[:, 13:]], axis=1)
    own_weight = lax.dynamic_slice_in_dim(whole_fine, core * half_channels, half_channels, 2)
    back_feats, rode_back = brick_pass(
        grad_fields,
        near,
        live_count,
        flip_weight(own_weight)[None],
        None,
        jnp.bfloat16,
        True,
        back_source[bricks:].reshape(2, moving * 16, 128),
        3,
    )
    up_octants = gather_back(
        back_source[:bricks], send_pick, rode_back.reshape(2 * moving, -1)
    ).reshape(bricks, half_channels, 64)
    mixed_feats = ((feats.astype(jnp.float32) + enlarge(up_octants)) * live_mask).astype(
        jnp.bfloat16
    )
    up_grad = pool_sum(back_feats).astype(jnp.bfloat16).reshape(bricks, -1)
    outgoing_grad = select_rows(send_pick, up_grad)
    incoming_grad, feat_fields, both_grad = trade(
        outgoing_grad.reshape(2, moving * 16, 128),
        mixed_feats,
        [up_grad.reshape(bricks * 16, 128)],
        4,
    )
    coarse_grad = place_octants(
        select_both(receive_pick, both_grad, incoming_grad.reshape(2, 2 * moving, 2048))
    )
    hidden_half = hidden.shape[1] // 2
    own_hidden = lax.dynamic_slice_in_dim(hidden, core * hidden_half, hidden_half, 1)
    project_matrix = jnp.einsum(
        "bcv,bjv->cj", coarse_grad, own_hidden, preferred_element_type=jnp.float32
    )
    hidden_grad = jnp.einsum(
        "cj,bcv->bjv", whole_project, coarse_grad, preferred_element_type=jnp.float32
    )
    sigmoid_pre = jax.nn.sigmoid(preactivation)
    pre_grad = (hidden_grad * sigmoid_pre * (1.0 + preactivation * (1.0 - sigmoid_pre))).astype(
        jnp.bfloat16
    )
    own_pre_grad = lax.dynamic_slice_in_dim(pre_grad, core * hidden_half, hidden_half, 1)
    coarse_total = brick_pass(
        coarse_in, lone, live_count, None, own_pre_grad, None, False
    )[0]
    own_coarse = flip_weight(
        lax.dynamic_slice_in_dim(whole_coarse, core * half_channels, half_channels, 2)
    )
    coarse_terms = brick_pass(
        pre_grad.reshape(2 * coarse_bricks, hidden_half, 512),
        lone_bricks(2 * coarse_bricks),
        live_count,
        jnp.stack([own_coarse[:, :, :hidden_half], own_coarse[:, :, hidden_half:]]),
        None,
        jnp.float32,
        False,
    )[0]
    coarse_back = (
        coarse_terms.reshape(coarse_bricks, 2, half_channels, 512).sum(1).astype(jnp.bfloat16)
    )
    down_source = select_rows(receive_pick.T, split_octants(coarse_back).reshape(bricks, -1))
    out_feats, wide_sum, slim_sum, rode_down = brick_pass(
        feat_fields,
        near,
        live_count,
        fine_weight[None],
        grad_rows,
        jnp.bfloat16,
        True,
        down_source[bricks:].reshape(2, moving * 16, 128),
        5,
        wide_pieces(coarse_total, project_matrix),
    )
    down_grad = gather_back(
        down_source[:bricks], send_pick, rode_down.reshape(2 * moving, -1)
    ).reshape(bricks, half_channels, 64)
    grad_feats = (back_feats.astype(jnp.float32) + live_mask * enlarge(down_grad) * 0.125).astype(
        jnp.bfloat16
    )
    fine_scale = 1.0 / math.sqrt(512.0 * bricks * devices)
    coarse_scale = 1.0 / math.sqrt(512.0 * coarse_bricks * devices)
    fine_weight_grad, coarse_weight_grad, project_total = finish(
        slim_sum, wide_sum, half_channels, hidden_half, (fine_scale, coarse_scale)
    )
    project_weight_grad = project_total * coarse_scale
    return (out_feats, grad_feats, fine_weight_grad, coarse_weight_grad, project_weight_grad)


def solution(mesh):
    placed = (
        P("space", "chan", None),
        P("space"),
        P("space", None),
        P("space"),
        P(None, "chan", None),
        P(None, "chan", None),
        P(None, "chan"),
        P("space", "chan", None),
    )
    return jax.shard_map(
        per_device,
        mesh=mesh,
        in_specs=placed,
        out_specs=(
            P("space", "chan", None),
            P("space", "chan", None),
            P(None, "chan", None),
            P(None, "chan", None),
            P(None, "chan"),
        ),
        check_vma=False,
    )
```

```python
import math

import jax
import jax.numpy as jnp
import numpy as np
from jax import lax
from jax.experimental import pallas as pl
from jax.experimental.pallas import tpu as pltpu
from jax.sharding import PartitionSpec as P


def lean_list():
    leans = []
    for lean_x in (-1, 0, 1):
        for lean_y in (-1, 0, 1):
            for lean_z in (-1, 0, 1):
                leans.append((lean_x, lean_y, lean_z))
    return leans


def pool_table():
    voxel = np.arange(512)
    octant_voxel = 16 * (voxel // 128) + 4 * (voxel // 16 % 4) + voxel % 8 // 2
    return (octant_voxel[:, None] == np.arange(64)[None, :]).astype(np.float32)


def octant_table():
    voxel = np.arange(512)
    coord_x = voxel // 64
    coord_y = voxel // 8 % 8
    coord_z = voxel % 8
    octant = 4 * (coord_x // 4) + 2 * (coord_y // 4) + coord_z // 4
    inner = 16 * (coord_x % 4) + 4 * (coord_y % 4) + coord_z % 4
    table = np.zeros((8, 64, 512), np.float32)
    table[octant, inner, voxel] = 1.0
    return table


def flip_weight(weight):
    return jnp.transpose(weight[::-1], (0, 2, 1))


def pool_sum(field_in):
    table = jnp.asarray(pool_table()).astype(jnp.bfloat16)
    return jnp.einsum("bcv,vu->bcu", field_in, table, preferred_element_type=jnp.float32)


def enlarge(octants):
    table = jnp.asarray(pool_table()).astype(jnp.bfloat16)
    return jnp.einsum("bcu,vu->bcv", octants, table, preferred_element_type=jnp.float32)


def place_octants(octants):
    amount, channels = (octants.shape[0] // 8, octants.shape[1])
    grouped = octants.reshape(amount, 8, channels, 64)
    table = jnp.asarray(octant_table()).astype(jnp.bfloat16)
    return jnp.einsum("jocu,ouv->jcv", grouped, table, preferred_element_type=jnp.float32).astype(
        jnp.bfloat16
    )


def split_octants(coarse):
    amount, channels = (coarse.shape[0], coarse.shape[1])
    table = jnp.asarray(octant_table()).astype(jnp.bfloat16)
    parts = jnp.einsum("jcv,ouv->jocu", coarse, table, preferred_element_type=jnp.float32).astype(
        jnp.bfloat16
    )
    return parts.reshape(amount * 8, channels, 64)


def select_rows(picker, values):
    return jnp.dot(picker, values, preferred_element_type=jnp.float32).astype(jnp.bfloat16)


def route_places(slot_list, dev_index, moving, bricks):
    direction = slot_list // bricks - dev_index
    to_left = (direction == -1).astype(jnp.int32)
    to_right = (direction == 1).astype(jnp.int32)
    left_rank = jnp.cumsum(to_left) - to_left
    right_rank = jnp.cumsum(to_right) - to_right
    return jnp.where(
        to_left == 1, left_rank, jnp.where(to_right == 1, moving + right_rank, 2 * moving)
    ).astype(jnp.int32)


def lone_bricks(amount):
    centre = jnp.arange(27, dtype=jnp.int32)[None, :] == 13
    return jnp.where(centre, jnp.arange(amount, dtype=jnp.int32)[:, None], amount)


def select_both(picker, body, moved):
    values = jnp.concatenate([body.reshape(2, -1, 2048), moved], axis=1)
    picked = jnp.einsum("rs,csv->rcv", picker, values, preferred_element_type=jnp.float32)
    return picked.astype(jnp.bfloat16).reshape(picker.shape[0], -1, 64)


def gather_back(local_part, send_pick, returned):
    total = local_part.astype(jnp.float32) + jnp.dot(
        send_pick.T, returned, preferred_element_type=jnp.float32
    )
    return total.astype(jnp.bfloat16)


SPANS = {-1: (slice(0, 1), slice(7, 8)), 0: (slice(1, 9), slice(0, 8)), 1: (slice(9, 10), slice(0, 1))}
TAP_ORDER = np.array([1, 0, 2, 5, 4, 3, 7, 6, 8])
WIDTH = 640


def greet(devices):
    barrier = pltpu.get_barrier_semaphore()
    for device in devices:
        pl.semaphore_signal(
            barrier, inc=1, device_id=device, device_id_type=pl.DeviceIdType.MESH
        )
    pl.semaphore_wait(barrier, len(devices))


def nearby(count):
    me, core = lax.axis_index("space"), lax.axis_index("chan")
    return ((me + count - 1) % count, core), ((me + 1) % count, core), (me, 1 - core)


def sender(send_sems, recv_sems):
    def send(number, source, target, device):
        copy = pltpu.make_async_remote_copy(
            src_ref=source,
            dst_ref=target,
            send_sem=send_sems.at[number],
            recv_sem=recv_sems.at[number],
            device_id=device,
            device_id_type=pl.DeviceIdType.MESH,
        )
        copy.start()
        return copy

    return send


def trade_kernel(count, amount, *refs):
    rows, own = refs[:2]
    shares = refs[2 : 2 + amount]
    rows_all, fields = refs[2 + amount : 4 + amount]
    shares_all = refs[4 + amount : 4 + 2 * amount]
    send_sems, recv_sems, keep_sem = refs[4 + 2 * amount :]
    core = lax.axis_index("chan")
    left, right, mate = nearby(count)
    left_mate, right_mate = (left[0], 1 - core), (right[0], 1 - core)
    greet((left, right, mate, left_mate, right_mate))
    send = sender(send_sems, recv_sems)
    quick = [
        send(0, rows.at[0], rows_all.at[core, 1], left),
        send(1, rows.at[1], rows_all.at[core, 0], right),
        send(2, rows.at[0], rows_all.at[core, 1], left_mate),
        send(3, rows.at[1], rows_all.at[core, 0], right_mate),
    ]
    to_right = send(4, own, fields.at[core, 0], right)
    to_left = send(5, own, fields.at[core, 2], left)
    for number, (share, share_all) in enumerate(zip(shares, shares_all)):
        quick.append(send(8 + number, share, share_all.at[core], mate))
        share_all[core] = share[...]
    quick.append(send(8 + amount, own, fields.at[core, 1], mate))
    keep = pltpu.make_async_copy(own, fields.at[core, 1], keep_sem)
    keep.start()
    to_right.wait_recv()
    quick.append(send(6, fields.at[core, 0], fields.at[core, 0], mate))
    to_left.wait_recv()
    quick.append(send(7, fields.at[core, 2], fields.at[core, 2], mate))
    for copy in quick:
        copy.wait_recv()
    for copy in quick + [to_right, to_left]:
        copy.wait_send()
    keep.wait()


def trade(rows, own, shares, number):
    count = lax.axis_size("space")
    amount = len(shares)
    shapes = [(2,) + rows.shape, (2, 3) + own.shape] + [(2,) + share.shape for share in shares]
    return pl.pallas_call(
        lambda *refs: trade_kernel(count, amount, *refs),
        in_specs=[pl.BlockSpec(memory_space=pltpu.VMEM)] * (2 + amount),
        out_specs=[
            pl.BlockSpec(memory_space=pl.ANY if place == 1 else pltpu.VMEM)
            for place in range(2 + amount)
        ],
        out_shape=[jax.ShapeDtypeStruct(shape, rows.dtype) for shape in shapes],
        scratch_shapes=[
            pltpu.SemaphoreType.DMA((9 + amount,)),
            pltpu.SemaphoreType.DMA((9 + amount,)),
            pltpu.SemaphoreType.DMA,
        ],
        compiler_params=pltpu.CompilerParams(
            collective_id=number, has_side_effects=True, vmem_limit_bytes=12 * 1024 * 1024
        ),
    )(rows, own, *shares)


def ride_copies(count, refs):
    return [
        pltpu.make_async_remote_copy(
            src_ref=refs["ride"].at[side],
            dst_ref=refs["ride_in"].at[1 - side],
            send_sem=refs["ride_send"].at[side],
            recv_sem=refs["ride_recv"].at[side],
            device_id=device,
            device_id_type=pl.DeviceIdType.MESH,
        )
        for side, device in enumerate(nearby(count)[:2])
    ]


def hail(devices):
    barrier = pltpu.get_barrier_semaphore()
    for device in devices:
        pl.semaphore_signal(
            barrier, inc=1, device_id=device, device_id_type=pl.DeviceIdType.MESH
        )


def torus_sizes(count):
    return (16, 8) if count == 128 else (1, count)


class TorusSum:
    def __init__(self, count, refs, label):
        self.plane, self.depth = torus_sizes(count)
        me, self.core = lax.axis_index("space"), lax.axis_index("chan")
        self.at, self.level = me // self.depth, me % self.depth
        self.refs = {name: refs[label + name] for name in SUM_NAMES}

    def across(self, step):
        return (self.at + step) % self.plane * self.depth + self.level, self.core

    def along(self, step):
        return self.at * self.depth + (self.level + step) % self.depth, self.core

    def peers(self):
        return [self.across(step) for step in range(1, self.plane)] + [
            self.along(step) for step in range(1, self.depth)
        ]

    def copies(self, phase):
        refs = self.refs
        made = []
        for step in range(1, self.depth if phase == 1 else self.plane):
            if phase == 0:
                source = refs["data"].at[(self.at + step) % self.plane]
                target = refs["part"].at[step - 1]
            elif phase == 1:
                source = target = refs["levels"].at[self.level]
            else:
                source = target = refs["total"].at[self.at]
            made.append(
                pltpu.make_async_remote_copy(
                    src_ref=source,
                    dst_ref=target,
                    send_sem=refs["send"].at[phase, step - 1],
                    recv_sem=refs["recv"].at[phase, step - 1],
                    device_id=self.along(step) if phase == 1 else self.across(step),
                    device_id_type=pl.DeviceIdType.MESH,
                )
            )
        return made

    def start(self, phase):
        refs = self.refs
        if phase == 1:
            value = refs["data"][self.at]
            for step in range(1, self.plane):
                value = value + refs["part"][step - 1]
            refs["levels"][self.level] = value
        elif phase == 2:
            value = refs["levels"][0]
            for level in range(1, self.depth):
                value = value + refs["levels"][level]
            refs["total"][self.at] = value
        for copy in self.copies(phase):
            copy.start()

    def wait(self, phase):
        for copy in self.copies(phase):
            copy.wait_recv()

    def leave(self):
        for phase in range(3):
            for copy in self.copies(phase):
                copy.wait_send()


SUM_NAMES = ("data", "part", "levels", "total", "send", "recv")


def sum_scratch(count, rows, label, with_data):
    plane, depth = torus_sizes(count)
    piece = (128 // plane, rows, 128)
    firsts = {"part": max(1, plane - 1), "levels": depth, "total": plane}
    if with_data:
        firsts["data"] = plane
    scratch = {
        label + name: pltpu.VMEM((first,) + piece, jnp.float32) for name, first in firsts.items()
    }
    most = max(plane, depth) - 1
    scratch[label + "send"] = pltpu.SemaphoreType.DMA((3, most))
    scratch[label + "recv"] = pltpu.SemaphoreType.DMA((3, most))
    return scratch, (plane,) + piece


def fine_pieces(acc):
    pieces = []
    for tap_x in range(3):
        for block in range(acc.shape[1] // 4):
            for lane in range(WIDTH // 128):
                pieces.append((tap_x, slice(4 * block, 4 * block + 4), slice(128 * lane, 128 * lane + 128)))
    return pieces


def brick_kernel(count, masked, names, *refs):
    refs = dict(zip(names, refs))
    field_ref, table, padded, columns = [
        refs[name] for name in ("field", "table", "padded", "columns")
    ]
    brick = pl.program_id(0)
    last = pl.num_programs(0) - 1
    sums = "wide_data" in refs
    if sums:
        wide = TorusSum(count, refs, "wide_")
        slim = TorusSum(count, refs, "slim_")

    @pl.when(brick == 0)
    def fill():
        if count:
            greeted = list(nearby(count)[:2]) + (wide.peers() if sums else [])
            hail(greeted)
        slots = table.shape[0] - 1
        table[slots] = jnp.zeros((8, 8, 8, 128), jnp.float32)
        halves = len(field_ref.shape) == 5
        amount = field_ref.shape[2]

        def turn(slot, carry):
            if halves:
                place, one = slot // amount, slot % amount
                field = jnp.concatenate(
                    [field_ref[0, place, one], field_ref[1, place, one]], axis=0
                ).astype(jnp.float32)
            else:
                field = field_ref[slot].astype(jnp.float32)
            turned = jnp.concatenate([field, field], axis=0).T
            table[slot] = turned.reshape(8, 8, 8, 128)
            return carry

        lax.fori_loop(0, slots, turn, 0)
        if "acc" in refs:
            refs["acc"][...] = jnp.zeros_like(refs["acc"])
        if count:
            pl.semaphore_wait(pltpu.get_barrier_semaphore(), len(greeted))
            for copy in ride_copies(count, refs):
                copy.start()
        if sums:
            wide.start(0)

    if sums:

        @pl.when(brick == last - 2)
        def second():
            wide.wait(0)
            wide.start(1)

        @pl.when(brick == last)
        def third():
            wide.wait(1)
            wide.start(2)

    for index, (lean_x, lean_y, lean_z) in enumerate(lean_list()):
        slot = refs["near"][brick, index]
        to_x, from_x = SPANS[lean_x]
        to_y, from_y = SPANS[lean_y]
        padded[lean_z + 1, to_x, to_y] = table[slot, from_x, from_y]
    shape = (10, 8, 8, 128)
    place_z = lax.broadcasted_iota(jnp.int32, shape, 2)
    low_half = lax.broadcasted_iota(jnp.int32, shape, 3) < 64

    def put(position, low, high):
        both = jnp.where(low_half, low, high).reshape(640, 128)
        columns[:, 128 * position : 128 * position + 128] = both.astype(jnp.bfloat16)

    ahead = []
    for tap_y, position in enumerate((0, 2, 3)):
        below = padded[0, :, tap_y : tap_y + 8]
        level = padded[1, :, tap_y : tap_y + 8]
        above = padded[2, :, tap_y : tap_y + 8]
        minus = pltpu.roll(jnp.where(place_z == 7, below, level), 1, 2)
        put(position, level, minus)
        ahead.append(pltpu.roll(jnp.where(place_z == 0, above, level), 7, 2))
        if tap_y == 1:
            put(1, ahead[0], ahead[1])
    put(4, ahead[2], 0.0)
    if "weight" in refs:
        total = None
        for tap_x in range(3):
            part = lax.dot_general(
                refs["weight"][0, tap_x],
                columns[64 * tap_x : 64 * tap_x + 512, :],
                (((1,), (1,)), ((), ())),
                preferred_element_type=jnp.float32,
            )
            total = part if total is None else total + part
        if masked:
            total = jnp.where(brick < refs["live"][0], total, 0.0)
        refs["out"][0] = total.astype(refs["out"].dtype)
    if "grad" in refs:
        for tap_x in range(3):
            refs["acc"][tap_x] += jnp.dot(
                refs["grad"][0],
                columns[64 * tap_x : 64 * tap_x + 512, :],
                preferred_element_type=jnp.float32,
            )

    @pl.when(brick == last)
    def close():
        if sums:
            acc, data = refs["acc"], refs["slim_data"]
            cells = list(np.ndindex(data.shape[:2]))
            spans = fine_pieces(acc)
            for cell, span in zip(cells, spans):
                data[cell] = acc[span]
            for cell in cells[len(spans) :]:
                data[cell] = jnp.zeros(data.shape[2:], jnp.float32)
            slim.start(0)
            wide.wait(2)
            refs["wide_out"][...] = refs["wide_total"][...]
            slim.wait(0)
            slim.start(1)
            slim.wait(1)
            slim.start(2)
            slim.wait(2)
            refs["slim_out"][...] = refs["slim_total"][...]
            wide.leave()
            slim.leave()
        elif "acc" in refs:
            refs["total"][...] = refs["acc"][...]
        if count:
            for copy in ride_copies(count, refs):
                copy.wait()
            refs["ride_out"][...] = refs["ride_in"][...]


def brick_pass(
    field_in, near, live_count, weight, grad_rows, out_dtype, masked, ride=None, number=None,
    wide=None,
):
    amount = near.shape[0]
    count = 0 if ride is None else lax.axis_size("space")
    slots = 3 * field_in.shape[2] if field_in.ndim == 5 else field_in.shape[0]
    rows = weight.shape[2] if weight is not None else grad_rows.shape[1]
    ins, outs, scratch = {}, {}, {}

    def whole(shape):
        return pl.BlockSpec(shape, lambda b: (0,) * len(shape))

    def result(name, shape, dtype, spec=None):
        outs[name] = (jax.ShapeDtypeStruct(shape, dtype), spec or whole(shape))

    ins["near"] = (near, pl.BlockSpec(memory_space=pltpu.SMEM))
    ins["live"] = (live_count, pl.BlockSpec(memory_space=pltpu.SMEM))
    ins["field"] = (field_in, whole(field_in.shape))
    scratch["table"] = pltpu.VMEM((slots + 1, 8, 8, 8, 128), jnp.float32)
    scratch["padded"] = pltpu.VMEM((3, 10, 10, 8, 128), jnp.float32)
    scratch["columns"] = pltpu.VMEM((640, WIDTH), jnp.bfloat16)
    by_brick = pl.BlockSpec((1, rows, 512), lambda b: (b, 0, 0))
    if weight is not None:
        parts = weight.shape[0]
        blocks = jnp.stack([weight_blocks(part) for part in weight])
        ins["weight"] = (
            blocks, pl.BlockSpec((1, 3, rows, WIDTH), lambda b: (b % parts, 0, 0, 0))
        )
        result("out", (amount, rows, 512), out_dtype, by_brick)
    if grad_rows is not None:
        ins["grad"] = (grad_rows, by_brick)
        scratch["acc"] = pltpu.VMEM((3, rows, WIDTH), jnp.float32)
        if wide is None:
            result("total", (3, rows, WIDTH), jnp.float32)
    if wide is not None:
        wide_scratch, wide_shape = sum_scratch(count, 8, "wide_", False)
        slim_scratch, slim_shape = sum_scratch(count, 4, "slim_", True)
        scratch.update(wide_scratch)
        scratch.update(slim_scratch)
        ins["wide_data"] = (wide.reshape(wide_shape), whole(wide_shape))
        result("wide_out", wide_shape, jnp.float32)
        result("slim_out", slim_shape, jnp.float32)
    if count:
        ins["ride"] = (ride, whole(ride.shape))
        result("ride_out", ride.shape, ride.dtype)
        scratch["ride_in"] = pltpu.VMEM(ride.shape, ride.dtype)
        scratch["ride_send"] = pltpu.SemaphoreType.DMA((2,))
        scratch["ride_recv"] = pltpu.SemaphoreType.DMA((2,))
    names = list(ins) + list(outs) + list(scratch)
    remote = {"collective_id": number, "has_side_effects": True} if count else {}
    room = 12 if slots < 8 else 20 if wide is None else 30
    products = (weight is not None) + (grad_rows is not None)
    return pl.pallas_call(
        lambda *refs: brick_kernel(count, masked, names, *refs),
        grid=(amount,),
        in_specs=[spec for _, spec in ins.values()],
        out_specs=[spec for _, spec in outs.values()],
        out_shape=[shape for shape, _ in outs.values()],
        scratch_shapes=list(scratch.values()),
        compiler_params=pltpu.CompilerParams(vmem_limit_bytes=room * 1024 * 1024, **remote),
        cost_estimate=pl.CostEstimate(
            flops=amount * products * 2 * rows * 3 * WIDTH * 512,
            bytes_accessed=slots * 64 * 512 * 2,
            transcendentals=0,
        ),
    )(*[value for value, _ in ins.values()])


def weight_blocks(weight):
    rows, channels = weight.shape[1:]
    taps = weight.reshape(3, 9, rows, channels)
    taps = jnp.stack(
        [taps[:, tap] for tap in TAP_ORDER] + [jnp.zeros_like(taps[:, 0])], axis=1
    )
    return jnp.transpose(taps, (0, 2, 1, 3)).reshape(3, rows, WIDTH)


def finish_kernel(scales, slim, wide, fine_out, coarse_out):
    for pieces, out, scale in zip((slim, wide), (fine_out, coarse_out), scales):
        high = pieces.shape[1]
        blocks = out.shape[1] // high
        for tap_x in range(3):
            for block in range(blocks):
                first = WIDTH // 128 * (tap_x * blocks + block)
                rows = slice(high * block, high * block + high)
                for place, tap in enumerate(TAP_ORDER):
                    lanes = slice(64 * (place % 2), 64 * (place % 2) + 64)
                    out[9 * tap_x + int(tap), rows, :] = pieces[first + place // 2, :, lanes] * scale


def wide_pieces(coarse, project):
    tiles = jnp.transpose(coarse.reshape(-1, 8, WIDTH // 128, 128), (0, 2, 1, 3))
    tiles = tiles.reshape(-1, 8, 128)
    small = project.reshape(-1, 8, 128)
    spare = 128 - tiles.shape[0] - small.shape[0]
    return jnp.concatenate([tiles, small, jnp.zeros((spare, 8, 128), jnp.float32)], axis=0)


def finish(slim, wide, fine_rows, coarse_rows, scales):
    slim, wide = slim.reshape(128, 4, 128), wide.reshape(128, 8, 128)
    fine_sum, coarse_sum = pl.pallas_call(
        lambda *refs: finish_kernel(scales, *refs),
        in_specs=[pl.BlockSpec(memory_space=pltpu.VMEM)] * 2,
        out_specs=[pl.BlockSpec(memory_space=pltpu.VMEM)] * 2,
        out_shape=[
            jax.ShapeDtypeStruct((27, rows, 64), jnp.float32) for rows in (fine_rows, coarse_rows)
        ],
    )(slim, wide)
    used = 3 * coarse_rows // 8 * (WIDTH // 128)
    return fine_sum, coarse_sum, wide[used : used + 4].reshape(64, 64)


def per_device(
    feats, live_count, neighbours, parent, fine_weight, coarse_weight, project_weight, cotangent
):
    bricks = feats.shape[0]
    half_channels = feats.shape[1]
    devices = lax.axis_size("space")
    own_index = lax.axis_index("space")
    moving = max(1, bricks // 8)
    coarse_bricks = bricks // 8
    live_mask = (jnp.arange(bricks, dtype=jnp.int32) < live_count[0]).astype(jnp.float32)[
        :, None, None
    ]
    core = lax.axis_index("chan")
    send_place = route_places(parent, own_index, moving, bricks)
    send_pick = (jnp.arange(2 * moving, dtype=jnp.int32)[:, None] == send_place[None, :]).astype(
        jnp.bfloat16
    )
    pooled = (pool_sum(feats) * 0.125 * live_mask).astype(jnp.bfloat16).reshape(bricks, -1)
    slot_rows = jnp.broadcast_to(
        (parent % bricks + 1).astype(jnp.bfloat16)[:, None], (bricks, 2048)
    )
    outgoing = select_rows(send_pick, jnp.concatenate([pooled, slot_rows], axis=1))
    grad_rows = (cotangent.astype(jnp.float32) * live_mask).astype(jnp.bfloat16)
    incoming, grad_fields, both_pooled, both_coarse, both_fine, both_project = trade(
        outgoing.reshape(2, moving * 32, 128),
        grad_rows,
        [pooled.reshape(bricks * 16, 128), coarse_weight, fine_weight, project_weight],
        2,
    )
    whole_coarse = jnp.concatenate([both_coarse[0], both_coarse[1]], axis=1)
    whole_fine = jnp.concatenate([both_fine[0], both_fine[1]], axis=1)
    whole_project = jnp.concatenate([both_project[0], both_project[1]], axis=1)
    incoming = incoming.reshape(2, 2 * moving, 4096)
    incoming_slots = incoming[0, :, -1].astype(jnp.int32) - 1
    local_slots = jnp.where(parent // bricks == own_index, parent % bricks, -1)
    all_slots = jnp.concatenate([local_slots, incoming_slots])
    receive_pick = (jnp.arange(bricks, dtype=jnp.int32)[:, None] == all_slots[None, :]).astype(
        jnp.bfloat16
    )
    arrived = select_both(receive_pick, both_pooled, incoming[:, :, :2048])
    coarse_in = place_octants(arrived)
    lone = lone_bricks(coarse_bricks)
    preactivation = brick_pass(
        coarse_in, lone, live_count, whole_coarse[None], None, jnp.float32, False
    )[0]
    hidden = jax.nn.silu(preactivation).astype(jnp.bfloat16)
    own_project = lax.dynamic_slice_in_dim(
        whole_project, core * half_channels, half_channels, 0
    )
    coarse_out = jnp.einsum(
        "cj,bjv->bcv", own_project, hidden, preferred_element_type=jnp.float32
    ).astype(jnp.bfloat16)
    back_source = select_rows(receive_pick.T, split_octants(coarse_out).reshape(bricks, -1))
    last_brick = devices * bricks
    near_local = jnp.where(
        neighbours >= last_brick, 3 * bricks, neighbours - (own_index - 1) * bricks
    ).astype(jnp.int32)
    slots = jnp.arange(bricks, dtype=jnp.int32)[:, None] + bricks
    near = jnp.concatenate([near_local[:, :13], slots, near_local[:, 13:]], axis=1)
    own_weight = lax.dynamic_slice_in_dim(whole_fine, core * half_channels, half_channels, 2)
    back_feats, rode_back = brick_pass(
        grad_fields,
        near,
        live_count,
        flip_weight(own_weight)[None],
        None,
        jnp.bfloat16,
        True,
        back_source[bricks:].reshape(2, moving * 16, 128),
        3,
    )
    up_octants = gather_back(
        back_source[:bricks], send_pick, rode_back.reshape(2 * moving, -1)
    ).reshape(bricks, half_channels, 64)
    mixed_feats = ((feats.astype(jnp.float32) + enlarge(up_octants)) * live_mask).astype(
        jnp.bfloat16
    )
    up_grad = pool_sum(back_feats).astype(jnp.bfloat16).reshape(bricks, -1)
    outgoing_grad = select_rows(send_pick, up_grad)
    incoming_grad, feat_fields, both_grad = trade(
        outgoing_grad.reshape(2, moving * 16, 128),
        mixed_feats,
        [up_grad.reshape(bricks * 16, 128)],
        4,
    )
    coarse_grad = place_octants(
        select_both(receive_pick, both_grad, incoming_grad.reshape(2, 2 * moving, 2048))
    )
    hidden_half = hidden.shape[1] // 2
    own_hidden = lax.dynamic_slice_in_dim(hidden, core * hidden_half, hidden_half, 1)
    project_matrix = jnp.einsum(
        "bcv,bjv->cj", coarse_grad, own_hidden, preferred_element_type=jnp.float32
    )
    hidden_grad = jnp.einsum(
        "cj,bcv->bjv", whole_project, coarse_grad, preferred_element_type=jnp.float32
    )
    sigmoid_pre = jax.nn.sigmoid(preactivation)
    pre_grad = (hidden_grad * sigmoid_pre * (1.0 + preactivation * (1.0 - sigmoid_pre))).astype(
        jnp.bfloat16
    )
    own_pre_grad = lax.dynamic_slice_in_dim(pre_grad, core * hidden_half, hidden_half, 1)
    coarse_total = brick_pass(
        coarse_in, lone, live_count, None, own_pre_grad, None, False
    )[0]
    own_coarse = flip_weight(
        lax.dynamic_slice_in_dim(whole_coarse, core * half_channels, half_channels, 2)
    )
    coarse_terms = brick_pass(
        pre_grad.reshape(2 * coarse_bricks, hidden_half, 512),
        lone_bricks(2 * coarse_bricks),
        live_count,
        jnp.stack([own_coarse[:, :, :hidden_half], own_coarse[:, :, hidden_half:]]),
        None,
        jnp.float32,
        False,
    )[0]
    coarse_back = (
        coarse_terms.reshape(coarse_bricks, 2, half_channels, 512).sum(1).astype(jnp.bfloat16)
    )
    down_source = select_rows(receive_pick.T, split_octants(coarse_back).reshape(bricks, -1))
    out_feats, wide_sum, slim_sum, rode_down = brick_pass(
        feat_fields,
        near,
        live_count,
        fine_weight[None],
        grad_rows,
        jnp.bfloat16,
        True,
        down_source[bricks:].reshape(2, moving * 16, 128),
        5,
        wide_pieces(coarse_total, project_matrix),
    )
    down_grad = gather_back(
        down_source[:bricks], send_pick, rode_down.reshape(2 * moving, -1)
    ).reshape(bricks, half_channels, 64)
    grad_feats = (back_feats.astype(jnp.float32) + live_mask * enlarge(down_grad) * 0.125).astype(
        jnp.bfloat16
    )
    fine_scale = 1.0 / math.sqrt(512.0 * bricks * devices)
    coarse_scale = 1.0 / math.sqrt(512.0 * coarse_bricks * devices)
    fine_weight_grad, coarse_weight_grad, project_total = finish(
        slim_sum, wide_sum, half_channels, hidden_half, (fine_scale, coarse_scale)
    )
    project_weight_grad = project_total * coarse_scale
    return (out_feats, grad_feats, fine_weight_grad, coarse_weight_grad, project_weight_grad)


def solution(mesh):
    placed = (
        P("space", "chan", None),
        P("space"),
        P("space", None),
        P("space"),
        P(None, "chan", None),
        P(None, "chan", None),
        P(None, "chan"),
        P("space", "chan", None),
    )
    return jax.shard_map(
        per_device,
        mesh=mesh,
        in_specs=placed,
        out_specs=(
            P("space", "chan", None),
            P("space", "chan", None),
            P(None, "chan", None),
            P(None, "chan", None),
            P(None, "chan"),
        ),
        check_vma=False,
    )
```

```python
import math

import jax
import jax.numpy as jnp
import numpy as np
from jax import lax
from jax.experimental import pallas as pl
from jax.experimental.pallas import tpu as pltpu
from jax.sharding import PartitionSpec as P


def lean_list():
    leans = []
    for lean_x in (-1, 0, 1):
        for lean_y in (-1, 0, 1):
            for lean_z in (-1, 0, 1):
                leans.append((lean_x, lean_y, lean_z))
    return leans


def pool_table():
    voxel = np.arange(512)
    octant_voxel = 16 * (voxel // 128) + 4 * (voxel // 16 % 4) + voxel % 8 // 2
    return (octant_voxel[:, None] == np.arange(64)[None, :]).astype(np.float32)


def octant_table():
    voxel = np.arange(512)
    coord_x = voxel // 64
    coord_y = voxel // 8 % 8
    coord_z = voxel % 8
    octant = 4 * (coord_x // 4) + 2 * (coord_y // 4) + coord_z // 4
    inner = 16 * (coord_x % 4) + 4 * (coord_y % 4) + coord_z % 4
    table = np.zeros((8, 64, 512), np.float32)
    table[octant, inner, voxel] = 1.0
    return table


def flip_weight(weight):
    return jnp.transpose(weight[::-1], (0, 2, 1))


def pool_sum(field_in):
    table = jnp.asarray(pool_table()).astype(jnp.bfloat16)
    return jnp.einsum("bcv,vu->bcu", field_in, table, preferred_element_type=jnp.float32)


def enlarge(octants):
    table = jnp.asarray(pool_table()).astype(jnp.bfloat16)
    return jnp.einsum("bcu,vu->bcv", octants, table, preferred_element_type=jnp.float32)


def place_octants(octants):
    amount, channels = (octants.shape[0] // 8, octants.shape[1])
    grouped = octants.reshape(amount, 8, channels, 64)
    table = jnp.asarray(octant_table()).astype(jnp.bfloat16)
    return jnp.einsum("jocu,ouv->jcv", grouped, table, preferred_element_type=jnp.float32).astype(
        jnp.bfloat16
    )


def split_octants(coarse):
    amount, channels = (coarse.shape[0], coarse.shape[1])
    table = jnp.asarray(octant_table()).astype(jnp.bfloat16)
    parts = jnp.einsum("jcv,ouv->jocu", coarse, table, preferred_element_type=jnp.float32).astype(
        jnp.bfloat16
    )
    return parts.reshape(amount * 8, channels, 64)


def select_rows(picker, values):
    return jnp.dot(picker, values, preferred_element_type=jnp.float32).astype(jnp.bfloat16)


def route_places(slot_list, dev_index, moving, bricks):
    direction = slot_list // bricks - dev_index
    to_left = (direction == -1).astype(jnp.int32)
    to_right = (direction == 1).astype(jnp.int32)
    left_rank = jnp.cumsum(to_left) - to_left
    right_rank = jnp.cumsum(to_right) - to_right
    return jnp.where(
        to_left == 1, left_rank, jnp.where(to_right == 1, moving + right_rank, 2 * moving)
    ).astype(jnp.int32)


def lone_bricks(amount):
    centre = jnp.arange(27, dtype=jnp.int32)[None, :] == 13
    return jnp.where(centre, jnp.arange(amount, dtype=jnp.int32)[:, None], amount)


def select_both(picker, body, moved):
    values = jnp.concatenate([body.reshape(2, -1, 2048), moved], axis=1)
    picked = jnp.einsum("rs,csv->rcv", picker, values, preferred_element_type=jnp.float32)
    return picked.astype(jnp.bfloat16).reshape(picker.shape[0], -1, 64)


def gather_back(local_part, send_pick, returned):
    total = local_part.astype(jnp.float32) + jnp.dot(
        send_pick.T, returned, preferred_element_type=jnp.float32
    )
    return total.astype(jnp.bfloat16)


SPANS = {-1: (slice(0, 1), slice(7, 8)), 0: (slice(1, 9), slice(0, 8)), 1: (slice(9, 10), slice(0, 1))}
TAP_ORDER = np.array([1, 0, 2, 5, 4, 3, 7, 6, 8])
WIDTH = 640


def greet(devices):
    barrier = pltpu.get_barrier_semaphore()
    for device in devices:
        pl.semaphore_signal(
            barrier, inc=1, device_id=device, device_id_type=pl.DeviceIdType.MESH
        )
    pl.semaphore_wait(barrier, len(devices))


def nearby(count):
    me, core = lax.axis_index("space"), lax.axis_index("chan")
    return ((me + count - 1) % count, core), ((me + 1) % count, core), (me, 1 - core)


def sender(send_sems, recv_sems):
    def send(number, source, target, device):
        copy = pltpu.make_async_remote_copy(
            src_ref=source,
            dst_ref=target,
            send_sem=send_sems.at[number],
            recv_sem=recv_sems.at[number],
            device_id=device,
            device_id_type=pl.DeviceIdType.MESH,
        )
        copy.start()
        return copy

    return send


def trade_kernel(count, amount, *refs):
    rows, own = refs[:2]
    shares = refs[2 : 2 + amount]
    rows_all, fields = refs[2 + amount : 4 + amount]
    shares_all = refs[4 + amount : 4 + 2 * amount]
    send_sems, recv_sems, keep_sems = refs[4 + 2 * amount :]
    core = lax.axis_index("chan")
    left, right, mate = nearby(count)
    left_mate, right_mate = (left[0], 1 - core), (right[0], 1 - core)
    greet((left, right, mate, left_mate, right_mate))
    send = sender(send_sems, recv_sems)
    quick = [
        send(0, rows.at[0], rows_all.at[core, 1], left),
        send(1, rows.at[1], rows_all.at[core, 0], right),
        send(2, rows.at[0], rows_all.at[core, 1], left_mate),
        send(3, rows.at[1], rows_all.at[core, 0], right_mate),
    ]
    to_right = send(4, own, fields.at[core, 0], right)
    to_left = send(5, own, fields.at[core, 2], left)
    kept = []
    for number, (share, share_all) in enumerate(zip(shares, shares_all)):
        if len(share.shape) == 3:
            half = share.shape[1]
            spot = share_all.at[:, pl.ds(pl.multiple_of(core * half, half), half)]
        else:
            spot = share_all.at[core]
        quick.append(send(8 + number, share, spot, mate))
        kept.append(pltpu.make_async_copy(share, spot, keep_sems.at[1 + number]))
    quick.append(send(8 + amount, own, fields.at[core, 1], mate))
    kept.append(pltpu.make_async_copy(own, fields.at[core, 1], keep_sems.at[0]))
    for copy in kept:
        copy.start()
    to_right.wait_recv()
    quick.append(send(6, fields.at[core, 0], fields.at[core, 0], mate))
    to_left.wait_recv()
    quick.append(send(7, fields.at[core, 2], fields.at[core, 2], mate))
    for copy in quick:
        copy.wait_recv()
    for copy in quick + [to_right, to_left]:
        copy.wait_send()
    for copy in kept:
        copy.wait()


def trade(rows, own, shares, number):
    count = lax.axis_size("space")
    amount = len(shares)
    shapes = [(2,) + rows.shape, (2, 3) + own.shape]
    for share in shares:
        if share.ndim == 3:
            shapes.append((share.shape[0], 2 * share.shape[1], share.shape[2]))
        else:
            shapes.append((2,) + share.shape)
    return pl.pallas_call(
        lambda *refs: trade_kernel(count, amount, *refs),
        in_specs=[pl.BlockSpec(memory_space=pltpu.VMEM)] * 2
        + [pl.BlockSpec(memory_space=pltpu.HBM if share.ndim == 3 else pltpu.VMEM) for share in shares],
        out_specs=[
            pl.BlockSpec(memory_space=pltpu.HBM if len(shape) in (3, 5) and place else pltpu.VMEM)
            for place, shape in enumerate(shapes)
        ],
        out_shape=[jax.ShapeDtypeStruct(shape, rows.dtype) for shape in shapes],
        scratch_shapes=[
            pltpu.SemaphoreType.DMA((9 + amount,)),
            pltpu.SemaphoreType.DMA((9 + amount,)),
            pltpu.SemaphoreType.DMA((1 + amount,)),
        ],
        compiler_params=pltpu.CompilerParams(
            collective_id=number, has_side_effects=True, vmem_limit_bytes=12 * 1024 * 1024
        ),
    )(rows, own, *shares)


def ride_copies(count, refs):
    return [
        pltpu.make_async_remote_copy(
            src_ref=refs["ride"].at[side],
            dst_ref=refs["ride_in"].at[1 - side],
            send_sem=refs["ride_send"].at[side],
            recv_sem=refs["ride_recv"].at[side],
            device_id=device,
            device_id_type=pl.DeviceIdType.MESH,
        )
        for side, device in enumerate(nearby(count)[:2])
    ]


def hail(devices):
    barrier = pltpu.get_barrier_semaphore()
    for device in devices:
        pl.semaphore_signal(
            barrier, inc=1, device_id=device, device_id_type=pl.DeviceIdType.MESH
        )


def torus_sizes(count):
    return (16, 8) if count == 128 else (1, count)


class TorusSum:
    def __init__(self, count, refs, label):
        self.plane, self.depth = torus_sizes(count)
        me, self.core = lax.axis_index("space"), lax.axis_index("chan")
        self.at, self.level = me // self.depth, me % self.depth
        self.refs = {name: refs[label + name] for name in SUM_NAMES}

    def across(self, step):
        return (self.at + step) % self.plane * self.depth + self.level, self.core

    def along(self, step):
        return self.at * self.depth + (self.level + step) % self.depth, self.core

    def peers(self):
        return [self.across(step) for step in range(1, self.plane)] + [
            self.along(step) for step in range(1, self.depth)
        ]

    def copies(self, phase):
        refs = self.refs
        made = []
        for step in range(1, self.depth if phase == 1 else self.plane):
            if phase == 0:
                source = refs["data"].at[(self.at + step) % self.plane]
                target = refs["part"].at[step - 1]
            elif phase == 1:
                source = target = refs["levels"].at[self.level]
            else:
                source = target = refs["total"].at[self.at]
            made.append(
                pltpu.make_async_remote_copy(
                    src_ref=source,
                    dst_ref=target,
                    send_sem=refs["send"].at[phase, step - 1],
                    recv_sem=refs["recv"].at[phase, step - 1],
                    device_id=self.along(step) if phase == 1 else self.across(step),
                    device_id_type=pl.DeviceIdType.MESH,
                )
            )
        return made

    def start(self, phase):
        refs = self.refs
        if phase == 1:
            value = refs["data"][self.at]
            for step in range(1, self.plane):
                value = value + refs["part"][step - 1]
            refs["levels"][self.level] = value
        elif phase == 2:
            value = refs["levels"][0]
            for level in range(1, self.depth):
                value = value + refs["levels"][level]
            refs["total"][self.at] = value
        for copy in self.copies(phase):
            copy.start()

    def wait(self, phase):
        for copy in self.copies(phase):
            copy.wait_recv()

    def leave(self):
        for phase in range(3):
            for copy in self.copies(phase):
                copy.wait_send()


SUM_NAMES = ("data", "part", "levels", "total", "send", "recv")


def sum_scratch(count, rows, label, with_data):
    plane, depth = torus_sizes(count)
    piece = (128 // plane, rows, 128)
    firsts = {"part": max(1, plane - 1), "levels": depth, "total": plane}
    if with_data:
        firsts["data"] = plane
    scratch = {
        label + name: pltpu.VMEM((first,) + piece, jnp.float32) for name, first in firsts.items()
    }
    most = max(plane, depth) - 1
    scratch[label + "send"] = pltpu.SemaphoreType.DMA((3, most))
    scratch[label + "recv"] = pltpu.SemaphoreType.DMA((3, most))
    return scratch, (plane,) + piece


def fine_pieces(acc):
    pieces = []
    for tap_x in range(3):
        for block in range(acc.shape[1] // 4):
            for lane in range(WIDTH // 128):
                pieces.append((tap_x, slice(4 * block, 4 * block + 4), slice(128 * lane, 128 * lane + 128)))
    return pieces


def brick_kernel(count, masked, names, *refs):
    refs = dict(zip(names, refs))
    field_ref, table, padded, columns = [
        refs[name] for name in ("field", "table", "padded", "columns")
    ]
    brick = pl.program_id(0)
    last = pl.num_programs(0) - 1
    sums = "wide_data" in refs
    if sums:
        wide = TorusSum(count, refs, "wide_")
        slim = TorusSum(count, refs, "slim_")

    @pl.when(brick == 0)
    def fill():
        if count:
            fetch = pltpu.make_async_copy(refs["far_field"], field_ref, refs["field_sem"])
            fetch.start()
            greeted = list(nearby(count)[:2]) + (wide.peers() if sums else [])
            hail(greeted)
        slots = table.shape[0] - 1
        table[slots] = jnp.zeros((8, 8, 8, 128), jnp.float32)
        halves = len(field_ref.shape) == 5
        amount = field_ref.shape[2]

        def turn(slot, carry):
            if halves:
                place, one = slot // amount, slot % amount
                field = jnp.concatenate(
                    [field_ref[0, place, one], field_ref[1, place, one]], axis=0
                ).astype(jnp.float32)
            else:
                field = field_ref[slot].astype(jnp.float32)
            turned = jnp.concatenate([field, field], axis=0).T
            table[slot] = turned.reshape(8, 8, 8, 128)
            return carry

        if count:
            fetch.wait()
        lax.fori_loop(0, slots, turn, 0)
        if "acc" in refs:
            refs["acc"][...] = jnp.zeros_like(refs["acc"])

    if count:

        @pl.when(brick == 3)
        def depart():
            met = 2 + (len(wide.peers()) if sums else 0)
            pl.semaphore_wait(pltpu.get_barrier_semaphore(), met)
            for copy in ride_copies(count, refs):
                copy.start()
            if sums:
                wide.start(0)

    for index, (lean_x, lean_y, lean_z) in enumerate(lean_list()):
        slot = refs["near"][brick, index]
        to_x, from_x = SPANS[lean_x]
        to_y, from_y = SPANS[lean_y]
        padded[lean_z + 1, to_x, to_y] = table[slot, from_x, from_y]
    shape = (10, 8, 8, 128)
    place_z = lax.broadcasted_iota(jnp.int32, shape, 2)
    low_half = lax.broadcasted_iota(jnp.int32, shape, 3) < 64

    def put(position, low, high):
        both = jnp.where(low_half, low, high).reshape(640, 128)
        columns[:, 128 * position : 128 * position + 128] = both.astype(jnp.bfloat16)

    ahead = []
    for tap_y, position in enumerate((0, 2, 3)):
        below = padded[0, :, tap_y : tap_y + 8]
        level = padded[1, :, tap_y : tap_y + 8]
        above = padded[2, :, tap_y : tap_y + 8]
        minus = pltpu.roll(jnp.where(place_z == 7, below, level), 1, 2)
        put(position, level, minus)
        ahead.append(pltpu.roll(jnp.where(place_z == 0, above, level), 7, 2))
        if tap_y == 1:
            put(1, ahead[0], ahead[1])
    put(4, ahead[2], 0.0)
    if "weight" in refs:
        total = None
        for tap_x in range(3):
            part = lax.dot_general(
                refs["weight"][0, tap_x],
                columns[64 * tap_x : 64 * tap_x + 512, :],
                (((1,), (1,)), ((), ())),
                preferred_element_type=jnp.float32,
            )
            total = part if total is None else total + part
        if masked:
            total = jnp.where(brick < refs["live"][0], total, 0.0)
        refs["out"][0] = total.astype(refs["out"].dtype)
    if "grad" in refs:
        for tap_x in range(3):
            refs["acc"][tap_x] += jnp.dot(
                refs["grad"][0],
                columns[64 * tap_x : 64 * tap_x + 512, :],
                preferred_element_type=jnp.float32,
            )

    @pl.when(brick == last)
    def close():
        if sums:
            acc, data = refs["acc"], refs["slim_data"]
            cells = list(np.ndindex(data.shape[:2]))
            spans = fine_pieces(acc)
            for cell, span in zip(cells, spans):
                data[cell] = acc[span]
            for cell in cells[len(spans) :]:
                data[cell] = jnp.zeros(data.shape[2:], jnp.float32)
            slim.start(0)
            wide.wait(0)
            wide.start(1)
            slim.wait(0)
            slim.start(1)
            wide.wait(1)
            wide.start(2)
            slim.wait(1)
            slim.start(2)
            wide.wait(2)
            refs["wide_out"][...] = refs["wide_total"][...]
            slim.wait(2)
            refs["slim_out"][...] = refs["slim_total"][...]
            wide.leave()
            slim.leave()
        elif "acc" in refs:
            refs["total"][...] = refs["acc"][...]
        if count:
            for copy in ride_copies(count, refs):
                copy.wait()
            refs["ride_out"][...] = refs["ride_in"][...]


def brick_pass(
    field_in, near, live_count, weight, grad_rows, out_dtype, masked, ride=None, number=None,
    wide=None,
):
    amount = near.shape[0]
    count = 0 if ride is None else lax.axis_size("space")
    slots = 3 * field_in.shape[2] if field_in.ndim == 5 else field_in.shape[0]
    rows = weight.shape[2] if weight is not None else grad_rows.shape[1]
    ins, outs, scratch = {}, {}, {}

    def whole(shape):
        return pl.BlockSpec(shape, lambda b: (0,) * len(shape))

    def result(name, shape, dtype, spec=None):
        outs[name] = (jax.ShapeDtypeStruct(shape, dtype), spec or whole(shape))

    ins["near"] = (near, pl.BlockSpec(memory_space=pltpu.SMEM))
    ins["live"] = (live_count, pl.BlockSpec(memory_space=pltpu.SMEM))
    if count:
        ins["far_field"] = (field_in, pl.BlockSpec(memory_space=pltpu.HBM))
        scratch["field"] = pltpu.VMEM(field_in.shape, field_in.dtype)
        scratch["field_sem"] = pltpu.SemaphoreType.DMA
    else:
        ins["field"] = (field_in, whole(field_in.shape))
    scratch["table"] = pltpu.VMEM((slots + 1, 8, 8, 8, 128), jnp.float32)
    scratch["padded"] = pltpu.VMEM((3, 10, 10, 8, 128), jnp.float32)
    scratch["columns"] = pltpu.VMEM((640, WIDTH), jnp.bfloat16)
    by_brick = pl.BlockSpec((1, rows, 512), lambda b: (b, 0, 0))
    if weight is not None:
        parts = weight.shape[0]
        blocks = jnp.stack([weight_blocks(part) for part in weight])
        ins["weight"] = (
            blocks, pl.BlockSpec((1, 3, rows, WIDTH), lambda b: (b % parts, 0, 0, 0))
        )
        result("out", (amount, rows, 512), out_dtype, by_brick)
    if grad_rows is not None:
        ins["grad"] = (grad_rows, by_brick)
        scratch["acc"] = pltpu.VMEM((3, rows, WIDTH), jnp.float32)
        if wide is None:
            result("total", (3, rows, WIDTH), jnp.float32)
    if wide is not None:
        wide_scratch, wide_shape = sum_scratch(count, 8, "wide_", False)
        slim_scratch, slim_shape = sum_scratch(count, 4, "slim_", True)
        scratch.update(wide_scratch)
        scratch.update(slim_scratch)
        ins["wide_data"] = (wide.reshape(wide_shape), whole(wide_shape))
        result("wide_out", wide_shape, jnp.float32)
        result("slim_out", slim_shape, jnp.float32)
    if count:
        ins["ride"] = (ride, whole(ride.shape))
        result("ride_out", ride.shape, ride.dtype)
        scratch["ride_in"] = pltpu.VMEM(ride.shape, ride.dtype)
        scratch["ride_send"] = pltpu.SemaphoreType.DMA((2,))
        scratch["ride_recv"] = pltpu.SemaphoreType.DMA((2,))
    names = list(ins) + list(outs) + list(scratch)
    remote = {"collective_id": number, "has_side_effects": True} if count else {}
    room = 12 if slots < 8 else 20 if wide is None else 30
    products = (weight is not None) + (grad_rows is not None)
    return pl.pallas_call(
        lambda *refs: brick_kernel(count, masked, names, *refs),
        grid=(amount,),
        in_specs=[spec for _, spec in ins.values()],
        out_specs=[spec for _, spec in outs.values()],
        out_shape=[shape for shape, _ in outs.values()],
        scratch_shapes=list(scratch.values()),
        compiler_params=pltpu.CompilerParams(vmem_limit_bytes=room * 1024 * 1024, **remote),
        cost_estimate=pl.CostEstimate(
            flops=amount * products * 2 * rows * 3 * WIDTH * 512,
            bytes_accessed=slots * 64 * 512 * 2,
            transcendentals=0,
        ),
    )(*[value for value, _ in ins.values()])


def weight_blocks(weight):
    rows, channels = weight.shape[1:]
    taps = weight.reshape(3, 9, rows, channels)[:, TAP_ORDER]
    taps = jnp.concatenate([taps, jnp.zeros_like(taps[:, :1])], axis=1)
    return jnp.transpose(taps, (0, 2, 1, 3)).reshape(3, rows, WIDTH)


def finish_kernel(scales, slim, wide, fine_out, coarse_out):
    for pieces, out, scale in zip((slim, wide), (fine_out, coarse_out), scales):
        high = pieces.shape[1]
        blocks = out.shape[1] // high
        for tap_x in range(3):
            for block in range(blocks):
                first = WIDTH // 128 * (tap_x * blocks + block)
                rows = slice(high * block, high * block + high)
                for place, tap in enumerate(TAP_ORDER):
                    lanes = slice(64 * (place % 2), 64 * (place % 2) + 64)
                    out[9 * tap_x + int(tap), rows, :] = pieces[first + place // 2, :, lanes] * scale


def wide_pieces(coarse, project):
    tiles = jnp.transpose(coarse.reshape(-1, 8, WIDTH // 128, 128), (0, 2, 1, 3))
    tiles = tiles.reshape(-1, 8, 128)
    small = project.reshape(-1, 8, 128)
    spare = 128 - tiles.shape[0] - small.shape[0]
    return jnp.concatenate([tiles, small, jnp.zeros((spare, 8, 128), jnp.float32)], axis=0)


def finish(slim, wide, fine_rows, coarse_rows, scales):
    slim, wide = slim.reshape(128, 4, 128), wide.reshape(128, 8, 128)
    fine_sum, coarse_sum = pl.pallas_call(
        lambda *refs: finish_kernel(scales, *refs),
        in_specs=[pl.BlockSpec(memory_space=pltpu.VMEM)] * 2,
        out_specs=[pl.BlockSpec(memory_space=pltpu.VMEM)] * 2,
        out_shape=[
            jax.ShapeDtypeStruct((27, rows, 64), jnp.float32) for rows in (fine_rows, coarse_rows)
        ],
    )(slim, wide)
    used = 3 * coarse_rows // 8 * (WIDTH // 128)
    return fine_sum, coarse_sum, wide[used : used + 4].reshape(64, 64)


def per_device(
    feats, live_count, neighbours, parent, fine_weight, coarse_weight, project_weight, cotangent
):
    bricks = feats.shape[0]
    half_channels = feats.shape[1]
    devices = lax.axis_size("space")
    own_index = lax.axis_index("space")
    moving = max(1, bricks // 8)
    coarse_bricks = bricks // 8
    live_mask = (jnp.arange(bricks, dtype=jnp.int32) < live_count[0]).astype(jnp.float32)[
        :, None, None
    ]
    core = lax.axis_index("chan")
    send_place = route_places(parent, own_index, moving, bricks)
    send_pick = (jnp.arange(2 * moving, dtype=jnp.int32)[:, None] == send_place[None, :]).astype(
        jnp.bfloat16
    )
    pooled = (pool_sum(feats) * 0.125 * live_mask).astype(jnp.bfloat16).reshape(bricks, -1)
    slot_rows = jnp.broadcast_to(
        (parent % bricks + 1).astype(jnp.bfloat16)[:, None], (bricks, 2048)
    )
    outgoing = select_rows(send_pick, jnp.concatenate([pooled, slot_rows], axis=1))
    grad_rows = (cotangent.astype(jnp.float32) * live_mask).astype(jnp.bfloat16)
    incoming, grad_fields, both_pooled, whole_coarse, whole_fine, both_project = trade(
        outgoing.reshape(2, moving * 32, 128),
        grad_rows,
        [pooled.reshape(bricks * 16, 128), coarse_weight, fine_weight, project_weight],
        2,
    )
    whole_project = jnp.concatenate([both_project[0], both_project[1]], axis=1)
    incoming = incoming.reshape(2, 2 * moving, 4096)
    incoming_slots = incoming[0, :, -1].astype(jnp.int32) - 1
    local_slots = jnp.where(parent // bricks == own_index, parent % bricks, -1)
    all_slots = jnp.concatenate([local_slots, incoming_slots])
    receive_pick = (jnp.arange(bricks, dtype=jnp.int32)[:, None] == all_slots[None, :]).astype(
        jnp.bfloat16
    )
    arrived = select_both(receive_pick, both_pooled, incoming[:, :, :2048])
    coarse_in = place_octants(arrived)
    lone = lone_bricks(coarse_bricks)
    preactivation = brick_pass(
        coarse_in, lone, live_count, whole_coarse[None], None, jnp.float32, False
    )[0]
    hidden = jax.nn.silu(preactivation).astype(jnp.bfloat16)
    own_project = lax.dynamic_slice_in_dim(
        whole_project, core * half_channels, half_channels, 0
    )
    coarse_out = jnp.einsum(
        "cj,bjv->bcv", own_project, hidden, preferred_element_type=jnp.float32
    ).astype(jnp.bfloat16)
    back_source = select_rows(receive_pick.T, split_octants(coarse_out).reshape(bricks, -1))
    last_brick = devices * bricks
    near_local = jnp.where(
        neighbours >= last_brick, 3 * bricks, neighbours - (own_index - 1) * bricks
    ).astype(jnp.int32)
    slots = jnp.arange(bricks, dtype=jnp.int32)[:, None] + bricks
    near = jnp.concatenate([near_local[:, :13], slots, near_local[:, 13:]], axis=1)
    own_weight = lax.dynamic_slice_in_dim(whole_fine, core * half_channels, half_channels, 2)
    back_feats, rode_back = brick_pass(
        grad_fields,
        near,
        live_count,
        flip_weight(own_weight)[None],
        None,
        jnp.bfloat16,
        True,
        back_source[bricks:].reshape(2, moving * 16, 128),
        3,
    )
    up_octants = gather_back(
        back_source[:bricks], send_pick, rode_back.reshape(2 * moving, -1)
    ).reshape(bricks, half_channels, 64)
    mixed_feats = ((feats.astype(jnp.float32) + enlarge(up_octants)) * live_mask).astype(
        jnp.bfloat16
    )
    up_grad = pool_sum(back_feats).astype(jnp.bfloat16).reshape(bricks, -1)
    outgoing_grad = select_rows(send_pick, up_grad)
    incoming_grad, feat_fields, both_grad = trade(
        outgoing_grad.reshape(2, moving * 16, 128),
        mixed_feats,
        [up_grad.reshape(bricks * 16, 128)],
        4,
    )
    coarse_grad = place_octants(
        select_both(receive_pick, both_grad, incoming_grad.reshape(2, 2 * moving, 2048))
    )
    hidden_half = hidden.shape[1] // 2
    own_hidden = lax.dynamic_slice_in_dim(hidden, core * hidden_half, hidden_half, 1)
    project_matrix = jnp.einsum(
        "bcv,bjv->cj", coarse_grad, own_hidden, preferred_element_type=jnp.float32
    )
    hidden_grad = jnp.einsum(
        "cj,bcv->bjv", whole_project, coarse_grad, preferred_element_type=jnp.float32
    )
    sigmoid_pre = jax.nn.sigmoid(preactivation)
    pre_grad = (hidden_grad * sigmoid_pre * (1.0 + preactivation * (1.0 - sigmoid_pre))).astype(
        jnp.bfloat16
    )
    own_pre_grad = lax.dynamic_slice_in_dim(pre_grad, core * hidden_half, hidden_half, 1)
    coarse_total = brick_pass(
        coarse_in, lone, live_count, None, own_pre_grad, None, False
    )[0]
    own_coarse = flip_weight(
        lax.dynamic_slice_in_dim(whole_coarse, core * half_channels, half_channels, 2)
    )
    coarse_terms = brick_pass(
        pre_grad.reshape(2 * coarse_bricks, hidden_half, 512),
        lone_bricks(2 * coarse_bricks),
        live_count,
        jnp.stack([own_coarse[:, :, :hidden_half], own_coarse[:, :, hidden_half:]]),
        None,
        jnp.float32,
        False,
    )[0]
    coarse_back = (
        coarse_terms.reshape(coarse_bricks, 2, half_channels, 512).sum(1).astype(jnp.bfloat16)
    )
    down_source = select_rows(receive_pick.T, split_octants(coarse_back).reshape(bricks, -1))
    out_feats, wide_sum, slim_sum, rode_down = brick_pass(
        feat_fields,
        near,
        live_count,
        fine_weight[None],
        grad_rows,
        jnp.bfloat16,
        True,
        down_source[bricks:].reshape(2, moving * 16, 128),
        5,
        wide_pieces(coarse_total, project_matrix),
    )
    down_grad = gather_back(
        down_source[:bricks], send_pick, rode_down.reshape(2 * moving, -1)
    ).reshape(bricks, half_channels, 64)
    grad_feats = (back_feats.astype(jnp.float32) + live_mask * enlarge(down_grad) * 0.125).astype(
        jnp.bfloat16
    )
    fine_scale = 1.0 / math.sqrt(512.0 * bricks * devices)
    coarse_scale = 1.0 / math.sqrt(512.0 * coarse_bricks * devices)
    fine_weight_grad, coarse_weight_grad, project_total = finish(
        slim_sum, wide_sum, half_channels, hidden_half, (fine_scale, coarse_scale)
    )
    project_weight_grad = project_total * coarse_scale
    return (out_feats, grad_feats, fine_weight_grad, coarse_weight_grad, project_weight_grad)


def solution(mesh):
    placed = (
        P("space", "chan", None),
        P("space"),
        P("space", None),
        P("space"),
        P(None, "chan", None),
        P(None, "chan", None),
        P(None, "chan"),
        P("space", "chan", None),
    )
    return jax.shard_map(
        per_device,
        mesh=mesh,
        in_specs=placed,
        out_specs=(
            P("space", "chan", None),
            P("space", "chan", None),
            P(None, "chan", None),
            P(None, "chan", None),
            P(None, "chan"),
        ),
        check_vma=False,
    )
```

```python
import math

import jax
import jax.numpy as jnp
import numpy as np
from jax import lax
from jax.experimental import pallas as pl
from jax.experimental.pallas import tpu as pltpu
from jax.sharding import PartitionSpec as P


def lean_list():
    leans = []
    for lean_x in (-1, 0, 1):
        for lean_y in (-1, 0, 1):
            for lean_z in (-1, 0, 1):
                leans.append((lean_x, lean_y, lean_z))
    return leans


def pool_table():
    voxel = np.arange(512)
    octant_voxel = 16 * (voxel // 128) + 4 * (voxel // 16 % 4) + voxel % 8 // 2
    return (octant_voxel[:, None] == np.arange(64)[None, :]).astype(np.float32)


def octant_table():
    voxel = np.arange(512)
    coord_x = voxel // 64
    coord_y = voxel // 8 % 8
    coord_z = voxel % 8
    octant = 4 * (coord_x // 4) + 2 * (coord_y // 4) + coord_z // 4
    inner = 16 * (coord_x % 4) + 4 * (coord_y % 4) + coord_z % 4
    table = np.zeros((8, 64, 512), np.float32)
    table[octant, inner, voxel] = 1.0
    return table


def flip_weight(weight):
    return jnp.transpose(weight[::-1], (0, 2, 1))


def pool_sum(field_in):
    table = jnp.asarray(pool_table()).astype(jnp.bfloat16)
    return jnp.einsum("bcv,vu->bcu", field_in, table, preferred_element_type=jnp.float32)


def enlarge(octants):
    table = jnp.asarray(pool_table()).astype(jnp.bfloat16)
    return jnp.einsum("bcu,vu->bcv", octants, table, preferred_element_type=jnp.float32)


def place_octants(octants):
    amount, channels = (octants.shape[0] // 8, octants.shape[1])
    grouped = octants.reshape(amount, 8, channels, 64)
    table = jnp.asarray(octant_table()).astype(jnp.bfloat16)
    return jnp.einsum("jocu,ouv->jcv", grouped, table, preferred_element_type=jnp.float32).astype(
        jnp.bfloat16
    )


def split_octants(coarse):
    amount, channels = (coarse.shape[0], coarse.shape[1])
    table = jnp.asarray(octant_table()).astype(jnp.bfloat16)
    parts = jnp.einsum("jcv,ouv->jocu", coarse, table, preferred_element_type=jnp.float32).astype(
        jnp.bfloat16
    )
    return parts.reshape(amount * 8, channels, 64)


def select_rows(picker, values):
    return jnp.dot(picker, values, preferred_element_type=jnp.float32).astype(jnp.bfloat16)


def route_places(slot_list, dev_index, moving, bricks):
    direction = slot_list // bricks - dev_index
    to_left = (direction == -1).astype(jnp.int32)
    to_right = (direction == 1).astype(jnp.int32)
    left_rank = jnp.cumsum(to_left) - to_left
    right_rank = jnp.cumsum(to_right) - to_right
    return jnp.where(
        to_left == 1, left_rank, jnp.where(to_right == 1, moving + right_rank, 2 * moving)
    ).astype(jnp.int32)


def lone_bricks(amount):
    centre = jnp.arange(27, dtype=jnp.int32)[None, :] == 13
    return jnp.where(centre, jnp.arange(amount, dtype=jnp.int32)[:, None], amount)


def select_both(picker, body, moved):
    values = jnp.concatenate([body.reshape(2, -1, 2048), moved], axis=1)
    picked = jnp.einsum("rs,csv->rcv", picker, values, preferred_element_type=jnp.float32)
    return picked.astype(jnp.bfloat16).reshape(picker.shape[0], -1, 64)


def gather_back(local_part, send_pick, returned):
    total = local_part.astype(jnp.float32) + jnp.dot(
        send_pick.T, returned, preferred_element_type=jnp.float32
    )
    return total.astype(jnp.bfloat16)


SPANS = {-1: (slice(0, 1), slice(7, 8)), 0: (slice(1, 9), slice(0, 8)), 1: (slice(9, 10), slice(0, 1))}
TAP_ORDER = np.array([1, 0, 2, 5, 4, 3, 7, 6, 8])
WIDTH = 640


def greet(devices):
    barrier = pltpu.get_barrier_semaphore()
    for device in devices:
        pl.semaphore_signal(
            barrier, inc=1, device_id=device, device_id_type=pl.DeviceIdType.MESH
        )
    pl.semaphore_wait(barrier, len(devices))


def nearby(count):
    me, core = lax.axis_index("space"), lax.axis_index("chan")
    return ((me + count - 1) % count, core), ((me + 1) % count, core), (me, 1 - core)


def sender(send_sems, recv_sems):
    def send(number, source, target, device):
        copy = pltpu.make_async_remote_copy(
            src_ref=source,
            dst_ref=target,
            send_sem=send_sems.at[number],
            recv_sem=recv_sems.at[number],
            device_id=device,
            device_id_type=pl.DeviceIdType.MESH,
        )
        copy.start()
        return copy

    return send


def trade_kernel(count, amount, *refs):
    rows, own = refs[:2]
    shares = refs[2 : 2 + amount]
    rows_all, fields = refs[2 + amount : 4 + amount]
    shares_all = refs[4 + amount : 4 + 2 * amount]
    send_sems, recv_sems, keep_sems = refs[4 + 2 * amount :]
    core = lax.axis_index("chan")
    left, right, mate = nearby(count)
    left_mate, right_mate = (left[0], 1 - core), (right[0], 1 - core)
    greet((left, right, mate, left_mate, right_mate))
    send = sender(send_sems, recv_sems)
    quick = [
        send(0, rows.at[0], rows_all.at[core, 1], left),
        send(1, rows.at[1], rows_all.at[core, 0], right),
        send(2, rows.at[0], rows_all.at[core, 1], left_mate),
        send(3, rows.at[1], rows_all.at[core, 0], right_mate),
    ]
    to_right = send(4, own, fields.at[core, 0], right)
    to_left = send(5, own, fields.at[core, 2], left)
    kept = []
    for number, (share, share_all) in enumerate(zip(shares, shares_all)):
        if len(share.shape) == 3:
            half = share.shape[1]
            spot = share_all.at[:, pl.ds(pl.multiple_of(core * half, half), half)]
        else:
            spot = share_all.at[core]
        quick.append(send(8 + number, share, spot, mate))
        kept.append(pltpu.make_async_copy(share, spot, keep_sems.at[1 + number]))
    quick.append(send(8 + amount, own, fields.at[core, 1], mate))
    kept.append(pltpu.make_async_copy(own, fields.at[core, 1], keep_sems.at[0]))
    for copy in kept:
        copy.start()
    to_right.wait_recv()
    quick.append(send(6, fields.at[core, 0], fields.at[core, 0], mate))
    to_left.wait_recv()
    quick.append(send(7, fields.at[core, 2], fields.at[core, 2], mate))
    for copy in quick:
        copy.wait_recv()
    for copy in quick + [to_right, to_left]:
        copy.wait_send()
    for copy in kept:
        copy.wait()


def trade(rows, own, shares, number):
    count = lax.axis_size("space")
    amount = len(shares)
    shapes = [(2,) + rows.shape, (2, 3) + own.shape]
    for share in shares:
        if share.ndim == 3:
            shapes.append((share.shape[0], 2 * share.shape[1], share.shape[2]))
        else:
            shapes.append((2,) + share.shape)
    return pl.pallas_call(
        lambda *refs: trade_kernel(count, amount, *refs),
        in_specs=[pl.BlockSpec(memory_space=pltpu.VMEM)] * 2
        + [pl.BlockSpec(memory_space=pltpu.HBM if share.ndim == 3 else pltpu.VMEM) for share in shares],
        out_specs=[
            pl.BlockSpec(memory_space=pltpu.HBM if len(shape) in (3, 5) and place else pltpu.VMEM)
            for place, shape in enumerate(shapes)
        ],
        out_shape=[jax.ShapeDtypeStruct(shape, rows.dtype) for shape in shapes],
        scratch_shapes=[
            pltpu.SemaphoreType.DMA((9 + amount,)),
            pltpu.SemaphoreType.DMA((9 + amount,)),
            pltpu.SemaphoreType.DMA((1 + amount,)),
        ],
        compiler_params=pltpu.CompilerParams(
            collective_id=number, has_side_effects=True, vmem_limit_bytes=12 * 1024 * 1024
        ),
    )(rows, own, *shares)


def ride_copies(count, refs):
    return [
        pltpu.make_async_remote_copy(
            src_ref=refs["ride"].at[side],
            dst_ref=refs["ride_in"].at[1 - side],
            send_sem=refs["ride_send"].at[side],
            recv_sem=refs["ride_recv"].at[side],
            device_id=device,
            device_id_type=pl.DeviceIdType.MESH,
        )
        for side, device in enumerate(nearby(count)[:2])
    ]


def hail(devices):
    barrier = pltpu.get_barrier_semaphore()
    for device in devices:
        pl.semaphore_signal(
            barrier, inc=1, device_id=device, device_id_type=pl.DeviceIdType.MESH
        )


def torus_sizes(count):
    return (16, 8) if count == 128 else (1, count)


class TorusSum:
    def __init__(self, count, refs, label):
        self.plane, self.depth = torus_sizes(count)
        me, self.core = lax.axis_index("space"), lax.axis_index("chan")
        self.at, self.level = me // self.depth, me % self.depth
        self.refs = {name: refs[label + name] for name in SUM_NAMES}

    def across(self, step):
        return (self.at + step) % self.plane * self.depth + self.level, self.core

    def along(self, step):
        return self.at * self.depth + (self.level + step) % self.depth, self.core

    def peers(self):
        return [self.across(step) for step in range(1, self.plane)] + [
            self.along(step) for step in range(1, self.depth)
        ]

    def copies(self, phase):
        refs = self.refs
        made = []
        for step in range(1, self.depth if phase == 1 else self.plane):
            if phase == 0:
                source = refs["data"].at[(self.at + step) % self.plane]
                target = refs["part"].at[step - 1]
            elif phase == 1:
                source = target = refs["levels"].at[self.level]
            else:
                source = target = refs["total"].at[self.at]
            made.append(
                pltpu.make_async_remote_copy(
                    src_ref=source,
                    dst_ref=target,
                    send_sem=refs["send"].at[phase, step - 1],
                    recv_sem=refs["recv"].at[phase, step - 1],
                    device_id=self.along(step) if phase == 1 else self.across(step),
                    device_id_type=pl.DeviceIdType.MESH,
                )
            )
        return made

    def start(self, phase):
        refs = self.refs
        if phase == 1:
            value = refs["data"][self.at]
            for step in range(1, self.plane):
                value = value + refs["part"][step - 1]
            refs["levels"][self.level] = value
        elif phase == 2:
            value = refs["levels"][0]
            for level in range(1, self.depth):
                value = value + refs["levels"][level]
            refs["total"][self.at] = value
        for copy in self.copies(phase):
            copy.start()

    def wait(self, phase):
        for copy in self.copies(phase):
            copy.wait_recv()

    def leave(self):
        for phase in range(3):
            for copy in self.copies(phase):
                copy.wait_send()


SUM_NAMES = ("data", "part", "levels", "total", "send", "recv")


def sum_scratch(count, rows, label, with_data):
    plane, depth = torus_sizes(count)
    piece = (128 // plane, rows, 128)
    firsts = {"part": max(1, plane - 1), "levels": depth, "total": plane}
    if with_data:
        firsts["data"] = plane
    scratch = {
        label + name: pltpu.VMEM((first,) + piece, jnp.float32) for name, first in firsts.items()
    }
    most = max(plane, depth) - 1
    scratch[label + "send"] = pltpu.SemaphoreType.DMA((3, most))
    scratch[label + "recv"] = pltpu.SemaphoreType.DMA((3, most))
    return scratch, (plane,) + piece


def fine_pieces(acc):
    pieces = []
    for tap_x in range(3):
        for block in range(acc.shape[1] // 4):
            for lane in range(WIDTH // 128):
                pieces.append((tap_x, slice(4 * block, 4 * block + 4), slice(128 * lane, 128 * lane + 128)))
    return pieces


def brick_kernel(count, masked, scales, names, *refs):
    refs = dict(zip(names, refs))
    field_ref, table, padded, columns = [
        refs[name] for name in ("field", "table", "padded", "columns")
    ]
    brick = pl.program_id(0)
    last = pl.num_programs(0) - 1
    sums = "wide_data" in refs
    if sums:
        wide = TorusSum(count, refs, "wide_")
        slim = TorusSum(count, refs, "slim_")

    @pl.when(brick == 0)
    def fill():
        if count:
            fetch = pltpu.make_async_copy(refs["far_field"], field_ref, refs["field_sem"])
            fetch.start()
            greeted = list(nearby(count)[:2]) + (wide.peers() if sums else [])
            hail(greeted)
        slots = table.shape[0] - 1
        table[slots] = jnp.zeros((8, 8, 8, 128), jnp.float32)
        halves = len(field_ref.shape) == 5
        amount = field_ref.shape[2]

        def turn(slot, carry):
            if halves:
                place, one = slot // amount, slot % amount
                field = jnp.concatenate(
                    [field_ref[0, place, one], field_ref[1, place, one]], axis=0
                ).astype(jnp.float32)
            else:
                field = field_ref[slot].astype(jnp.float32)
            turned = jnp.concatenate([field, field], axis=0).T
            table[slot] = turned.reshape(8, 8, 8, 128)
            return carry

        if count:
            fetch.wait()
        lax.fori_loop(0, slots, turn, 0)
        if "acc" in refs:
            refs["acc"][...] = jnp.zeros_like(refs["acc"])

    if count:

        @pl.when(brick == 2)
        def depart():
            met = 2 + (len(wide.peers()) if sums else 0)
            pl.semaphore_wait(pltpu.get_barrier_semaphore(), met)
            for copy in ride_copies(count, refs):
                copy.start()
            if sums:
                wide.start(0)

    if sums:

        @pl.when(brick == last - 1)
        def second():
            wide.wait(0)
            wide.start(1)

    for index, (lean_x, lean_y, lean_z) in enumerate(lean_list()):
        slot = refs["near"][brick, index]
        to_x, from_x = SPANS[lean_x]
        to_y, from_y = SPANS[lean_y]
        padded[lean_z + 1, to_x, to_y] = table[slot, from_x, from_y]
    shape = (10, 8, 8, 128)
    place_z = lax.broadcasted_iota(jnp.int32, shape, 2)
    low_half = lax.broadcasted_iota(jnp.int32, shape, 3) < 64

    def put(position, low, high):
        both = jnp.where(low_half, low, high).reshape(640, 128)
        columns[:, 128 * position : 128 * position + 128] = both.astype(jnp.bfloat16)

    ahead = []
    for tap_y, position in enumerate((0, 2, 3)):
        below = padded[0, :, tap_y : tap_y + 8]
        level = padded[1, :, tap_y : tap_y + 8]
        above = padded[2, :, tap_y : tap_y + 8]
        minus = pltpu.roll(jnp.where(place_z == 7, below, level), 1, 2)
        put(position, level, minus)
        ahead.append(pltpu.roll(jnp.where(place_z == 0, above, level), 7, 2))
        if tap_y == 1:
            put(1, ahead[0], ahead[1])
    put(4, ahead[2], 0.0)
    if "weight" in refs:
        total = None
        for tap_x in range(3):
            part = lax.dot_general(
                refs["weight"][0, tap_x],
                columns[64 * tap_x : 64 * tap_x + 512, :],
                (((1,), (1,)), ((), ())),
                preferred_element_type=jnp.float32,
            )
            total = part if total is None else total + part
        if masked:
            total = jnp.where(brick < refs["live"][0], total, 0.0)
        refs["out"][0] = total.astype(refs["out"].dtype)
    if "grad" in refs:
        for tap_x in range(3):
            refs["acc"][tap_x] += jnp.dot(
                refs["grad"][0],
                columns[64 * tap_x : 64 * tap_x + 512, :],
                preferred_element_type=jnp.float32,
            )

    @pl.when(brick == last)
    def close():
        if sums:
            acc, data = refs["acc"], refs["slim_data"]
            cells = list(np.ndindex(data.shape[:2]))
            spans = fine_pieces(acc)
            for cell, span in zip(cells, spans):
                data[cell] = acc[span]
            for cell in cells[len(spans) :]:
                data[cell] = jnp.zeros(data.shape[2:], jnp.float32)
            slim.start(0)
            wide.wait(1)
            wide.start(2)
            slim.wait(0)
            slim.start(1)
            wide.wait(2)
            unpack(refs["wide_total"], refs["coarse_out"], scales[1])
            used = 3 * refs["coarse_out"].shape[1] // 8 * (WIDTH // 128)
            plain = refs["wide_total"]
            for tile in range(refs["project_out"].shape[0]):
                at = divmod(used + tile, plain.shape[1])
                refs["project_out"][tile] = plain[at] * scales[1]
            slim.wait(1)
            slim.start(2)
            slim.wait(2)
            unpack(refs["slim_total"], refs["fine_out"], scales[0])
            wide.leave()
            slim.leave()
        elif "acc" in refs:
            refs["total"][...] = refs["acc"][...]
        if count:
            for copy in ride_copies(count, refs):
                copy.wait()
            refs["ride_out"][...] = refs["ride_in"][...]


def brick_pass(
    field_in, near, live_count, weight, grad_rows, out_dtype, masked, ride=None, number=None,
    wide=None, scales=None,
):
    amount = near.shape[0]
    count = 0 if ride is None else lax.axis_size("space")
    slots = 3 * field_in.shape[2] if field_in.ndim == 5 else field_in.shape[0]
    rows = weight.shape[2] if weight is not None else grad_rows.shape[1]
    ins, outs, scratch = {}, {}, {}

    def whole(shape):
        return pl.BlockSpec(shape, lambda b: (0,) * len(shape))

    def result(name, shape, dtype, spec=None):
        outs[name] = (jax.ShapeDtypeStruct(shape, dtype), spec or whole(shape))

    ins["near"] = (near, pl.BlockSpec(memory_space=pltpu.SMEM))
    ins["live"] = (live_count, pl.BlockSpec(memory_space=pltpu.SMEM))
    if count:
        ins["far_field"] = (field_in, pl.BlockSpec(memory_space=pltpu.HBM))
        scratch["field"] = pltpu.VMEM(field_in.shape, field_in.dtype)
        scratch["field_sem"] = pltpu.SemaphoreType.DMA
    else:
        ins["field"] = (field_in, whole(field_in.shape))
    scratch["table"] = pltpu.VMEM((slots + 1, 8, 8, 8, 128), jnp.float32)
    scratch["padded"] = pltpu.VMEM((3, 10, 10, 8, 128), jnp.float32)
    scratch["columns"] = pltpu.VMEM((640, WIDTH), jnp.bfloat16)
    by_brick = pl.BlockSpec((1, rows, 512), lambda b: (b, 0, 0))
    if weight is not None:
        parts = weight.shape[0]
        blocks = jnp.stack([weight_blocks(part) for part in weight])
        ins["weight"] = (
            blocks, pl.BlockSpec((1, 3, rows, WIDTH), lambda b: (b % parts, 0, 0, 0))
        )
        result("out", (amount, rows, 512), out_dtype, by_brick)
    if grad_rows is not None:
        ins["grad"] = (grad_rows, by_brick)
        scratch["acc"] = pltpu.VMEM((3, rows, WIDTH), jnp.float32)
        if wide is None:
            result("total", (3, rows, WIDTH), jnp.float32)
    if wide is not None:
        wide_scratch, wide_shape = sum_scratch(count, 8, "wide_", False)
        slim_scratch, slim_shape = sum_scratch(count, 4, "slim_", True)
        scratch.update(wide_scratch)
        scratch.update(slim_scratch)
        ins["wide_data"] = (wide.reshape(wide_shape), whole(wide_shape))
        result("fine_out", (27, rows, 64), jnp.float32)
        result("coarse_out", (27, 64, 64), jnp.float32)
        result("project_out", (4, 8, 128), jnp.float32)
    if count:
        ins["ride"] = (ride, whole(ride.shape))
        result("ride_out", ride.shape, ride.dtype)
        scratch["ride_in"] = pltpu.VMEM(ride.shape, ride.dtype)
        scratch["ride_send"] = pltpu.SemaphoreType.DMA((2,))
        scratch["ride_recv"] = pltpu.SemaphoreType.DMA((2,))
    names = list(ins) + list(outs) + list(scratch)
    remote = {"collective_id": number, "has_side_effects": True} if count else {}
    room = 12 if slots < 8 else 20 if wide is None else 30
    products = (weight is not None) + (grad_rows is not None)
    return pl.pallas_call(
        lambda *refs: brick_kernel(count, masked, scales, names, *refs),
        grid=(amount,),
        in_specs=[spec for _, spec in ins.values()],
        out_specs=[spec for _, spec in outs.values()],
        out_shape=[shape for shape, _ in outs.values()],
        scratch_shapes=list(scratch.values()),
        compiler_params=pltpu.CompilerParams(vmem_limit_bytes=room * 1024 * 1024, **remote),
        cost_estimate=pl.CostEstimate(
            flops=amount * products * 2 * rows * 3 * WIDTH * 512,
            bytes_accessed=slots * 64 * 512 * 2,
            transcendentals=0,
        ),
    )(*[value for value, _ in ins.values()])


def weight_blocks(weight):
    rows, channels = weight.shape[1:]
    taps = weight.reshape(3, 9, rows, channels)[:, TAP_ORDER]
    taps = jnp.concatenate([taps, jnp.zeros_like(taps[:, :1])], axis=1)
    return jnp.transpose(taps, (0, 2, 1, 3)).reshape(3, rows, WIDTH)


def unpack(total, out, scale):
    high = total.shape[2]
    blocks = out.shape[1] // high
    for tap_x in range(3):
        for block in range(blocks):
            first = WIDTH // 128 * (tap_x * blocks + block)
            rows = slice(high * block, high * block + high)
            for place, tap in enumerate(TAP_ORDER):
                lanes = slice(64 * (place % 2), 64 * (place % 2) + 64)
                plane, piece = divmod(first + place // 2, total.shape[1])
                out[9 * tap_x + int(tap), rows, :] = total[plane, piece, :, lanes] * scale


def wide_pieces(coarse, project):
    tiles = jnp.transpose(coarse.reshape(-1, 8, WIDTH // 128, 128), (0, 2, 1, 3))
    tiles = tiles.reshape(-1, 8, 128)
    small = project.reshape(-1, 8, 128)
    spare = 128 - tiles.shape[0] - small.shape[0]
    return jnp.concatenate([tiles, small, jnp.zeros((spare, 8, 128), jnp.float32)], axis=0)


def per_device(
    feats, live_count, neighbours, parent, fine_weight, coarse_weight, project_weight, cotangent
):
    bricks = feats.shape[0]
    half_channels = feats.shape[1]
    devices = lax.axis_size("space")
    own_index = lax.axis_index("space")
    moving = max(1, bricks // 8)
    coarse_bricks = bricks // 8
    live_mask = (jnp.arange(bricks, dtype=jnp.int32) < live_count[0]).astype(jnp.float32)[
        :, None, None
    ]
    core = lax.axis_index("chan")
    send_place = route_places(parent, own_index, moving, bricks)
    send_pick = (jnp.arange(2 * moving, dtype=jnp.int32)[:, None] == send_place[None, :]).astype(
        jnp.bfloat16
    )
    pooled = (pool_sum(feats) * 0.125 * live_mask).astype(jnp.bfloat16).reshape(bricks, -1)
    slot_rows = jnp.broadcast_to(
        (parent % bricks + 1).astype(jnp.bfloat16)[:, None], (bricks, 2048)
    )
    outgoing = select_rows(send_pick, jnp.concatenate([pooled, slot_rows], axis=1))
    grad_rows = (cotangent.astype(jnp.float32) * live_mask).astype(jnp.bfloat16)
    incoming, grad_fields, both_pooled, whole_coarse, whole_fine, both_project = trade(
        outgoing.reshape(2, moving * 32, 128),
        grad_rows,
        [pooled.reshape(bricks * 16, 128), coarse_weight, fine_weight, project_weight],
        2,
    )
    whole_project = jnp.concatenate([both_project[0], both_project[1]], axis=1)
    incoming = incoming.reshape(2, 2 * moving, 4096)
    incoming_slots = incoming[0, :, -1].astype(jnp.int32) - 1
    local_slots = jnp.where(parent // bricks == own_index, parent % bricks, -1)
    all_slots = jnp.concatenate([local_slots, incoming_slots])
    receive_pick = (jnp.arange(bricks, dtype=jnp.int32)[:, None] == all_slots[None, :]).astype(
        jnp.bfloat16
    )
    arrived = select_both(receive_pick, both_pooled, incoming[:, :, :2048])
    coarse_in = place_octants(arrived)
    lone = lone_bricks(coarse_bricks)
    preactivation = brick_pass(
        coarse_in, lone, live_count, whole_coarse[None], None, jnp.float32, False
    )[0]
    hidden = jax.nn.silu(preactivation).astype(jnp.bfloat16)
    own_project = lax.dynamic_slice_in_dim(
        whole_project, core * half_channels, half_channels, 0
    )
    coarse_out = jnp.einsum(
        "cj,bjv->bcv", own_project, hidden, preferred_element_type=jnp.float32
    ).astype(jnp.bfloat16)
    back_source = select_rows(receive_pick.T, split_octants(coarse_out).reshape(bricks, -1))
    last_brick = devices * bricks
    near_local = jnp.where(
        neighbours >= last_brick, 3 * bricks, neighbours - (own_index - 1) * bricks
    ).astype(jnp.int32)
    slots = jnp.arange(bricks, dtype=jnp.int32)[:, None] + bricks
    near = jnp.concatenate([near_local[:, :13], slots, near_local[:, 13:]], axis=1)
    own_weight = lax.dynamic_slice_in_dim(whole_fine, core * half_channels, half_channels, 2)
    back_feats, rode_back = brick_pass(
        grad_fields,
        near,
        live_count,
        flip_weight(own_weight)[None],
        None,
        jnp.bfloat16,
        True,
        back_source[bricks:].reshape(2, moving * 16, 128),
        3,
    )
    up_octants = gather_back(
        back_source[:bricks], send_pick, rode_back.reshape(2 * moving, -1)
    ).reshape(bricks, half_channels, 64)
    mixed_feats = ((feats.astype(jnp.float32) + enlarge(up_octants)) * live_mask).astype(
        jnp.bfloat16
    )
    up_grad = pool_sum(back_feats).astype(jnp.bfloat16).reshape(bricks, -1)
    outgoing_grad = select_rows(send_pick, up_grad)
    incoming_grad, feat_fields, both_grad = trade(
        outgoing_grad.reshape(2, moving * 16, 128),
        mixed_feats,
        [up_grad.reshape(bricks * 16, 128)],
        4,
    )
    coarse_grad = place_octants(
        select_both(receive_pick, both_grad, incoming_grad.reshape(2, 2 * moving, 2048))
    )
    hidden_half = hidden.shape[1] // 2
    own_hidden = lax.dynamic_slice_in_dim(hidden, core * hidden_half, hidden_half, 1)
    project_matrix = jnp.einsum(
        "bcv,bjv->cj", coarse_grad, own_hidden, preferred_element_type=jnp.float32
    )
    hidden_grad = jnp.einsum(
        "cj,bcv->bjv", whole_project, coarse_grad, preferred_element_type=jnp.float32
    )
    sigmoid_pre = jax.nn.sigmoid(preactivation)
    pre_grad = (hidden_grad * sigmoid_pre * (1.0 + preactivation * (1.0 - sigmoid_pre))).astype(
        jnp.bfloat16
    )
    own_pre_grad = lax.dynamic_slice_in_dim(pre_grad, core * hidden_half, hidden_half, 1)
    coarse_total = brick_pass(
        coarse_in, lone, live_count, None, own_pre_grad, None, False
    )[0]
    own_coarse = flip_weight(
        lax.dynamic_slice_in_dim(whole_coarse, core * half_channels, half_channels, 2)
    )
    coarse_terms = brick_pass(
        pre_grad.reshape(2 * coarse_bricks, hidden_half, 512),
        lone_bricks(2 * coarse_bricks),
        live_count,
        jnp.stack([own_coarse[:, :, :hidden_half], own_coarse[:, :, hidden_half:]]),
        None,
        jnp.float32,
        False,
    )[0]
    coarse_back = (
        coarse_terms.reshape(coarse_bricks, 2, half_channels, 512).sum(1).astype(jnp.bfloat16)
    )
    down_source = select_rows(receive_pick.T, split_octants(coarse_back).reshape(bricks, -1))
    fine_scale = 1.0 / math.sqrt(512.0 * bricks * devices)
    coarse_scale = 1.0 / math.sqrt(512.0 * coarse_bricks * devices)
    out_feats, fine_weight_grad, coarse_weight_grad, project_tiles, rode_down = brick_pass(
        feat_fields,
        near,
        live_count,
        fine_weight[None],
        grad_rows,
        jnp.bfloat16,
        True,
        down_source[bricks:].reshape(2, moving * 16, 128),
        5,
        wide_pieces(coarse_total, project_matrix),
        (fine_scale, coarse_scale),
    )
    down_grad = gather_back(
        down_source[:bricks], send_pick, rode_down.reshape(2 * moving, -1)
    ).reshape(bricks, half_channels, 64)
    grad_feats = (back_feats.astype(jnp.float32) + live_mask * enlarge(down_grad) * 0.125).astype(
        jnp.bfloat16
    )
    project_weight_grad = project_tiles.reshape(project_matrix.shape)
    return (out_feats, grad_feats, fine_weight_grad, coarse_weight_grad, project_weight_grad)


def solution(mesh):
    placed = (
        P("space", "chan", None),
        P("space"),
        P("space", None),
        P("space"),
        P(None, "chan", None),
        P(None, "chan", None),
        P(None, "chan"),
        P("space", "chan", None),
    )
    return jax.shard_map(
        per_device,
        mesh=mesh,
        in_specs=placed,
        out_specs=(
            P("space", "chan", None),
            P("space", "chan", None),
            P(None, "chan", None),
            P(None, "chan", None),
            P(None, "chan"),
        ),
        check_vma=False,
    )
```

```python
import math

import jax
import jax.numpy as jnp
import numpy as np
from jax import lax
from jax.experimental import pallas as pl
from jax.experimental.pallas import tpu as pltpu
from jax.sharding import PartitionSpec as P


def lean_list():
    leans = []
    for lean_x in (-1, 0, 1):
        for lean_y in (-1, 0, 1):
            for lean_z in (-1, 0, 1):
                leans.append((lean_x, lean_y, lean_z))
    return leans


def pool_table():
    voxel = np.arange(512)
    octant_voxel = 16 * (voxel // 128) + 4 * (voxel // 16 % 4) + voxel % 8 // 2
    return (octant_voxel[:, None] == np.arange(64)[None, :]).astype(np.float32)


def octant_table():
    voxel = np.arange(512)
    coord_x = voxel // 64
    coord_y = voxel // 8 % 8
    coord_z = voxel % 8
    octant = 4 * (coord_x // 4) + 2 * (coord_y // 4) + coord_z // 4
    inner = 16 * (coord_x % 4) + 4 * (coord_y % 4) + coord_z % 4
    table = np.zeros((8, 64, 512), np.float32)
    table[octant, inner, voxel] = 1.0
    return table


def flip_weight(weight):
    return jnp.transpose(weight[::-1], (0, 2, 1))


def pool_sum(field_in):
    table = jnp.asarray(pool_table()).astype(jnp.bfloat16)
    return jnp.einsum("bcv,vu->bcu", field_in, table, preferred_element_type=jnp.float32)


def enlarge(octants):
    table = jnp.asarray(pool_table()).astype(jnp.bfloat16)
    return jnp.einsum("bcu,vu->bcv", octants, table, preferred_element_type=jnp.float32)


def place_octants(octants):
    amount, channels = (octants.shape[0] // 8, octants.shape[1])
    grouped = octants.reshape(amount, 8, channels, 64)
    table = jnp.asarray(octant_table()).astype(jnp.bfloat16)
    return jnp.einsum("jocu,ouv->jcv", grouped, table, preferred_element_type=jnp.float32).astype(
        jnp.bfloat16
    )


def split_octants(coarse):
    amount, channels = (coarse.shape[0], coarse.shape[1])
    table = jnp.asarray(octant_table()).astype(jnp.bfloat16)
    parts = jnp.einsum("jcv,ouv->jocu", coarse, table, preferred_element_type=jnp.float32).astype(
        jnp.bfloat16
    )
    return parts.reshape(amount * 8, channels, 64)


def select_rows(picker, values):
    return jnp.dot(picker, values, preferred_element_type=jnp.float32).astype(jnp.bfloat16)


def route_places(slot_list, dev_index, moving, bricks):
    direction = slot_list // bricks - dev_index
    to_left = (direction == -1).astype(jnp.int32)
    to_right = (direction == 1).astype(jnp.int32)
    left_rank = jnp.cumsum(to_left) - to_left
    right_rank = jnp.cumsum(to_right) - to_right
    return jnp.where(
        to_left == 1, left_rank, jnp.where(to_right == 1, moving + right_rank, 2 * moving)
    ).astype(jnp.int32)


def lone_bricks(amount):
    centre = jnp.arange(27, dtype=jnp.int32)[None, :] == 13
    return jnp.where(centre, jnp.arange(amount, dtype=jnp.int32)[:, None], amount)


def select_both(picker, body, moved):
    values = jnp.concatenate([body.reshape(2, -1, 2048), moved], axis=1)
    picked = jnp.einsum("rs,csv->rcv", picker, values, preferred_element_type=jnp.float32)
    return picked.astype(jnp.bfloat16).reshape(picker.shape[0], -1, 64)


def gather_back(local_part, send_pick, returned):
    total = local_part.astype(jnp.float32) + jnp.dot(
        send_pick.T, returned, preferred_element_type=jnp.float32
    )
    return total.astype(jnp.bfloat16)


SPANS = {-1: (slice(0, 1), slice(7, 8)), 0: (slice(1, 9), slice(0, 8)), 1: (slice(9, 10), slice(0, 1))}
TAP_ORDER = np.array([1, 0, 2, 5, 4, 3, 7, 6, 8])
WIDTH = 640


def greet(devices):
    barrier = pltpu.get_barrier_semaphore()
    for device in devices:
        pl.semaphore_signal(
            barrier, inc=1, device_id=device, device_id_type=pl.DeviceIdType.MESH
        )
    pl.semaphore_wait(barrier, len(devices))


def nearby(count):
    me, core = lax.axis_index("space"), lax.axis_index("chan")
    return ((me + count - 1) % count, core), ((me + 1) % count, core), (me, 1 - core)


def sender(send_sems, recv_sems):
    def send(number, source, target, device):
        copy = pltpu.make_async_remote_copy(
            src_ref=source,
            dst_ref=target,
            send_sem=send_sems.at[number],
            recv_sem=recv_sems.at[number],
            device_id=device,
            device_id_type=pl.DeviceIdType.MESH,
        )
        copy.start()
        return copy

    return send


def trade_kernel(count, amount, *refs):
    rows, own = refs[:2]
    shares = refs[2 : 2 + amount]
    rows_all, fields = refs[2 + amount : 4 + amount]
    shares_all = refs[4 + amount : 4 + 2 * amount]
    send_sems, recv_sems, keep_sems = refs[4 + 2 * amount :]
    core = lax.axis_index("chan")
    left, right, mate = nearby(count)
    left_mate, right_mate = (left[0], 1 - core), (right[0], 1 - core)
    greet((left, right, mate, left_mate, right_mate))
    send = sender(send_sems, recv_sems)
    quick = [
        send(0, rows.at[0], rows_all.at[core, 1], left),
        send(1, rows.at[1], rows_all.at[core, 0], right),
        send(2, rows.at[0], rows_all.at[core, 1], left_mate),
        send(3, rows.at[1], rows_all.at[core, 0], right_mate),
    ]
    to_right = send(4, own, fields.at[core, 0], right)
    to_left = send(5, own, fields.at[core, 2], left)
    kept = []
    for number, (share, share_all) in enumerate(zip(shares, shares_all)):
        if len(share.shape) == 3:
            half = share.shape[1]
            spot = share_all.at[:, pl.ds(pl.multiple_of(core * half, half), half)]
        else:
            spot = share_all.at[core]
        quick.append(send(8 + number, share, spot, mate))
        kept.append(pltpu.make_async_copy(share, spot, keep_sems.at[1 + number]))
    quick.append(send(8 + amount, own, fields.at[core, 1], mate))
    kept.append(pltpu.make_async_copy(own, fields.at[core, 1], keep_sems.at[0]))
    for copy in kept:
        copy.start()
    to_right.wait_recv()
    quick.append(send(6, fields.at[core, 0], fields.at[core, 0], mate))
    to_left.wait_recv()
    quick.append(send(7, fields.at[core, 2], fields.at[core, 2], mate))
    for copy in quick:
        copy.wait_recv()
    for copy in quick + [to_right, to_left]:
        copy.wait_send()
    for copy in kept:
        copy.wait()


def trade(rows, own, shares, number):
    count = lax.axis_size("space")
    amount = len(shares)
    shapes = [(2,) + rows.shape, (2, 3) + own.shape]
    for share in shares:
        if share.ndim == 3:
            shapes.append((share.shape[0], 2 * share.shape[1], share.shape[2]))
        else:
            shapes.append((2,) + share.shape)
    return pl.pallas_call(
        lambda *refs: trade_kernel(count, amount, *refs),
        in_specs=[pl.BlockSpec(memory_space=pltpu.VMEM)] * 2
        + [pl.BlockSpec(memory_space=pltpu.HBM if share.ndim == 3 else pltpu.VMEM) for share in shares],
        out_specs=[
            pl.BlockSpec(memory_space=pltpu.HBM if len(shape) in (3, 5) and place else pltpu.VMEM)
            for place, shape in enumerate(shapes)
        ],
        out_shape=[jax.ShapeDtypeStruct(shape, rows.dtype) for shape in shapes],
        scratch_shapes=[
            pltpu.SemaphoreType.DMA((9 + amount,)),
            pltpu.SemaphoreType.DMA((9 + amount,)),
            pltpu.SemaphoreType.DMA((1 + amount,)),
        ],
        compiler_params=pltpu.CompilerParams(
            collective_id=number, has_side_effects=True, vmem_limit_bytes=12 * 1024 * 1024
        ),
    )(rows, own, *shares)


def ride_copies(count, refs):
    return [
        pltpu.make_async_remote_copy(
            src_ref=refs["ride"].at[side],
            dst_ref=refs["ride_in"].at[1 - side],
            send_sem=refs["ride_send"].at[side],
            recv_sem=refs["ride_recv"].at[side],
            device_id=device,
            device_id_type=pl.DeviceIdType.MESH,
        )
        for side, device in enumerate(nearby(count)[:2])
    ]


def hail(devices):
    barrier = pltpu.get_barrier_semaphore()
    for device in devices:
        pl.semaphore_signal(
            barrier, inc=1, device_id=device, device_id_type=pl.DeviceIdType.MESH
        )


def torus_sizes(count):
    return (16, 8) if count == 128 else (1, count)


class TorusSum:
    def __init__(self, count, refs, label):
        self.plane, self.depth = torus_sizes(count)
        me, self.core = lax.axis_index("space"), lax.axis_index("chan")
        self.at, self.level = me // self.depth, me % self.depth
        self.refs = {name: refs[label + name] for name in SUM_NAMES}

    def across(self, step):
        return (self.at + step) % self.plane * self.depth + self.level, self.core

    def along(self, step):
        return self.at * self.depth + (self.level + step) % self.depth, self.core

    def peers(self):
        return [self.across(step) for step in range(1, self.plane)] + [
            self.along(step) for step in range(1, self.depth)
        ]

    def copies(self, phase):
        refs = self.refs
        made = []
        for step in range(1, self.depth if phase == 1 else self.plane):
            if phase == 0:
                source = refs["data"].at[(self.at + step) % self.plane]
                target = refs["part"].at[step - 1]
            elif phase == 1:
                source = target = refs["levels"].at[self.level]
            else:
                source = target = refs["total"].at[self.at]
            made.append(
                pltpu.make_async_remote_copy(
                    src_ref=source,
                    dst_ref=target,
                    send_sem=refs["send"].at[phase, step - 1],
                    recv_sem=refs["recv"].at[phase, step - 1],
                    device_id=self.along(step) if phase == 1 else self.across(step),
                    device_id_type=pl.DeviceIdType.MESH,
                )
            )
        return made

    def start(self, phase):
        refs = self.refs
        if phase == 1:
            value = refs["data"][self.at]
            for step in range(1, self.plane):
                value = value + refs["part"][step - 1]
            refs["levels"][self.level] = value
        elif phase == 2:
            value = refs["levels"][0]
            for level in range(1, self.depth):
                value = value + refs["levels"][level]
            refs["total"][self.at] = value
        for copy in self.copies(phase):
            copy.start()

    def wait(self, phase):
        for copy in self.copies(phase):
            copy.wait_recv()

    def leave(self):
        for phase in range(3):
            for copy in self.copies(phase):
                copy.wait_send()


SUM_NAMES = ("data", "part", "levels", "total", "send", "recv")


def sum_scratch(count, rows, label, with_data):
    plane, depth = torus_sizes(count)
    piece = (128 // plane, rows, 128)
    firsts = {"part": max(1, plane - 1), "levels": depth, "total": plane}
    if with_data:
        firsts["data"] = plane
    scratch = {
        label + name: pltpu.VMEM((first,) + piece, jnp.float32) for name, first in firsts.items()
    }
    most = max(plane, depth) - 1
    scratch[label + "send"] = pltpu.SemaphoreType.DMA((3, most))
    scratch[label + "recv"] = pltpu.SemaphoreType.DMA((3, most))
    return scratch, (plane,) + piece


def fine_pieces(acc):
    pieces = []
    for tap_x in range(3):
        for block in range(acc.shape[1] // 4):
            for lane in range(WIDTH // 128):
                pieces.append((tap_x, slice(4 * block, 4 * block + 4), slice(128 * lane, 128 * lane + 128)))
    return pieces


def brick_kernel(count, masked, scales, parts, names, *refs):
    refs = dict(zip(names, refs))
    field_ref, table, padded, columns = [
        refs[name] for name in ("field", "table", "padded", "columns")
    ]
    brick = pl.program_id(0)
    last = pl.num_programs(0) - 1
    sums = "wide_data" in refs
    if sums:
        wide = TorusSum(count, refs, "wide_")
        slim = TorusSum(count, refs, "slim_")

    @pl.when(brick == 0)
    def fill():
        if count:
            fetch = pltpu.make_async_copy(refs["far_field"], field_ref, refs["field_sem"])
            fetch.start()
            greeted = list(nearby(count)[:2]) + (wide.peers() if sums else [])
            hail(greeted)
        slots = table.shape[0] - 1
        table[slots] = jnp.zeros((8, 8, 8, 128), jnp.float32)
        halves = len(field_ref.shape) == 5
        amount = field_ref.shape[2]

        def turn(slot, carry):
            if halves:
                place, one = slot // amount, slot % amount
                field = jnp.concatenate(
                    [field_ref[0, place, one], field_ref[1, place, one]], axis=0
                ).astype(jnp.float32)
            else:
                field = field_ref[slot].astype(jnp.float32)
            turned = jnp.concatenate([field, field], axis=0).T
            table[slot] = turned.reshape(8, 8, 8, 128)
            return carry

        if count:
            fetch.wait()
        lax.fori_loop(0, slots, turn, 0)
        if "acc" in refs:
            refs["acc"][...] = jnp.zeros_like(refs["acc"])

    if count:

        @pl.when(brick == 2)
        def depart():
            met = 2 + (len(wide.peers()) if sums else 0)
            pl.semaphore_wait(pltpu.get_barrier_semaphore(), met)
            for copy in ride_copies(count, refs):
                copy.start()
            if sums:
                wide.start(0)

    if sums:

        @pl.when(brick == last - 1)
        def second():
            wide.wait(0)
            wide.start(1)

    for index, (lean_x, lean_y, lean_z) in enumerate(lean_list()):
        slot = refs["near"][brick, index]
        to_x, from_x = SPANS[lean_x]
        to_y, from_y = SPANS[lean_y]
        padded[lean_z + 1, to_x, to_y] = table[slot, from_x, from_y]
    shape = (10, 8, 8, 128)
    place_z = lax.broadcasted_iota(jnp.int32, shape, 2)
    low_half = lax.broadcasted_iota(jnp.int32, shape, 3) < 64

    def put(position, low, high):
        both = jnp.where(low_half, low, high).reshape(640, 128)
        columns[:, 128 * position : 128 * position + 128] = both.astype(jnp.bfloat16)

    ahead = []
    for tap_y, position in enumerate((0, 2, 3)):
        below = padded[0, :, tap_y : tap_y + 8]
        level = padded[1, :, tap_y : tap_y + 8]
        above = padded[2, :, tap_y : tap_y + 8]
        minus = pltpu.roll(jnp.where(place_z == 7, below, level), 1, 2)
        put(position, level, minus)
        ahead.append(pltpu.roll(jnp.where(place_z == 0, above, level), 7, 2))
        if tap_y == 1:
            put(1, ahead[0], ahead[1])
    put(4, ahead[2], 0.0)
    if "weight" in refs:
        weight, blocks = refs["weight"], refs["blocks"]

        @pl.when(jnp.logical_or(brick == 0, parts > 1))
        def order_taps():
            zeros = jnp.zeros(weight.shape[2:], weight.dtype)
            for tap_x in range(3):
                taps = [weight[0, 9 * tap_x + int(tap)] for tap in TAP_ORDER] + [zeros]
                for pair in range(WIDTH // 128):
                    blocks[tap_x, :, 128 * pair : 128 * pair + 128] = jnp.concatenate(
                        taps[2 * pair : 2 * pair + 2], axis=1
                    )

        total = None
        for tap_x in range(3):
            part = lax.dot_general(
                blocks[tap_x],
                columns[64 * tap_x : 64 * tap_x + 512, :],
                (((1,), (1,)), ((), ())),
                preferred_element_type=jnp.float32,
            )
            total = part if total is None else total + part
        if masked:
            total = jnp.where(brick < refs["live"][0], total, 0.0)
        refs["out"][0] = total.astype(refs["out"].dtype)
    if "grad" in refs:
        for tap_x in range(3):
            refs["acc"][tap_x] += jnp.dot(
                refs["grad"][0],
                columns[64 * tap_x : 64 * tap_x + 512, :],
                preferred_element_type=jnp.float32,
            )

    @pl.when(brick == last)
    def close():
        if sums:
            acc, data = refs["acc"], refs["slim_data"]
            cells = list(np.ndindex(data.shape[:2]))
            spans = fine_pieces(acc)
            for cell, span in zip(cells, spans):
                data[cell] = acc[span]
            for cell in cells[len(spans) :]:
                data[cell] = jnp.zeros(data.shape[2:], jnp.float32)
            slim.start(0)
            wide.wait(1)
            wide.start(2)
            slim.wait(0)
            slim.start(1)
            wide.wait(2)
            unpack(refs["wide_total"], refs["coarse_out"], scales[1])
            used = 3 * refs["coarse_out"].shape[1] // 8 * (WIDTH // 128)
            plain = refs["wide_total"]
            for tile in range(refs["project_out"].shape[0]):
                at = divmod(used + tile, plain.shape[1])
                refs["project_out"][tile] = plain[at] * scales[1]
            slim.wait(1)
            slim.start(2)
            slim.wait(2)
            unpack(refs["slim_total"], refs["fine_out"], scales[0])
            wide.leave()
            slim.leave()
        elif "acc" in refs:
            refs["total"][...] = refs["acc"][...]
        if count:
            for copy in ride_copies(count, refs):
                copy.wait()
            refs["ride_out"][...] = refs["ride_in"][...]


def brick_pass(
    field_in, near, live_count, weight, grad_rows, out_dtype, masked, ride=None, number=None,
    wide=None, scales=None,
):
    amount = near.shape[0]
    count = 0 if ride is None else lax.axis_size("space")
    slots = 3 * field_in.shape[2] if field_in.ndim == 5 else field_in.shape[0]
    rows = weight.shape[2] if weight is not None else grad_rows.shape[1]
    ins, outs, scratch = {}, {}, {}
    parts = 1

    def whole(shape):
        return pl.BlockSpec(shape, lambda b: (0,) * len(shape))

    def result(name, shape, dtype, spec=None):
        outs[name] = (jax.ShapeDtypeStruct(shape, dtype), spec or whole(shape))

    ins["near"] = (near, pl.BlockSpec(memory_space=pltpu.SMEM))
    ins["live"] = (live_count, pl.BlockSpec(memory_space=pltpu.SMEM))
    if count:
        ins["far_field"] = (field_in, pl.BlockSpec(memory_space=pltpu.HBM))
        scratch["field"] = pltpu.VMEM(field_in.shape, field_in.dtype)
        scratch["field_sem"] = pltpu.SemaphoreType.DMA
    else:
        ins["field"] = (field_in, whole(field_in.shape))
    scratch["table"] = pltpu.VMEM((slots + 1, 8, 8, 8, 128), jnp.float32)
    scratch["padded"] = pltpu.VMEM((3, 10, 10, 8, 128), jnp.float32)
    scratch["columns"] = pltpu.VMEM((640, WIDTH), jnp.bfloat16)
    by_brick = pl.BlockSpec((1, rows, 512), lambda b: (b, 0, 0))
    if weight is not None:
        parts = weight.shape[0]
        ins["weight"] = (
            weight, pl.BlockSpec((1, 27, rows, 64), lambda b: (b % parts, 0, 0, 0))
        )
        scratch["blocks"] = pltpu.VMEM((3, rows, WIDTH), weight.dtype)
        result("out", (amount, rows, 512), out_dtype, by_brick)
    if grad_rows is not None:
        ins["grad"] = (grad_rows, by_brick)
        scratch["acc"] = pltpu.VMEM((3, rows, WIDTH), jnp.float32)
        if wide is None:
            result("total", (3, rows, WIDTH), jnp.float32)
    if wide is not None:
        wide_scratch, wide_shape = sum_scratch(count, 8, "wide_", False)
        slim_scratch, slim_shape = sum_scratch(count, 4, "slim_", True)
        scratch.update(wide_scratch)
        scratch.update(slim_scratch)
        ins["wide_data"] = (wide.reshape(wide_shape), whole(wide_shape))
        result("fine_out", (27, rows, 64), jnp.float32)
        result("coarse_out", (27, 64, 64), jnp.float32)
        result("project_out", (4, 8, 128), jnp.float32)
    if count:
        ins["ride"] = (ride, whole(ride.shape))
        result("ride_out", ride.shape, ride.dtype)
        scratch["ride_in"] = pltpu.VMEM(ride.shape, ride.dtype)
        scratch["ride_send"] = pltpu.SemaphoreType.DMA((2,))
        scratch["ride_recv"] = pltpu.SemaphoreType.DMA((2,))
    names = list(ins) + list(outs) + list(scratch)
    remote = {"collective_id": number, "has_side_effects": True} if count else {}
    room = 12 if slots < 8 else 20 if wide is None else 30
    products = (weight is not None) + (grad_rows is not None)
    return pl.pallas_call(
        lambda *refs: brick_kernel(count, masked, scales, parts, names, *refs),
        grid=(amount,),
        in_specs=[spec for _, spec in ins.values()],
        out_specs=[spec for _, spec in outs.values()],
        out_shape=[shape for shape, _ in outs.values()],
        scratch_shapes=list(scratch.values()),
        compiler_params=pltpu.CompilerParams(vmem_limit_bytes=room * 1024 * 1024, **remote),
        cost_estimate=pl.CostEstimate(
            flops=amount * products * 2 * rows * 3 * WIDTH * 512,
            bytes_accessed=slots * 64 * 512 * 2,
            transcendentals=0,
        ),
    )(*[value for value, _ in ins.values()])


def unpack(total, out, scale):
    high = total.shape[2]
    blocks = out.shape[1] // high
    for tap_x in range(3):
        for block in range(blocks):
            first = WIDTH // 128 * (tap_x * blocks + block)
            rows = slice(high * block, high * block + high)
            for place, tap in enumerate(TAP_ORDER):
                lanes = slice(64 * (place % 2), 64 * (place % 2) + 64)
                plane, piece = divmod(first + place // 2, total.shape[1])
                out[9 * tap_x + int(tap), rows, :] = total[plane, piece, :, lanes] * scale


def wide_pieces(coarse, project):
    tiles = jnp.transpose(coarse.reshape(-1, 8, WIDTH // 128, 128), (0, 2, 1, 3))
    tiles = tiles.reshape(-1, 8, 128)
    small = project.reshape(-1, 8, 128)
    spare = 128 - tiles.shape[0] - small.shape[0]
    return jnp.concatenate([tiles, small, jnp.zeros((spare, 8, 128), jnp.float32)], axis=0)


def per_device(
    feats, live_count, neighbours, parent, fine_weight, coarse_weight, project_weight, cotangent
):
    bricks = feats.shape[0]
    half_channels = feats.shape[1]
    devices = lax.axis_size("space")
    own_index = lax.axis_index("space")
    moving = max(1, bricks // 8)
    coarse_bricks = bricks // 8
    live_mask = (jnp.arange(bricks, dtype=jnp.int32) < live_count[0]).astype(jnp.float32)[
        :, None, None
    ]
    core = lax.axis_index("chan")
    send_place = route_places(parent, own_index, moving, bricks)
    send_pick = (jnp.arange(2 * moving, dtype=jnp.int32)[:, None] == send_place[None, :]).astype(
        jnp.bfloat16
    )
    pooled = (pool_sum(feats) * 0.125 * live_mask).astype(jnp.bfloat16).reshape(bricks, -1)
    slot_rows = jnp.broadcast_to(
        (parent % bricks + 1).astype(jnp.bfloat16)[:, None], (bricks, 2048)
    )
    outgoing = select_rows(send_pick, jnp.concatenate([pooled, slot_rows], axis=1))
    grad_rows = (cotangent.astype(jnp.float32) * live_mask).astype(jnp.bfloat16)
    incoming, grad_fields, both_pooled, whole_coarse, whole_fine, both_project = trade(
        outgoing.reshape(2, moving * 32, 128),
        grad_rows,
        [pooled.reshape(bricks * 16, 128), coarse_weight, fine_weight, project_weight],
        2,
    )
    whole_project = jnp.concatenate([both_project[0], both_project[1]], axis=1)
    incoming = incoming.reshape(2, 2 * moving, 4096)
    incoming_slots = incoming[0, :, -1].astype(jnp.int32) - 1
    local_slots = jnp.where(parent // bricks == own_index, parent % bricks, -1)
    all_slots = jnp.concatenate([local_slots, incoming_slots])
    receive_pick = (jnp.arange(bricks, dtype=jnp.int32)[:, None] == all_slots[None, :]).astype(
        jnp.bfloat16
    )
    arrived = select_both(receive_pick, both_pooled, incoming[:, :, :2048])
    coarse_in = place_octants(arrived)
    lone = lone_bricks(coarse_bricks)
    preactivation = brick_pass(
        coarse_in, lone, live_count, whole_coarse[None], None, jnp.float32, False
    )[0]
    hidden = jax.nn.silu(preactivation).astype(jnp.bfloat16)
    own_project = lax.dynamic_slice_in_dim(
        whole_project, core * half_channels, half_channels, 0
    )
    coarse_out = jnp.einsum(
        "cj,bjv->bcv", own_project, hidden, preferred_element_type=jnp.float32
    ).astype(jnp.bfloat16)
    back_source = select_rows(receive_pick.T, split_octants(coarse_out).reshape(bricks, -1))
    last_brick = devices * bricks
    near_local = jnp.where(
        neighbours >= last_brick, 3 * bricks, neighbours - (own_index - 1) * bricks
    ).astype(jnp.int32)
    slots = jnp.arange(bricks, dtype=jnp.int32)[:, None] + bricks
    near = jnp.concatenate([near_local[:, :13], slots, near_local[:, 13:]], axis=1)
    own_weight = lax.dynamic_slice_in_dim(whole_fine, core * half_channels, half_channels, 2)
    back_feats, rode_back = brick_pass(
        grad_fields,
        near,
        live_count,
        flip_weight(own_weight)[None],
        None,
        jnp.bfloat16,
        True,
        back_source[bricks:].reshape(2, moving * 16, 128),
        3,
    )
    up_octants = gather_back(
        back_source[:bricks], send_pick, rode_back.reshape(2 * moving, -1)
    ).reshape(bricks, half_channels, 64)
    mixed_feats = ((feats.astype(jnp.float32) + enlarge(up_octants)) * live_mask).astype(
        jnp.bfloat16
    )
    up_grad = pool_sum(back_feats).astype(jnp.bfloat16).reshape(bricks, -1)
    outgoing_grad = select_rows(send_pick, up_grad)
    incoming_grad, feat_fields, both_grad = trade(
        outgoing_grad.reshape(2, moving * 16, 128),
        mixed_feats,
        [up_grad.reshape(bricks * 16, 128)],
        4,
    )
    coarse_grad = place_octants(
        select_both(receive_pick, both_grad, incoming_grad.reshape(2, 2 * moving, 2048))
    )
    hidden_half = hidden.shape[1] // 2
    own_hidden = lax.dynamic_slice_in_dim(hidden, core * hidden_half, hidden_half, 1)
    project_matrix = jnp.einsum(
        "bcv,bjv->cj", coarse_grad, own_hidden, preferred_element_type=jnp.float32
    )
    hidden_grad = jnp.einsum(
        "cj,bcv->bjv", whole_project, coarse_grad, preferred_element_type=jnp.float32
    )
    sigmoid_pre = jax.nn.sigmoid(preactivation)
    pre_grad = (hidden_grad * sigmoid_pre * (1.0 + preactivation * (1.0 - sigmoid_pre))).astype(
        jnp.bfloat16
    )
    own_pre_grad = lax.dynamic_slice_in_dim(pre_grad, core * hidden_half, hidden_half, 1)
    coarse_total = brick_pass(
        coarse_in, lone, live_count, None, own_pre_grad, None, False
    )[0]
    own_coarse = flip_weight(
        lax.dynamic_slice_in_dim(whole_coarse, core * half_channels, half_channels, 2)
    )
    coarse_terms = brick_pass(
        pre_grad.reshape(2 * coarse_bricks, hidden_half, 512),
        lone_bricks(2 * coarse_bricks),
        live_count,
        jnp.stack([own_coarse[:, :, :hidden_half], own_coarse[:, :, hidden_half:]]),
        None,
        jnp.float32,
        False,
    )[0]
    coarse_back = (
        coarse_terms.reshape(coarse_bricks, 2, half_channels, 512).sum(1).astype(jnp.bfloat16)
    )
    down_source = select_rows(receive_pick.T, split_octants(coarse_back).reshape(bricks, -1))
    fine_scale = 1.0 / math.sqrt(512.0 * bricks * devices)
    coarse_scale = 1.0 / math.sqrt(512.0 * coarse_bricks * devices)
    out_feats, fine_weight_grad, coarse_weight_grad, project_tiles, rode_down = brick_pass(
        feat_fields,
        near,
        live_count,
        fine_weight[None],
        grad_rows,
        jnp.bfloat16,
        True,
        down_source[bricks:].reshape(2, moving * 16, 128),
        5,
        wide_pieces(coarse_total, project_matrix),
        (fine_scale, coarse_scale),
    )
    down_grad = gather_back(
        down_source[:bricks], send_pick, rode_down.reshape(2 * moving, -1)
    ).reshape(bricks, half_channels, 64)
    grad_feats = (back_feats.astype(jnp.float32) + live_mask * enlarge(down_grad) * 0.125).astype(
        jnp.bfloat16
    )
    project_weight_grad = project_tiles.reshape(project_matrix.shape)
    return (out_feats, grad_feats, fine_weight_grad, coarse_weight_grad, project_weight_grad)


def solution(mesh):
    placed = (
        P("space", "chan", None),
        P("space"),
        P("space", None),
        P("space"),
        P(None, "chan", None),
        P(None, "chan", None),
        P(None, "chan"),
        P("space", "chan", None),
    )
    return jax.shard_map(
        per_device,
        mesh=mesh,
        in_specs=placed,
        out_specs=(
            P("space", "chan", None),
            P("space", "chan", None),
            P(None, "chan", None),
            P(None, "chan", None),
            P(None, "chan"),
        ),
        check_vma=False,
    )
```

```python
import math

import jax
import jax.numpy as jnp
import numpy as np
from jax import lax
from jax.experimental import pallas as pl
from jax.experimental.pallas import tpu as pltpu
from jax.sharding import PartitionSpec as P


def lean_list():
    leans = []
    for lean_x in (-1, 0, 1):
        for lean_y in (-1, 0, 1):
            for lean_z in (-1, 0, 1):
                leans.append((lean_x, lean_y, lean_z))
    return leans


def pool_table():
    voxel = np.arange(512)
    octant_voxel = 16 * (voxel // 128) + 4 * (voxel // 16 % 4) + voxel % 8 // 2
    return (octant_voxel[:, None] == np.arange(64)[None, :]).astype(np.float32)


def octant_table():
    voxel = np.arange(512)
    coord_x = voxel // 64
    coord_y = voxel // 8 % 8
    coord_z = voxel % 8
    octant = 4 * (coord_x // 4) + 2 * (coord_y // 4) + coord_z // 4
    inner = 16 * (coord_x % 4) + 4 * (coord_y % 4) + coord_z % 4
    table = np.zeros((8, 64, 512), np.float32)
    table[octant, inner, voxel] = 1.0
    return table


def flip_weight(weight):
    return jnp.transpose(weight[::-1], (0, 2, 1))


def pool_sum(field_in):
    table = jnp.asarray(pool_table()).astype(jnp.bfloat16)
    return jnp.einsum("bcv,vu->bcu", field_in, table, preferred_element_type=jnp.float32)


def enlarge(octants):
    table = jnp.asarray(pool_table()).astype(jnp.bfloat16)
    return jnp.einsum("bcu,vu->bcv", octants, table, preferred_element_type=jnp.float32)


def place_octants(octants):
    amount, channels = (octants.shape[0] // 8, octants.shape[1])
    grouped = octants.reshape(amount, 8, channels, 64)
    table = jnp.asarray(octant_table()).astype(jnp.bfloat16)
    return jnp.einsum("jocu,ouv->jcv", grouped, table, preferred_element_type=jnp.float32).astype(
        jnp.bfloat16
    )


def split_octants(coarse):
    amount, channels = (coarse.shape[0], coarse.shape[1])
    table = jnp.asarray(octant_table()).astype(jnp.bfloat16)
    parts = jnp.einsum("jcv,ouv->jocu", coarse, table, preferred_element_type=jnp.float32).astype(
        jnp.bfloat16
    )
    return parts.reshape(amount * 8, channels, 64)


def select_rows(picker, values):
    return jnp.dot(picker, values, preferred_element_type=jnp.float32).astype(jnp.bfloat16)


def route_places(slot_list, dev_index, moving, bricks):
    direction = slot_list // bricks - dev_index
    to_left = (direction == -1).astype(jnp.int32)
    to_right = (direction == 1).astype(jnp.int32)
    left_rank = jnp.cumsum(to_left) - to_left
    right_rank = jnp.cumsum(to_right) - to_right
    return jnp.where(
        to_left == 1, left_rank, jnp.where(to_right == 1, moving + right_rank, 2 * moving)
    ).astype(jnp.int32)


def lone_bricks(amount):
    centre = jnp.arange(27, dtype=jnp.int32)[None, :] == 13
    return jnp.where(centre, jnp.arange(amount, dtype=jnp.int32)[:, None], amount)


def select_both(picker, body, moved):
    values = jnp.concatenate([body.reshape(2, -1, 2048), moved], axis=1)
    picked = jnp.einsum("rs,csv->rcv", picker, values, preferred_element_type=jnp.float32)
    return picked.astype(jnp.bfloat16).reshape(picker.shape[0], -1, 64)


def gather_back(local_part, send_pick, returned):
    total = local_part.astype(jnp.float32) + jnp.dot(
        send_pick.T, returned, preferred_element_type=jnp.float32
    )
    return total.astype(jnp.bfloat16)


SPANS = {-1: (slice(0, 1), slice(7, 8)), 0: (slice(1, 9), slice(0, 8)), 1: (slice(9, 10), slice(0, 1))}
TAP_ORDER = np.array([1, 0, 2, 5, 4, 3, 7, 6, 8])
WIDTH = 640


def greet(devices):
    barrier = pltpu.get_barrier_semaphore()
    for device in devices:
        pl.semaphore_signal(
            barrier, inc=1, device_id=device, device_id_type=pl.DeviceIdType.MESH
        )
    pl.semaphore_wait(barrier, len(devices))


def nearby(count):
    me, core = lax.axis_index("space"), lax.axis_index("chan")
    return ((me + count - 1) % count, core), ((me + 1) % count, core), (me, 1 - core)


def sender(send_sems, recv_sems):
    def send(number, source, target, device):
        copy = pltpu.make_async_remote_copy(
            src_ref=source,
            dst_ref=target,
            send_sem=send_sems.at[number],
            recv_sem=recv_sems.at[number],
            device_id=device,
            device_id_type=pl.DeviceIdType.MESH,
        )
        copy.start()
        return copy

    return send


def trade_kernel(count, amount, *refs):
    rows, own = refs[:2]
    shares = refs[2 : 2 + amount]
    rows_all, fields = refs[2 + amount : 4 + amount]
    shares_all = refs[4 + amount : 4 + 2 * amount]
    send_sems, recv_sems, keep_sems = refs[4 + 2 * amount :]
    core = lax.axis_index("chan")
    left, right, mate = nearby(count)
    left_mate, right_mate = (left[0], 1 - core), (right[0], 1 - core)
    greet((left, right, mate, left_mate, right_mate))
    send = sender(send_sems, recv_sems)
    quick = [
        send(0, rows.at[0], rows_all.at[core, 1], left),
        send(1, rows.at[1], rows_all.at[core, 0], right),
        send(2, rows.at[0], rows_all.at[core, 1], left_mate),
        send(3, rows.at[1], rows_all.at[core, 0], right_mate),
    ]
    to_right = send(4, own, fields.at[core, 0], right)
    to_left = send(5, own, fields.at[core, 2], left)
    kept = []
    for number, (share, share_all) in enumerate(zip(shares, shares_all)):
        if len(share.shape) == 3:
            half = share.shape[1]
            spot = share_all.at[:, pl.ds(pl.multiple_of(core * half, half), half)]
        else:
            spot = share_all.at[core]
        quick.append(send(8 + number, share, spot, mate))
        kept.append(pltpu.make_async_copy(share, spot, keep_sems.at[1 + number]))
    quick.append(send(8 + amount, own, fields.at[core, 1], mate))
    kept.append(pltpu.make_async_copy(own, fields.at[core, 1], keep_sems.at[0]))
    for copy in kept:
        copy.start()
    to_right.wait_recv()
    quick.append(send(6, fields.at[core, 0], fields.at[core, 0], mate))
    to_left.wait_recv()
    quick.append(send(7, fields.at[core, 2], fields.at[core, 2], mate))
    for copy in quick:
        copy.wait_recv()
    for copy in quick + [to_right, to_left]:
        copy.wait_send()
    for copy in kept:
        copy.wait()


def trade(rows, own, shares, number):
    count = lax.axis_size("space")
    amount = len(shares)
    shapes = [(2,) + rows.shape, (2, 3) + own.shape]
    for share in shares:
        if share.ndim == 3:
            shapes.append((share.shape[0], 2 * share.shape[1], share.shape[2]))
        else:
            shapes.append((2,) + share.shape)
    return pl.pallas_call(
        lambda *refs: trade_kernel(count, amount, *refs),
        in_specs=[pl.BlockSpec(memory_space=pltpu.VMEM)] * 2
        + [pl.BlockSpec(memory_space=pltpu.HBM if share.ndim == 3 else pltpu.VMEM) for share in shares],
        out_specs=[
            pl.BlockSpec(memory_space=pltpu.HBM if len(shape) in (3, 5) and place else pltpu.VMEM)
            for place, shape in enumerate(shapes)
        ],
        out_shape=[jax.ShapeDtypeStruct(shape, rows.dtype) for shape in shapes],
        scratch_shapes=[
            pltpu.SemaphoreType.DMA((9 + amount,)),
            pltpu.SemaphoreType.DMA((9 + amount,)),
            pltpu.SemaphoreType.DMA((1 + amount,)),
        ],
        compiler_params=pltpu.CompilerParams(
            collective_id=number, has_side_effects=True, vmem_limit_bytes=12 * 1024 * 1024
        ),
    )(rows, own, *shares)


def ride_copies(count, refs):
    return [
        pltpu.make_async_remote_copy(
            src_ref=refs["ride"].at[side],
            dst_ref=refs["ride_in"].at[1 - side],
            send_sem=refs["ride_send"].at[side],
            recv_sem=refs["ride_recv"].at[side],
            device_id=device,
            device_id_type=pl.DeviceIdType.MESH,
        )
        for side, device in enumerate(nearby(count)[:2])
    ]


def hail(devices):
    barrier = pltpu.get_barrier_semaphore()
    for device in devices:
        pl.semaphore_signal(
            barrier, inc=1, device_id=device, device_id_type=pl.DeviceIdType.MESH
        )


def torus_sizes(count):
    return (16, 8) if count == 128 else (1, count)


class TorusSum:
    def __init__(self, count, refs, label):
        self.plane, self.depth = torus_sizes(count)
        me, self.core = lax.axis_index("space"), lax.axis_index("chan")
        self.at, self.level = me // self.depth, me % self.depth
        self.refs = {name: refs[label + name] for name in SUM_NAMES}

    def across(self, step):
        return (self.at + step) % self.plane * self.depth + self.level, self.core

    def along(self, step):
        return self.at * self.depth + (self.level + step) % self.depth, self.core

    def peers(self):
        return [self.across(step) for step in range(1, self.plane)] + [
            self.along(step) for step in range(1, self.depth)
        ]

    def copies(self, phase):
        refs = self.refs
        made = []
        for step in range(1, self.depth if phase == 1 else self.plane):
            if phase == 0:
                source = refs["data"].at[(self.at + step) % self.plane]
                target = refs["part"].at[step - 1]
            elif phase == 1:
                source = target = refs["levels"].at[self.level]
            else:
                source = target = refs["total"].at[self.at]
            made.append(
                pltpu.make_async_remote_copy(
                    src_ref=source,
                    dst_ref=target,
                    send_sem=refs["send"].at[phase, step - 1],
                    recv_sem=refs["recv"].at[phase, step - 1],
                    device_id=self.along(step) if phase == 1 else self.across(step),
                    device_id_type=pl.DeviceIdType.MESH,
                )
            )
        return made

    def start(self, phase):
        refs = self.refs
        if phase == 1:
            value = refs["data"][self.at]
            for step in range(1, self.plane):
                value = value + refs["part"][step - 1]
            refs["levels"][self.level] = value
        elif phase == 2:
            value = refs["levels"][0]
            for level in range(1, self.depth):
                value = value + refs["levels"][level]
            refs["total"][self.at] = value
        for copy in self.copies(phase):
            copy.start()

    def wait(self, phase):
        for copy in self.copies(phase):
            copy.wait_recv()

    def leave(self):
        for phase in range(3):
            for copy in self.copies(phase):
                copy.wait_send()


SUM_NAMES = ("data", "part", "levels", "total", "send", "recv")


def sum_scratch(count, rows, label, with_data):
    plane, depth = torus_sizes(count)
    piece = (128 // plane, rows, 128)
    firsts = {"part": max(1, plane - 1), "levels": depth, "total": plane}
    if with_data:
        firsts["data"] = plane
    scratch = {
        label + name: pltpu.VMEM((first,) + piece, jnp.float32) for name, first in firsts.items()
    }
    most = max(plane, depth) - 1
    scratch[label + "send"] = pltpu.SemaphoreType.DMA((3, most))
    scratch[label + "recv"] = pltpu.SemaphoreType.DMA((3, most))
    return scratch, (plane,) + piece


def fine_pieces(acc):
    pieces = []
    for tap_x in range(3):
        for block in range(acc.shape[1] // 4):
            for lane in range(WIDTH // 128):
                pieces.append((tap_x, slice(4 * block, 4 * block + 4), slice(128 * lane, 128 * lane + 128)))
    return pieces


def brick_kernel(count, masked, scales, parts, names, *refs):
    refs = dict(zip(names, refs))
    field_ref, table, padded, columns = [
        refs[name] for name in ("field", "table", "padded", "columns")
    ]
    brick = pl.program_id(0)
    last = pl.num_programs(0) - 1
    sums = "wide_data" in refs
    if sums:
        wide = TorusSum(count, refs, "wide_")
        slim = TorusSum(count, refs, "slim_")

    @pl.when(brick == 0)
    def fill():
        if count:
            fetch = pltpu.make_async_copy(refs["far_field"], field_ref, refs["field_sem"])
            fetch.start()
            greeted = list(nearby(count)[:2]) + (wide.peers() if sums else [])
            hail(greeted)
        slots = table.shape[0] - 1
        table[slots] = jnp.zeros((8, 8, 8, 128), jnp.float32)
        halves = len(field_ref.shape) == 5
        amount = field_ref.shape[2]

        def turn(slot, carry):
            if halves:
                place, one = slot // amount, slot % amount
                field = jnp.concatenate(
                    [field_ref[0, place, one], field_ref[1, place, one]], axis=0
                ).astype(jnp.float32)
            else:
                field = field_ref[slot].astype(jnp.float32)
            turned = jnp.concatenate([field, field], axis=0).T
            table[slot] = turned.reshape(8, 8, 8, 128)
            return carry

        if count:
            fetch.wait()
        stride = 3 if slots % 3 == 0 else 1

        def turn_some(group, carry):
            for offset in range(stride):
                turn(group * stride + offset, carry)
            return carry

        lax.fori_loop(0, slots // stride, turn_some, 0)
        if "acc" in refs:
            refs["acc"][...] = jnp.zeros_like(refs["acc"])

    if count:

        @pl.when(brick == 2)
        def depart():
            met = 2 + (len(wide.peers()) if sums else 0)
            pl.semaphore_wait(pltpu.get_barrier_semaphore(), met)
            for copy in ride_copies(count, refs):
                copy.start()
            if sums:
                wide.start(0)

    if sums:

        @pl.when(brick == last - 1)
        def second():
            wide.wait(0)
            wide.start(1)

    for index, (lean_x, lean_y, lean_z) in enumerate(lean_list()):
        slot = refs["near"][brick, index]
        to_x, from_x = SPANS[lean_x]
        to_y, from_y = SPANS[lean_y]
        padded[lean_z + 1, to_x, to_y] = table[slot, from_x, from_y]
    shape = (10, 8, 8, 128)
    place_z = lax.broadcasted_iota(jnp.int32, shape, 2)
    low_half = lax.broadcasted_iota(jnp.int32, shape, 3) < 64

    def put(position, low, high):
        both = jnp.where(low_half, low, high).reshape(640, 128)
        columns[:, 128 * position : 128 * position + 128] = both.astype(jnp.bfloat16)

    ahead = []
    for tap_y, position in enumerate((0, 2, 3)):
        below = padded[0, :, tap_y : tap_y + 8]
        level = padded[1, :, tap_y : tap_y + 8]
        above = padded[2, :, tap_y : tap_y + 8]
        minus = pltpu.roll(jnp.where(place_z == 7, below, level), 1, 2)
        put(position, level, minus)
        ahead.append(pltpu.roll(jnp.where(place_z == 0, above, level), 7, 2))
        if tap_y == 1:
            put(1, ahead[0], ahead[1])
    put(4, ahead[2], 0.0)
    if "weight" in refs:
        weight, blocks = refs["weight"], refs["blocks"]

        @pl.when(jnp.logical_or(brick == 0, parts > 1))
        def order_taps():
            zeros = jnp.zeros(weight.shape[2:], weight.dtype)
            for tap_x in range(3):
                taps = [weight[0, 9 * tap_x + int(tap)] for tap in TAP_ORDER] + [zeros]
                for pair in range(WIDTH // 128):
                    blocks[tap_x, :, 128 * pair : 128 * pair + 128] = jnp.concatenate(
                        taps[2 * pair : 2 * pair + 2], axis=1
                    )

        total = None
        for tap_x in range(3):
            part = lax.dot_general(
                blocks[tap_x],
                columns[64 * tap_x : 64 * tap_x + 512, :],
                (((1,), (1,)), ((), ())),
                preferred_element_type=jnp.float32,
            )
            total = part if total is None else total + part
        if masked:
            total = jnp.where(brick < refs["live"][0], total, 0.0)
        refs["out"][0] = total.astype(refs["out"].dtype)
    if "grad" in refs:
        for tap_x in range(3):
            refs["acc"][tap_x] += jnp.dot(
                refs["grad"][0],
                columns[64 * tap_x : 64 * tap_x + 512, :],
                preferred_element_type=jnp.float32,
            )

    @pl.when(brick == last)
    def close():
        if sums:
            acc, data = refs["acc"], refs["slim_data"]
            cells = list(np.ndindex(data.shape[:2]))
            spans = fine_pieces(acc)
            for cell, span in zip(cells, spans):
                data[cell] = acc[span]
            for cell in cells[len(spans) :]:
                data[cell] = jnp.zeros(data.shape[2:], jnp.float32)
            slim.start(0)
            wide.wait(1)
            wide.start(2)
            slim.wait(0)
            slim.start(1)
            wide.wait(2)
            unpack(refs["wide_total"], refs["coarse_out"], scales[1])
            used = 3 * refs["coarse_out"].shape[1] // 8 * (WIDTH // 128)
            plain = refs["wide_total"]
            for tile in range(refs["project_out"].shape[0]):
                at = divmod(used + tile, plain.shape[1])
                refs["project_out"][tile] = plain[at] * scales[1]
            slim.wait(1)
            slim.start(2)
            slim.wait(2)
            unpack(refs["slim_total"], refs["fine_out"], scales[0])
            wide.leave()
            slim.leave()
        elif "acc" in refs:
            refs["total"][...] = refs["acc"][...]
        if count:
            for copy in ride_copies(count, refs):
                copy.wait()
            refs["ride_out"][...] = refs["ride_in"][...]


def brick_pass(
    field_in, near, live_count, weight, grad_rows, out_dtype, masked, ride=None, number=None,
    wide=None, scales=None,
):
    amount = near.shape[0]
    count = 0 if ride is None else lax.axis_size("space")
    slots = 3 * field_in.shape[2] if field_in.ndim == 5 else field_in.shape[0]
    rows = weight.shape[2] if weight is not None else grad_rows.shape[1]
    ins, outs, scratch = {}, {}, {}
    parts = 1

    def whole(shape):
        return pl.BlockSpec(shape, lambda b: (0,) * len(shape))

    def result(name, shape, dtype, spec=None):
        outs[name] = (jax.ShapeDtypeStruct(shape, dtype), spec or whole(shape))

    ins["near"] = (near, pl.BlockSpec(memory_space=pltpu.SMEM))
    ins["live"] = (live_count, pl.BlockSpec(memory_space=pltpu.SMEM))
    if count:
        ins["far_field"] = (field_in, pl.BlockSpec(memory_space=pltpu.HBM))
        scratch["field"] = pltpu.VMEM(field_in.shape, field_in.dtype)
        scratch["field_sem"] = pltpu.SemaphoreType.DMA
    else:
        ins["field"] = (field_in, whole(field_in.shape))
    scratch["table"] = pltpu.VMEM((slots + 1, 8, 8, 8, 128), jnp.float32)
    scratch["padded"] = pltpu.VMEM((3, 10, 10, 8, 128), jnp.float32)
    scratch["columns"] = pltpu.VMEM((640, WIDTH), jnp.bfloat16)
    by_brick = pl.BlockSpec((1, rows, 512), lambda b: (b, 0, 0))
    if weight is not None:
        parts = weight.shape[0]
        ins["weight"] = (
            weight, pl.BlockSpec((1, 27, rows, 64), lambda b: (b % parts, 0, 0, 0))
        )
        scratch["blocks"] = pltpu.VMEM((3, rows, WIDTH), weight.dtype)
        result("out", (amount, rows, 512), out_dtype, by_brick)
    if grad_rows is not None:
        ins["grad"] = (grad_rows, by_brick)
        scratch["acc"] = pltpu.VMEM((3, rows, WIDTH), jnp.float32)
        if wide is None:
            result("total", (3, rows, WIDTH), jnp.float32)
    if wide is not None:
        wide_scratch, wide_shape = sum_scratch(count, 8, "wide_", False)
        slim_scratch, slim_shape = sum_scratch(count, 4, "slim_", True)
        scratch.update(wide_scratch)
        scratch.update(slim_scratch)
        ins["wide_data"] = (wide.reshape(wide_shape), whole(wide_shape))
        result("fine_out", (27, rows, 64), jnp.float32)
        result("coarse_out", (27, 64, 64), jnp.float32)
        result("project_out", (4, 8, 128), jnp.float32)
    if count:
        ins["ride"] = (ride, whole(ride.shape))
        result("ride_out", ride.shape, ride.dtype)
        scratch["ride_in"] = pltpu.VMEM(ride.shape, ride.dtype)
        scratch["ride_send"] = pltpu.SemaphoreType.DMA((2,))
        scratch["ride_recv"] = pltpu.SemaphoreType.DMA((2,))
    names = list(ins) + list(outs) + list(scratch)
    remote = {"collective_id": number, "has_side_effects": True} if count else {}
    room = 12 if slots < 8 else 20 if wide is None else 30
    products = (weight is not None) + (grad_rows is not None)
    return pl.pallas_call(
        lambda *refs: brick_kernel(count, masked, scales, parts, names, *refs),
        grid=(amount,),
        in_specs=[spec for _, spec in ins.values()],
        out_specs=[spec for _, spec in outs.values()],
        out_shape=[shape for shape, _ in outs.values()],
        scratch_shapes=list(scratch.values()),
        compiler_params=pltpu.CompilerParams(vmem_limit_bytes=room * 1024 * 1024, **remote),
        cost_estimate=pl.CostEstimate(
            flops=amount * products * 2 * rows * 3 * WIDTH * 512,
            bytes_accessed=slots * 64 * 512 * 2,
            transcendentals=0,
        ),
    )(*[value for value, _ in ins.values()])


def unpack(total, out, scale):
    high = total.shape[2]
    blocks = out.shape[1] // high
    for tap_x in range(3):
        for block in range(blocks):
            first = WIDTH // 128 * (tap_x * blocks + block)
            rows = slice(high * block, high * block + high)
            for place, tap in enumerate(TAP_ORDER):
                lanes = slice(64 * (place % 2), 64 * (place % 2) + 64)
                plane, piece = divmod(first + place // 2, total.shape[1])
                out[9 * tap_x + int(tap), rows, :] = total[plane, piece, :, lanes] * scale


def wide_pieces(coarse, project):
    tiles = jnp.transpose(coarse.reshape(-1, 8, WIDTH // 128, 128), (0, 2, 1, 3))
    tiles = tiles.reshape(-1, 8, 128)
    small = project.reshape(-1, 8, 128)
    spare = 128 - tiles.shape[0] - small.shape[0]
    return jnp.concatenate([tiles, small, jnp.zeros((spare, 8, 128), jnp.float32)], axis=0)


def per_device(
    feats, live_count, neighbours, parent, fine_weight, coarse_weight, project_weight, cotangent
):
    bricks = feats.shape[0]
    half_channels = feats.shape[1]
    devices = lax.axis_size("space")
    own_index = lax.axis_index("space")
    moving = max(1, bricks // 8)
    coarse_bricks = bricks // 8
    live_mask = (jnp.arange(bricks, dtype=jnp.int32) < live_count[0]).astype(jnp.float32)[
        :, None, None
    ]
    core = lax.axis_index("chan")
    send_place = route_places(parent, own_index, moving, bricks)
    send_pick = (jnp.arange(2 * moving, dtype=jnp.int32)[:, None] == send_place[None, :]).astype(
        jnp.bfloat16
    )
    pooled = (pool_sum(feats) * 0.125 * live_mask).astype(jnp.bfloat16).reshape(bricks, -1)
    slot_rows = jnp.broadcast_to(
        (parent % bricks + 1).astype(jnp.bfloat16)[:, None], (bricks, 2048)
    )
    outgoing = select_rows(send_pick, jnp.concatenate([pooled, slot_rows], axis=1))
    grad_rows = (cotangent.astype(jnp.float32) * live_mask).astype(jnp.bfloat16)
    incoming, grad_fields, both_pooled, whole_coarse, whole_fine, both_project = trade(
        outgoing.reshape(2, moving * 32, 128),
        grad_rows,
        [pooled.reshape(bricks * 16, 128), coarse_weight, fine_weight, project_weight],
        2,
    )
    whole_project = jnp.concatenate([both_project[0], both_project[1]], axis=1)
    incoming = incoming.reshape(2, 2 * moving, 4096)
    incoming_slots = incoming[0, :, -1].astype(jnp.int32) - 1
    local_slots = jnp.where(parent // bricks == own_index, parent % bricks, -1)
    all_slots = jnp.concatenate([local_slots, incoming_slots])
    receive_pick = (jnp.arange(bricks, dtype=jnp.int32)[:, None] == all_slots[None, :]).astype(
        jnp.bfloat16
    )
    arrived = select_both(receive_pick, both_pooled, incoming[:, :, :2048])
    coarse_in = place_octants(arrived)
    lone = lone_bricks(coarse_bricks)
    preactivation = brick_pass(
        coarse_in, lone, live_count, whole_coarse[None], None, jnp.float32, False
    )[0]
    hidden = jax.nn.silu(preactivation).astype(jnp.bfloat16)
    own_project = lax.dynamic_slice_in_dim(
        whole_project, core * half_channels, half_channels, 0
    )
    coarse_out = jnp.einsum(
        "cj,bjv->bcv", own_project, hidden, preferred_element_type=jnp.float32
    ).astype(jnp.bfloat16)
    back_source = select_rows(receive_pick.T, split_octants(coarse_out).reshape(bricks, -1))
    last_brick = devices * bricks
    near_local = jnp.where(
        neighbours >= last_brick, 3 * bricks, neighbours - (own_index - 1) * bricks
    ).astype(jnp.int32)
    slots = jnp.arange(bricks, dtype=jnp.int32)[:, None] + bricks
    near = jnp.concatenate([near_local[:, :13], slots, near_local[:, 13:]], axis=1)
    own_weight = lax.dynamic_slice_in_dim(whole_fine, core * half_channels, half_channels, 2)
    back_feats, rode_back = brick_pass(
        grad_fields,
        near,
        live_count,
        flip_weight(own_weight)[None],
        None,
        jnp.bfloat16,
        True,
        back_source[bricks:].reshape(2, moving * 16, 128),
        3,
    )
    up_octants = gather_back(
        back_source[:bricks], send_pick, rode_back.reshape(2 * moving, -1)
    ).reshape(bricks, half_channels, 64)
    mixed_feats = ((feats.astype(jnp.float32) + enlarge(up_octants)) * live_mask).astype(
        jnp.bfloat16
    )
    up_grad = pool_sum(back_feats).astype(jnp.bfloat16).reshape(bricks, -1)
    outgoing_grad = select_rows(send_pick, up_grad)
    incoming_grad, feat_fields, both_grad = trade(
        outgoing_grad.reshape(2, moving * 16, 128),
        mixed_feats,
        [up_grad.reshape(bricks * 16, 128)],
        4,
    )
    coarse_grad = place_octants(
        select_both(receive_pick, both_grad, incoming_grad.reshape(2, 2 * moving, 2048))
    )
    hidden_half = hidden.shape[1] // 2
    own_hidden = lax.dynamic_slice_in_dim(hidden, core * hidden_half, hidden_half, 1)
    project_matrix = jnp.einsum(
        "bcv,bjv->cj", coarse_grad, own_hidden, preferred_element_type=jnp.float32
    )
    hidden_grad = jnp.einsum(
        "cj,bcv->bjv", whole_project, coarse_grad, preferred_element_type=jnp.float32
    )
    sigmoid_pre = jax.nn.sigmoid(preactivation)
    pre_grad = (hidden_grad * sigmoid_pre * (1.0 + preactivation * (1.0 - sigmoid_pre))).astype(
        jnp.bfloat16
    )
    own_pre_grad = lax.dynamic_slice_in_dim(pre_grad, core * hidden_half, hidden_half, 1)
    coarse_total = brick_pass(
        coarse_in, lone, live_count, None, own_pre_grad, None, False
    )[0]
    own_coarse = flip_weight(
        lax.dynamic_slice_in_dim(whole_coarse, core * half_channels, half_channels, 2)
    )
    coarse_terms = brick_pass(
        pre_grad.reshape(2 * coarse_bricks, hidden_half, 512),
        lone_bricks(2 * coarse_bricks),
        live_count,
        jnp.stack([own_coarse[:, :, :hidden_half], own_coarse[:, :, hidden_half:]]),
        None,
        jnp.float32,
        False,
    )[0]
    coarse_back = (
        coarse_terms.reshape(coarse_bricks, 2, half_channels, 512).sum(1).astype(jnp.bfloat16)
    )
    down_source = select_rows(receive_pick.T, split_octants(coarse_back).reshape(bricks, -1))
    fine_scale = 1.0 / math.sqrt(512.0 * bricks * devices)
    coarse_scale = 1.0 / math.sqrt(512.0 * coarse_bricks * devices)
    out_feats, fine_weight_grad, coarse_weight_grad, project_tiles, rode_down = brick_pass(
        feat_fields,
        near,
        live_count,
        fine_weight[None],
        grad_rows,
        jnp.bfloat16,
        True,
        down_source[bricks:].reshape(2, moving * 16, 128),
        5,
        wide_pieces(coarse_total, project_matrix),
        (fine_scale, coarse_scale),
    )
    down_grad = gather_back(
        down_source[:bricks], send_pick, rode_down.reshape(2 * moving, -1)
    ).reshape(bricks, half_channels, 64)
    grad_feats = (back_feats.astype(jnp.float32) + live_mask * enlarge(down_grad) * 0.125).astype(
        jnp.bfloat16
    )
    project_weight_grad = project_tiles.reshape(project_matrix.shape)
    return (out_feats, grad_feats, fine_weight_grad, coarse_weight_grad, project_weight_grad)


def solution(mesh):
    placed = (
        P("space", "chan", None),
        P("space"),
        P("space", None),
        P("space"),
        P(None, "chan", None),
        P(None, "chan", None),
        P(None, "chan"),
        P("space", "chan", None),
    )
    return jax.shard_map(
        per_device,
        mesh=mesh,
        in_specs=placed,
        out_specs=(
            P("space", "chan", None),
            P("space", "chan", None),
            P(None, "chan", None),
            P(None, "chan", None),
            P(None, "chan"),
        ),
        check_vma=False,
    )
```
